32 devices in a mesh: gx: 4 (over y, core), gy: 8 (over z, x).
Axes of the slice: x: 2, y: 2, z: 4, core: 2. Of those that a mesh axis runs over, the one named last changes fastest.
Arguments:
- states: bfloat16 [32, 512, 768], P(('gx', 'gy')), may hold values from -6 to 6
- encoded: bfloat16 [32, 512, 768], P(('gx', 'gy')), may hold values from -6 to 6
- cotangent: bfloat16 [32, 512, 768], P(('gx', 'gy')), may hold values from -6 to 6
- dec_lens: int32 [32], P(('gx', 'gy')), may hold values from 1 to 512, 10240 in all
- enc_lens: int32 [32], P(('gx', 'gy')), may hold values from 1 to 512, 8192 in all
- self_query: bfloat16 [768, 768], P(('gx', 'gy')), may hold values from -0.02734375 to 0.02734375
- self_key: bfloat16 [768, 768], P(('gx', 'gy')), may hold values from -0.21875 to 0.21875
- self_value: bfloat16 [768, 768], P(('gx', 'gy')), may hold values from -0.21875 to 0.21875
- self_out: bfloat16 [768, 768], P(('gx', 'gy')), may hold values from -1.25 to 1.25
- cross_query: bfloat16 [768, 768], P(('gx', 'gy')), may hold values from -0.02734375 to 0.02734375
- cross_key: bfloat16 [768, 768], P(('gx', 'gy')), may hold values from -0.21875 to 0.21875
- cross_value: bfloat16 [768, 768], P(('gx', 'gy')), may hold values from -0.21875 to 0.21875
- cross_out: bfloat16 [768, 768], P(('gx', 'gy')), may hold values from -1.25 to 1.25
- ffn_gate: bfloat16 [768, 2048], P(('gx', 'gy')), may hold values from -0.21875 to 0.21875
- ffn_up: bfloat16 [768, 2048], P(('gx', 'gy')), may hold values from -0.21875 to 0.21875
- ffn_out: bfloat16 [768, 2048], P(('gx', 'gy')), may hold values from -0.125 to 0.125
- gain_self: bfloat16 [768], P(('gx', 'gy')), may hold values from 0.5 to 1.5
- gain_cross: bfloat16 [768], P(('gx', 'gy')), may hold values from 0.5 to 1.5
- gain_ffn: bfloat16 [768], P(('gx', 'gy')), may hold values from 0.5 to 1.5
- bucket_bias_table: bfloat16 [32, 12], replicated, may hold values from -4 to 4
Outputs:
- output: bfloat16 [32, 512, 768], P(('gx', 'gy'))
- grad_states: bfloat16 [32, 512, 768], P(('gx', 'gy'))
- grad_encoded: bfloat16 [32, 512, 768], P(('gx', 'gy'))
- grad_self_query: float32 [768, 768], P(('gx', 'gy'))
- grad_self_key: float32 [768, 768], P(('gx', 'gy'))
- grad_self_value: float32 [768, 768], P(('gx', 'gy'))
- grad_self_out: float32 [768, 768], P(('gx', 'gy'))
- grad_cross_query: float32 [768, 768], P(('gx', 'gy'))
- grad_cross_key: float32 [768, 768], P(('gx', 'gy'))
- grad_cross_value: float32 [768, 768], P(('gx', 'gy'))
- grad_cross_out: float32 [768, 768], P(('gx', 'gy'))
- grad_ffn_gate: float32 [768, 2048], P(('gx', 'gy'))
- grad_ffn_up: float32 [768, 2048], P(('gx', 'gy'))
- grad_ffn_out: float32 [768, 2048], P(('gx', 'gy'))
- grad_gain_self: float32 [768], P(('gx', 'gy'))
- grad_gain_cross: float32 [768], P(('gx', 'gy'))
- grad_gain_ffn: float32 [768], P(('gx', 'gy'))
- grad_bucket_table: float32 [32, 12], replicated
The draws below stay inside these ranges and needn't reach their ends.
Inputs may be any that keep to these rules, and one draw needn't show every extreme that they name: Row r holds one decoder sequence of dec_lens[r] tokens in its first slots; the longest has exactly 512. Row r has enc_lens[r] encoder outputs in its first slots; the longest has exactly 512.
All inputs are finite; a program needn't handle non-finite values. No bound on the sum of `dec_lens` or of `enc_lens` on one device may be relied on, other than what follows from the above.
Results may differ from the reference program's by a relative error of at most 0.025.
Values may be sent and summed in bfloat16 or wider, within the bound.
No kernel may reach another device: no remote copies, remote signals or barrier semaphores. Data moves between devices by JAX's collectives and lax.ppermute only.
A program may use at most 192 MiB of HBM per device.

```python
import math
import jax
import jax.numpy as jnp
import numpy as np
from jax import lax

D = 768
H = 12
HD = 64
FF = 2048
NB = 32
L = 512
LE = 512
INNER = 768
ROWS = 32


def block_scale(key, extent, shards, low, largest):
    factor_of, own = 1.0, jax.random.fold_in(key, 6)
    for axis_at, blocks in shards:
        heights = jnp.exp(jax.random.uniform(jax.random.fold_in(own, axis_at), (blocks,), jnp.float32, low / len(shards), largest / len(shards)))
        factor_of = factor_of * jnp.repeat(heights, extent[axis_at] // blocks).reshape([-1 if axis == axis_at else 1 for axis in range(len(extent))])
    return factor_of


def profile(count, total, limit, slope):
    loads = [(1 << 20) // math.isqrt(standing ** slope) + 1 for standing in range(2, count + 1)]
    surplus, counts = total - limit - (count - 1), [1] * (count - 1)
    while surplus > 0:
        candidates = [i for i in range(count - 1) if counts[i] < limit]
        pool, remaining = sum([loads[i] for i in candidates]), surplus
        for i in candidates:
            addition = min(limit - counts[i], max(1, remaining * loads[i] // pool), surplus)
            counts[i] = counts[i] + addition
            surplus = surplus - addition
    return np.array([limit] + counts)


def ragged_sizes(key, amount, total, most, skew):
    if amount == 2:
        one = jax.random.randint(key, (), max(1, total - most), min(most, total - 1) + 1)
        return jnp.stack([one, total - one])
    tallies = jnp.asarray(profile(amount, total, most, skew), jnp.int32)
    pairs = (amount - 1) // 2
    source_of, sink = tallies[1:1 + 2 * pairs:2], tallies[2:2 + 2 * pairs:2]
    margin = jnp.minimum(source_of - 1, most - sink)
    shifted = jax.random.randint(jax.random.fold_in(key, 1), (pairs,), 0, 1 << 20) % (margin + 1)
    tallies = tallies.at[1:1 + 2 * pairs:2].set(source_of - shifted).at[2:2 + 2 * pairs:2].set(sink + shifted)
    return tallies[jax.random.permutation(jax.random.fold_in(key, 2), amount)]


def gaussian(own_key, dims, scale, most, cuts=(), kind=jnp.bfloat16):
    values = jax.random.normal(own_key, dims, jnp.float32) * scale
    if len(cuts) > 0:
        values = block_scale(own_key, dims, cuts, -0.22, 0.18) * values
    return jnp.clip(values, min=-most, max=most).astype(kind)


def setup_inputs(seed: int = 0) -> dict:
    streams_of = jax.random.split(jax.random.key(seed), 21)
    states = gaussian(streams_of[0], (ROWS, L, D), 1.0, 6.0, ((0, 32),))
    encoded = gaussian(streams_of[1], (ROWS, LE, D), 1.0, 6.0, ((0, 32),))
    cotangent = gaussian(streams_of[2], (ROWS, L, D), 1.0, 6.0, ((0, 32),))
    dec_lens = ragged_sizes(streams_of[3], ROWS, ROWS * L * 5 // 8, L, 2).astype(jnp.int32)
    enc_lens = ragged_sizes(streams_of[4], ROWS, ROWS * LE // 2, LE, 2).astype(jnp.int32)
    self_query = gaussian(streams_of[5], (D, INNER), (D * HD) ** -0.5, 0.02734375, ((0, 32),))
    self_key = gaussian(streams_of[6], (D, INNER), D ** -0.5, 0.21875, ((0, 32),))
    self_value = gaussian(streams_of[7], (D, INNER), D ** -0.5, 0.21875, ((0, 32),))
    self_out = gaussian(streams_of[8], (D, INNER), (INNER // 32) ** -0.5, 1.25, ((0, 32),))
    cross_query = gaussian(streams_of[9], (D, INNER), (D * HD) ** -0.5, 0.02734375, ((0, 32),))
    cross_key = gaussian(streams_of[10], (D, INNER), D ** -0.5, 0.21875, ((0, 32),))
    cross_value = gaussian(streams_of[11], (D, INNER), D ** -0.5, 0.21875, ((0, 32),))
    cross_out = gaussian(streams_of[12], (D, INNER), (INNER // 32) ** -0.5, 1.25, ((0, 32),))
    ffn_gate = gaussian(streams_of[13], (D, FF), D ** -0.5, 0.21875, ((0, 32),))
    ffn_up = gaussian(streams_of[14], (D, FF), D ** -0.5, 0.21875, ((0, 32),))
    ffn_out = gaussian(streams_of[15], (D, FF), FF ** -0.5, 0.125, ((0, 32),))
    gain_self = jnp.clip(1.0 + 0.1 * jax.random.normal(streams_of[16], (D,), jnp.float32), 0.5, 1.5).astype(jnp.bfloat16)
    gain_cross = jnp.clip(1.0 + 0.1 * jax.random.normal(streams_of[17], (D,), jnp.float32), 0.5, 1.5).astype(jnp.bfloat16)
    gain_ffn = jnp.clip(1.0 + 0.1 * jax.random.normal(streams_of[18], (D,), jnp.float32), 0.5, 1.5).astype(jnp.bfloat16)
    bucket_bias_table = gaussian(streams_of[19], (NB, H), 1.0, 4.0)
    return {"states": states, "encoded": encoded, "cotangent": cotangent, "dec_lens": dec_lens, "enc_lens": enc_lens, "self_query": self_query, "self_key": self_key, "self_value": self_value, "self_out": self_out, "cross_query": cross_query, "cross_key": cross_key, "cross_value": cross_value, "cross_out": cross_out, "ffn_gate": ffn_gate, "ffn_up": ffn_up, "ffn_out": ffn_out, "gain_self": gain_self, "gain_cross": gain_cross, "gain_ffn": gain_ffn, "bucket_bias_table": bucket_bias_table}


norm_eps = 1e-06
masked_score = -1000000000.0
group_rows = 8
bucket_edges = [int(math.ceil(16 * 8 ** (power / 16.0))) for power in range(1, 16)]

@jax.custom_vjp
def low(v):
    return lax.optimization_barrier(v.astype(jnp.bfloat16)).astype(jnp.float32)

@jax.custom_vjp
def low_back(v):
    return v

def low_keep(v):
    return (low(v), None)

def low_pass(kept, grad):
    return (grad,)

def back_keep(v):
    return (v, None)

def back_low(kept, grad):
    return (low(grad),)
low.defvjp(low_keep, low_pass)
low_back.defvjp(back_keep, back_low)

def buckets_of(length):
    places = jnp.arange(length, dtype=jnp.int32)
    distance = jnp.maximum(places[:, None] - places[None, :], 0)
    counted = jnp.zeros_like(distance)
    for edge in bucket_edges:
        counted = counted + (distance >= edge).astype(jnp.int32)
    return jnp.where(distance < 16, distance, 16 + counted)

def rms_norm(values, gain):
    return values * lax.rsqrt(lax.optimization_barrier(jnp.mean(values * values, axis=-1, keepdims=True)) + norm_eps) * gain

def matmul(left, right):
    return jnp.dot(left, right, precision=lax.Precision.HIGHEST)

def matmul_t(left, right):
    return jnp.dot(left, right.T, precision=lax.Precision.HIGHEST)

def attend(queries, keys_in, values_in, position_bias, allowed):
    q_heads = queries.reshape(queries.shape[0], H, HD)
    k_heads = keys_in.reshape(keys_in.shape[0], H, HD)
    v_heads = values_in.reshape(values_in.shape[0], H, HD)
    scores = jnp.einsum('qhd,khd->hqk', q_heads, k_heads, precision=lax.Precision.HIGHEST) + position_bias
    scores = low_back(scores)
    scores = jnp.where(allowed[None], scores, masked_score)
    probs = low(jax.nn.softmax(scores, axis=-1))
    mixed = jnp.einsum('hqk,khd->qhd', probs, v_heads, precision=lax.Precision.HIGHEST)
    return low_back(low(mixed.reshape(queries.shape[0], H * HD)))

def forward(params, table, states, encoded, dec_lens, enc_lens):
    self_query, self_key, self_value, self_out, cross_query, cross_key, cross_value, cross_out, ffn_gate, ffn_up, ffn_out, gain_self, gain_cross, gain_ffn = params
    position_bias = jnp.transpose(table[buckets_of(L)], (2, 0, 1))

    def single_row(states_row, encoded_row, dec_len, enc_len):
        places = jnp.arange(L, dtype=jnp.int32)
        self_allowed = (places[None, :] <= places[:, None]) & (places[None, :] < dec_len)
        cross_allowed = jnp.broadcast_to((jnp.arange(LE, dtype=jnp.int32) < enc_len)[None, :], (L, LE))
        normed_one = low(rms_norm(states_row, gain_self))
        queries = low_back(low(matmul(normed_one, self_query)))
        keys_one = low_back(low(matmul(normed_one, self_key)))
        values_one = low_back(low(matmul(normed_one, self_value)))
        mixed_one = attend(queries, keys_one, values_one, position_bias, self_allowed)
        hidden_one = states_row + low_back(matmul_t(mixed_one, self_out))
        normed_two = low(rms_norm(hidden_one, gain_cross))
        cross_queries = low_back(low(matmul(normed_two, cross_query)))
        cross_keys = low_back(low(matmul(encoded_row, cross_key)))
        cross_values = low_back(low(matmul(encoded_row, cross_value)))
        mixed_two = attend(cross_queries, cross_keys, cross_values, 0.0, cross_allowed)
        hidden_two = hidden_one + low_back(matmul_t(mixed_two, cross_out))
        normed_three = low(rms_norm(hidden_two, gain_ffn))
        gate_pre = low_back(matmul(normed_three, ffn_gate))
        up_pre = low_back(matmul(normed_three, ffn_up))
        gated = low(jax.nn.gelu(gate_pre, approximate=True) * up_pre)
        return hidden_two + matmul_t(gated, ffn_out)

    def group_step(carry, pieces):
        return (carry, jax.vmap(single_row)(pieces[0], pieces[1], pieces[2], pieces[3]))
    groups = ROWS // group_rows
    grouped = (states.reshape(groups, group_rows, L, D), encoded.reshape(groups, group_rows, LE, D), dec_lens.reshape(groups, group_rows), enc_lens.reshape(groups, group_rows))
    carry_out, outputs = lax.scan(jax.checkpoint(group_step), jnp.zeros((), jnp.float32), grouped)
    return outputs.reshape(ROWS, L, D)

def reference(states, encoded, cotangent, dec_lens, enc_lens, self_query, self_key, self_value, self_out, cross_query, cross_key, cross_value, cross_out, ffn_gate, ffn_up, ffn_out, gain_self, gain_cross, gain_ffn, bucket_bias_table):
    params = tuple((weight.astype(jnp.float32) for weight in (self_query, self_key, self_value, self_out, cross_query, cross_key, cross_value, cross_out, ffn_gate, ffn_up, ffn_out, gain_self, gain_cross, gain_ffn)))

    def run(params_in, table_in, states_in, encoded_in):
        return forward(params_in, table_in, states_in, encoded_in, dec_lens, enc_lens)
    result, pullback = jax.vjp(run, params, bucket_bias_table.astype(jnp.float32), states.astype(jnp.float32), encoded.astype(jnp.float32))
    d_params, d_table, d_states, d_encoded = pullback(cotangent.astype(jnp.float32))
    return (result.astype(jnp.bfloat16), d_states.astype(jnp.bfloat16), d_encoded.astype(jnp.bfloat16), d_params[0], d_params[1], d_params[2], d_params[3], d_params[4], d_params[5], d_params[6], d_params[7], d_params[8], d_params[9], d_params[10], d_params[11], d_params[12], d_params[13], d_table)
```

```python
import math

import jax
import jax.numpy as jnp
import numpy as np
from jax import lax
from jax.sharding import PartitionSpec as P

H = 12
HD = 64
NB = 32

norm_eps = 1e-06
masked_score = -1000000000.0
bucket_edges = [int(math.ceil(16 * 8 ** (power / 16.0))) for power in range(1, 16)]

bf16 = jnp.bfloat16
f32 = jnp.float32


def buckets_of(length):
    places = jnp.arange(length, dtype=jnp.int32)
    distance = jnp.maximum(places[:, None] - places[None, :], 0)
    counted = jnp.zeros_like(distance)
    for edge in bucket_edges:
        counted = counted + (distance >= edge).astype(jnp.int32)
    return jnp.where(distance < 16, distance, 16 + counted)


class Cube:
    def __init__(self, mesh):
        self.nx, self.ny = mesh.shape["gx"], mesh.shape["gy"]
        self.n = self.nx * self.ny
        self.core, self.y, self.x = ("gx", 1), ("gx", 2), ("gy", 1)
        self.rest = []
        bit = self.ny // 2
        while bit > 1:
            self.rest.append(("gy", bit))
            bit //= 2
        bit = self.nx // 2
        while bit > 2:
            self.rest.append(("gx", bit))
            bit //= 2

    def send(self, value, step):
        axis, bit = step
        size = self.nx if axis == "gx" else self.ny
        return lax.ppermute(value, axis, [(i, i ^ bit) for i in range(size)])

    def owners(self):
        mask_x, mask_y = np.zeros(self.n, np.int32), np.zeros(self.n, np.int32)
        for place in range(self.n):
            steps = []
            inner, block = place % (self.n // 8), (place // (self.n // 8)) % 4
            for at, step in enumerate(self.rest):
                if (inner >> at) & 1:
                    steps.append(step)
            if block & 1:
                steps.append(self.x)
            if block & 2:
                steps.append(self.y)
            if place >= self.n // 2:
                steps.append(self.core)
            for axis, bit in steps:
                if axis == "gx":
                    mask_x[place] ^= bit
                else:
                    mask_y[place] ^= bit
        gx, gy = lax.axis_index("gx"), lax.axis_index("gy")
        return (gx ^ jnp.asarray(mask_x)) * self.ny + (gy ^ jnp.asarray(mask_y))

    def permutation(self, width):
        rows = width // self.n
        feature = (self.owners()[:, None] * rows + jnp.arange(rows, dtype=jnp.int32)).reshape(1, width)
        return (jnp.arange(width, dtype=jnp.int32)[:, None] == feature).astype(bf16)

    def gather(self, packed):
        own = packed
        for step in self.rest:
            own = jnp.concatenate([own, self.send(own, step)], axis=0)
        half = own.shape[0] // 2
        over_x = self.send(own, self.x)
        over_y = self.send(own, self.y)
        far_one = self.send(over_y[:half], self.x)
        far_two = self.send(over_x[half:], self.y)
        pieces = [own, over_x, over_y, far_one, far_two]
        return pieces + [self.send(piece, self.core) for piece in pieces]

    def reduce(self, low, high):
        total = low + self.send(high, self.core)
        size = total.shape[0] // 4
        half = size // 2
        own, to_x, to_y, far = (total[i * size : (i + 1) * size] for i in range(4))
        got_y = self.send(far[:half], self.x)
        got_x = self.send(far[half:], self.y)
        to_y = jnp.concatenate([to_y[:half] + got_y, to_y[half:]], axis=0)
        to_x = jnp.concatenate([to_x[:half], to_x[half:] + got_x], axis=0)
        own = own + self.send(to_x, self.x) + self.send(to_y, self.y)
        for step in reversed(self.rest):
            half = own.shape[0] // 2
            own = own[:half] + self.send(own[half:], step)
        return own

    def all_sum(self, value):
        for step in [self.core, self.x, self.y] + self.rest:
            value = value + self.send(value, step)
        return value


def times(left, right):
    return jnp.dot(left, right, preferred_element_type=f32)


def times_t(left, right):
    return lax.dot_general(left, right, (((1,), (1,)), ((), ())), preferred_element_type=f32)


def inner_t(left, right):
    return lax.dot_general(left, right, (((0,), (0,)), ((), ())), preferred_element_type=f32)


def norm(values, gain):
    return values * lax.rsqrt(jnp.mean(values * values, axis=-1, keepdims=True) + norm_eps) * gain


def norm_back(values, gain, d_normed):
    normed, pullback = jax.vjp(norm, values, gain)
    return pullback(d_normed)


def gated_unit(first, second):
    return jax.nn.gelu(first, approximate=True) * second


def gated_back(gate_pre, up_pre, d_gated):
    gated, pullback = jax.vjp(gated_unit, gate_pre, up_pre)
    return pullback(d_gated)


def heads(v):
    return v.reshape(v.shape[0], H, HD)


def attend_forward(q, k, v, bias, allowed):
    scores = jnp.einsum("qhd,khd->hqk", heads(q), heads(k), preferred_element_type=f32) + bias
    scores = jnp.where(allowed[None], scores, masked_score)
    highest = jnp.max(scores, axis=-1, keepdims=True)
    expo = jnp.exp(scores - highest)
    probs = (expo / jnp.sum(expo, axis=-1, keepdims=True)).astype(bf16)
    mixed = jnp.einsum("hqk,khd->qhd", probs, heads(v), preferred_element_type=f32)
    return mixed.reshape(q.shape).astype(bf16), probs


def attend_backward(q, k, v, probs, d_mixed):
    d_heads = heads(d_mixed)
    d_probs = jnp.einsum("qhd,khd->hqk", d_heads, heads(v), preferred_element_type=f32)
    d_v = jnp.einsum("hqk,qhd->khd", probs, d_heads, preferred_element_type=f32)
    p = probs.astype(f32)
    d_scores = (p * (d_probs - jnp.sum(p * d_probs, axis=-1, keepdims=True))).astype(bf16)
    d_q = jnp.einsum("hqk,khd->qhd", d_scores, heads(k), preferred_element_type=f32)
    d_k = jnp.einsum("hqk,qhd->khd", d_scores, heads(q), preferred_element_type=f32)
    return (
        d_q.reshape(q.shape).astype(bf16),
        d_k.reshape(q.shape).astype(bf16),
        d_v.reshape(q.shape).astype(bf16),
        d_scores,
    )


def layer(
    cube,
    states,
    encoded,
    cotangent,
    dec_lens,
    enc_lens,
    self_query,
    self_key,
    self_value,
    self_out,
    cross_query,
    cross_key,
    cross_value,
    cross_out,
    ffn_gate,
    ffn_up,
    ffn_out,
    gain_self,
    gain_cross,
    gain_ffn,
    table,
):
    rows, length, width = states.shape
    inner, hidden = self_query.shape[1], ffn_gate.shape[1]
    gains = jnp.stack([gain_self, gain_cross, gain_ffn], axis=1)
    gains = jnp.pad(gains, ((0, 0), (0, 125)))

    def collect(*parts):
        return jnp.concatenate(cube.gather(jnp.concatenate(parts, axis=1)), axis=0)

    first = collect(gains, self_query, self_key, self_value, self_out)
    second = collect(cross_query, cross_key, cross_value, cross_out)
    third = collect(ffn_gate, ffn_up)
    w_down = collect(ffn_out)
    gain_rows = first[:, :3].astype(f32).T
    g_self, g_cross, g_ffn = gain_rows[0:1], gain_rows[1:2], gain_rows[2:3]
    w_qkv, w_so = first[:, 128 : 128 + 3 * inner], first[:, 128 + 3 * inner :]
    c_q, c_kv, c_o = second[:, :inner], second[:, inner : 3 * inner], second[:, 3 * inner :]
    w_gu = third

    perm = cube.permutation(width)
    inputs = times(states[0], perm)
    enc = times(encoded[0], perm).astype(bf16)
    cot = times(cotangent[0], perm).astype(bf16)

    buckets = buckets_of(length)
    ids = jnp.arange(NB, dtype=jnp.int32)
    indicator = (buckets[None] == ids[:, None, None]).astype(bf16)
    bias = jnp.einsum("eri,ex->xri", indicator, table, preferred_element_type=f32)
    places = jnp.arange(length, dtype=jnp.int32)
    self_mask = (places[None, :] <= places[:, None]) & (places[None, :] < dec_lens[0])
    cross_mask = jnp.broadcast_to((places < enc_lens[0])[None, :], (length, length))

    normed_one = norm(inputs, g_self).astype(bf16)
    qkv = times(normed_one, w_qkv).astype(bf16)
    q1, k1, v1 = qkv[:, :inner], qkv[:, inner : 2 * inner], qkv[:, 2 * inner :]
    mixed_one, probs_one = attend_forward(q1, k1, v1, bias, self_mask)
    hidden_one = inputs + times_t(mixed_one, w_so)
    normed_two = norm(hidden_one, g_cross).astype(bf16)
    q2 = times(normed_two, c_q).astype(bf16)
    kv2 = times(enc, c_kv).astype(bf16)
    k2, v2 = kv2[:, :inner], kv2[:, inner:]
    mixed_two, probs_two = attend_forward(q2, k2, v2, 0.0, cross_mask)
    hidden_two = hidden_one + times_t(mixed_two, c_o)
    normed_three = norm(hidden_two, g_ffn).astype(bf16)
    pre = times(normed_three, w_gu)
    gate_pre, up_pre = pre[:, :hidden], pre[:, hidden:]
    gated = gated_unit(gate_pre, up_pre).astype(bf16)
    result = hidden_two + times_t(gated, w_down)
    output = times_t(result.astype(bf16), perm).astype(bf16)

    def give(*parts):
        half = width // 2
        low = jnp.concatenate([part[:half].astype(bf16) for part in parts], axis=1)
        high = jnp.concatenate([part[half:].astype(bf16) for part in parts], axis=1)
        return cube.reduce(low, high).astype(f32)

    grad_fo = give(inner_t(cot, gated))
    d_gated = times(cot, w_down)
    d_gate, d_up = gated_back(gate_pre, up_pre, d_gated)
    d_gu = jnp.concatenate([d_gate.astype(bf16), d_up.astype(bf16)], axis=1)
    grad_gu = give(inner_t(normed_three, d_gu))
    d_normed_three = times_t(d_gu, w_gu)
    d_hidden_two, grad_gf = norm_back(hidden_two, g_ffn, d_normed_three)
    d_hidden_two = d_hidden_two + cot.astype(f32)
    d_attn_two = d_hidden_two.astype(bf16)
    grad_co = inner_t(d_attn_two, mixed_two)
    d_mixed_two = times(d_attn_two, c_o).astype(bf16)
    d_q2, d_k2, d_v2, _ = attend_backward(q2, k2, v2, probs_two, d_mixed_two)
    d_kv2 = jnp.concatenate([d_k2, d_v2], axis=1)
    grad_c = give(grad_co, inner_t(normed_two, d_q2), inner_t(enc, d_kv2))
    d_normed_two = times_t(d_q2, c_q)
    grad_enc = times_t(times_t(d_kv2, c_kv).astype(bf16), perm).astype(bf16)
    d_hidden_one, grad_gc = norm_back(hidden_one, g_cross, d_normed_two)
    d_hidden_one = d_hidden_one + d_hidden_two
    d_attn_one = d_hidden_one.astype(bf16)
    grad_so = inner_t(d_attn_one, mixed_one)
    d_mixed_one = times(d_attn_one, w_so).astype(bf16)
    d_q1, d_k1, d_v1, d_s1 = attend_backward(q1, k1, v1, probs_one, d_mixed_one)
    table_part = jnp.einsum("hri,eri->eh", d_s1, indicator, preferred_element_type=f32)
    grad_table = cube.all_sum(table_part)
    d_qkv = jnp.concatenate([d_q1, d_k1, d_v1], axis=1)
    d_normed_one = times_t(d_qkv, w_qkv)
    d_inputs, grad_gs = norm_back(inputs, g_self, d_normed_one)
    grad_states = times_t((d_inputs + d_hidden_one).astype(bf16), perm).astype(bf16)
    grad_gains = jnp.pad(jnp.concatenate([grad_gs, grad_gc, grad_gf], axis=0).T, ((0, 0), (0, 125)))
    grad_s = give(grad_gains, grad_so, inner_t(normed_one, d_qkv))
    return (
        output[None],
        grad_states[None],
        grad_enc[None],
        grad_s[:, 128 + inner : 128 + 2 * inner],
        grad_s[:, 128 + 2 * inner : 128 + 3 * inner],
        grad_s[:, 128 + 3 * inner :],
        grad_s[:, 128 : 128 + inner],
        grad_c[:, inner : 2 * inner],
        grad_c[:, 2 * inner : 3 * inner],
        grad_c[:, 3 * inner :],
        grad_c[:, :inner],
        grad_gu[:, :hidden],
        grad_gu[:, hidden:],
        grad_fo,
        grad_s[:, 0],
        grad_s[:, 1],
        grad_s[:, 2],
        grad_table,
    )


def solution(mesh):
    cube = Cube(mesh)
    both = ("gx", "gy")
    row, flat, one = P(both, None, None), P(both, None), P(both)
    in_specs = (row, row, row, one, one) + (flat,) * 11 + (one,) * 3 + (P(),)
    out_specs = (row, row, row) + (flat,) * 11 + (one,) * 3 + (P(),)

    def per_device(*args):
        return layer(cube, *args)

    return jax.shard_map(per_device, mesh=mesh, in_specs=in_specs, out_specs=out_specs, check_vma=False)
```

```python
import math

import jax
import jax.numpy as jnp
import numpy as np
from jax import lax
from jax.experimental import pallas as pl
from jax.experimental.pallas import tpu as pltpu
from jax.sharding import PartitionSpec as P

H = 12
HD = 64
NB = 32

norm_eps = 1e-06
masked_score = -1000000000.0
bucket_edges = [int(math.ceil(16 * 8 ** (power / 16.0))) for power in range(1, 16)]

bf16 = jnp.bfloat16
f32 = jnp.float32


def tie(*values):
    return lax.optimization_barrier(values)


class Cube:
    def __init__(self, mesh):
        self.nx, self.ny = mesh.shape["gx"], mesh.shape["gy"]
        self.n = self.nx * self.ny
        self.core, self.y, self.x = ("gx", 1), ("gx", 2), ("gy", 1)
        self.rest = []
        bit = self.ny // 2
        while bit > 1:
            self.rest.append(("gy", bit))
            bit //= 2
        bit = self.nx // 2
        while bit > 2:
            self.rest.append(("gx", bit))
            bit //= 2

    def send(self, value, step):
        axis, bit = step
        size = self.nx if axis == "gx" else self.ny
        return lax.ppermute(value, axis, [(i, i ^ bit) for i in range(size)])

    def owners(self):
        mask_x, mask_y = np.zeros(self.n, np.int32), np.zeros(self.n, np.int32)
        for place in range(self.n):
            steps = []
            inner, block = place % (self.n // 8), (place // (self.n // 8)) % 4
            for at_bit, step in enumerate(self.rest):
                if (inner >> at_bit) & 1:
                    steps.append(step)
            if block & 1:
                steps.append(self.x)
            if block & 2:
                steps.append(self.y)
            if place >= self.n // 2:
                steps.append(self.core)
            for axis, bit in steps:
                if axis == "gx":
                    mask_x[place] ^= bit
                else:
                    mask_y[place] ^= bit
        gx, gy = lax.axis_index("gx"), lax.axis_index("gy")
        return (gx ^ jnp.asarray(mask_x)) * self.ny + (gy ^ jnp.asarray(mask_y))

    def permutation(self, width):
        rows = width // self.n
        feature = (self.owners()[:, None] * rows + jnp.arange(rows, dtype=jnp.int32)).reshape(1, width)
        return (jnp.arange(width, dtype=jnp.int32)[:, None] == feature).astype(bf16)

    def all_sum(self, value):
        for step in [self.core, self.x, self.y] + self.rest:
            value = value + self.send(value, step)
        return value


class Gather:
    def __init__(self, cube, packed):
        self.cube, self.own = cube, packed

    def line(self, steps):
        for step in steps:
            self.own = jnp.concatenate([self.own, self.cube.send(self.own, step)], axis=0)

    def plane(self):
        self.over_x = self.cube.send(self.own, self.cube.x)
        self.over_y = self.cube.send(self.own, self.cube.y)

    def far(self):
        half = self.own.shape[0] // 2
        self.far_one = self.cube.send(self.over_y[:half], self.cube.x)
        self.far_two = self.cube.send(self.over_x[half:], self.cube.y)

    def across(self):
        pieces = [self.own, self.over_x, self.over_y, self.far_one, self.far_two]
        self.pieces = pieces + [self.cube.send(piece, self.cube.core) for piece in pieces]


class Reduce:
    def __init__(self, cube, low, high):
        self.cube, self.low = cube, low
        self.got = cube.send(high, cube.core)

    def far(self):
        cube = self.cube
        self.own, self.to_x, self.to_y, far_x, far_y = core_add(self.low, self.got)
        self.got_y, self.got_x = cube.send(far_x, cube.x), cube.send(far_y, cube.y)

    def plane(self):
        cube = self.cube
        to_x, to_y = plane_add(self.to_x, self.got_x, self.to_y, self.got_y)
        self.got_x, self.got_y = cube.send(to_x, cube.x), cube.send(to_y, cube.y)

    def line(self):
        steps = list(reversed(self.cube.rest))
        self.own, away = own_add(self.own, self.got_x, self.got_y)
        self.got = self.cube.send(away, steps[0])

    def rest(self):
        steps = list(reversed(self.cube.rest))
        for step in steps[1:]:
            self.own, away = line_add(self.own, self.got)
            self.got = self.cube.send(away, step)

    def last(self, widths):
        return last_add(self.own, self.got, widths)


TILE = 128
HALF = 384


def nn(left, right):
    return lax.dot_general(left, right, (((1,), (0,)), ((), ())), preferred_element_type=f32)


def nt(left, right):
    return lax.dot_general(left, right, (((1,), (1,)), ((), ())), preferred_element_type=f32)


def tn(left, right):
    return lax.dot_general(left, right, (((0,), (0,)), ((), ())), preferred_element_type=f32)


def at(start, size):
    return pl.ds(pl.multiple_of(start, TILE), size)


VMEM = pl.BlockSpec(memory_space=pltpu.VMEM)
SMEM = pl.BlockSpec(memory_space=pltpu.SMEM)
ANY = pl.BlockSpec(memory_space=pl.ANY)


def shape(dims, kind):
    return jax.ShapeDtypeStruct(dims, kind)


def call(body, name, ins, outs, scratch, cost, *args):
    return pl.pallas_call(
        body,
        out_shape=[o[0] for o in outs],
        in_specs=ins,
        out_specs=[o[1] for o in outs],
        scratch_shapes=scratch,
        compiler_params=pltpu.CompilerParams(vmem_limit_bytes=60 * 2**20),
        cost_estimate=pl.CostEstimate(flops=0, bytes_accessed=int(cost * 3.6e6), transcendentals=0),
        name=name,
    )(*args)


def halves(value):
    lane = lax.broadcasted_iota(jnp.int32, value, 1)
    return (lane < HD, lane >= HD)


def inverse_rms(v):
    return lax.rsqrt(jnp.mean(v * v, axis=-1, keepdims=True) + norm_eps)


def norm_back(v, gain, dy, r):
    scaled = dy * gain
    mean = jnp.mean(scaled * v, axis=-1, keepdims=True)
    d_v = (scaled - v * (mean * (r * r))) * r
    return d_v, jnp.sum(dy * (v * r), axis=0, keepdims=True)


def softmax_rows(scores):
    top = jnp.max(scores, axis=-1, keepdims=True)
    expo = jnp.exp(scores - top)
    return (expo * (1.0 / jnp.sum(expo, axis=-1, keepdims=True))).astype(bf16)


def bias_body(lines, out):
    def one(i, _):
        line = lines[pl.ds(i, 1), :]
        wide = jnp.broadcast_to(line, (TILE, 2 * TILE))
        out[i] = pltpu.roll(wide, 0, 1, stride=1, stride_axis=0)[:, :TILE]
        return 0

    lax.fori_loop(0, out.shape[0], one, 0)


def copy_pieces(pieces, weights, sems, start=0):
    copies, row, cols = [], 0, weights.shape[1]
    for i, piece in enumerate(pieces):
        size = piece.shape[0]
        source = piece.at[:, pl.ds(start, cols)]
        copies.append(pltpu.make_async_copy(source, weights.at[pl.ds(row, size), :], sems.at[i]))
        copies[-1].start()
        row += size
    return copies


def wait(copies):
    for copy in copies:
        copy.wait()


def loop(count, body):
    def step(i, carry):
        body(i)
        return carry

    lax.fori_loop(0, count, step, 0)


WIDE = 2 * TILE


def wide(i, start=0):
    return pl.ds(pl.multiple_of(start + i * WIDE, TILE), WIDE)


def self_pairs(first, count, dec_len, bias, qkv, mixed, probs, probs_out, out_sems):
    tokens, inner = qkv.shape[0], qkv.shape[1] // 3
    blocks = tokens // TILE
    places = lax.broadcasted_iota(jnp.int32, (1, tokens), 1)
    limit = jnp.where(places < dec_len[0], 0.0, masked_score)

    def pair(i):
        lanes = at((first + i) * TILE, TILE)
        keys = qkv[:, at(inner + (first + i) * TILE, TILE)]
        values = qkv[:, at(2 * inner + (first + i) * TILE, TILE)]
        both = halves((TILE, TILE))
        for block in range(blocks):
            rows = pl.ds(block * TILE, TILE)
            seen = (block + 1) * TILE
            queries = qkv[rows, lanes]
            result = None
            for side in range(2):
                mine = jnp.where(both[side], queries, jnp.zeros_like(queries))
                scores = nt(mine, keys[:seen])
                strip = [bias[(2 * (first + i) + side) * blocks + block - j] for j in range(block + 1)]
                strip = strip[0] if block == 0 else jnp.concatenate(strip, axis=1)
                p = softmax_rows(scores + strip + limit[:, :seen])
                probs[2 * i + side, rows, pl.ds(0, seen)] = p
                got = nn(p, values[:seen])
                result = got if side == 0 else jnp.where(both[0], result, got)
            mixed[rows, at(i * TILE, TILE)] = result.astype(bf16)
        pltpu.make_async_copy(probs.at[pl.ds(2 * i, 2)], probs_out.at[pl.ds(2 * i, 2)], out_sems.at[i]).start()

    loop(count, pair)
    for i in range(count):
        pltpu.make_async_copy(probs.at[pl.ds(2 * i, 2)], probs_out.at[pl.ds(2 * i, 2)], out_sems.at[i]).wait()


def self_one_body(count, dec_len, x, bias, *refs):
    pieces, (gains, normed, qkv, mixed, probs_out, weights, probs, sems, out_sems) = refs[:10], refs[10:]
    copies = copy_pieces(pieces, weights, sems)
    xs = x[...].astype(f32)
    scaled = xs * inverse_rms(xs)
    wait(copies)
    gain_rows = jnp.transpose(weights[:, :TILE].astype(f32))
    gains[...] = gain_rows[:8]
    normed[...] = (scaled * gain_rows[0:1]).astype(bf16)

    def project(i):
        qkv[:, wide(i)] = nn(normed[...], weights[:, wide(i, TILE)]).astype(bf16)

    loop(qkv.shape[1] // WIDE, project)
    self_pairs(0, count, dec_len, bias, qkv, mixed, probs, probs_out, out_sems)


def self_two_body(first, count, dec_len, bias, qkv, mixed, probs_out, probs, out_sems):
    self_pairs(first, count, dec_len, bias, qkv, mixed, probs, probs_out, out_sems)


def cross_pairs(first, count, enc_len, queries, kv, mixed, probs, probs_out, out_sems):
    blocks, inner = queries.shape[0] // TILE, queries.shape[1]
    places = lax.broadcasted_iota(jnp.int32, (1, kv.shape[0]), 1)
    limit = jnp.where(places < enc_len[0], 0.0, masked_score)

    def pair(i):
        lanes = at((first + i) * TILE, TILE)
        keys = kv[:, lanes]
        values = kv[:, at(inner + (first + i) * TILE, TILE)]
        both = halves((TILE, TILE))
        for block in range(blocks):
            rows = pl.ds(block * TILE, TILE)
            here = queries[rows, lanes]
            result = None
            for side in range(2):
                mine = jnp.where(both[side], here, jnp.zeros_like(here))
                p = softmax_rows(nt(mine, keys) + limit)
                probs[2 * i + side, rows, :] = p
                got = nn(p, values)
                result = got if side == 0 else jnp.where(both[0], result, got)
            mixed[rows, at(i * TILE, TILE)] = result.astype(bf16)
        pltpu.make_async_copy(probs.at[pl.ds(2 * i, 2)], probs_out.at[pl.ds(2 * i, 2)], out_sems.at[i]).start()

    loop(count, pair)
    for i in range(count):
        pltpu.make_async_copy(probs.at[pl.ds(2 * i, 2)], probs_out.at[pl.ds(2 * i, 2)], out_sems.at[i]).wait()


def cross_one_body(count, enc_len, x, mixed_a, mixed_b, enc, gains, *refs):
    pieces, (hidden, normed, queries, kv, mixed, probs_out, weights, probs, sems, out_sems) = refs[:10], refs[10:]
    copies = copy_pieces(pieces, weights, sems)
    inner = queries.shape[1]
    part = mixed_a.shape[1]
    wait(copies)

    def enter(i):
        rows = wide(i)
        got = nt(mixed_a[...], weights[rows, pl.ds(0, part)]) + nt(mixed_b[...], weights[rows, pl.ds(part, inner - part)])
        hidden[:, rows] = x[:, rows].astype(f32) + got

    loop(hidden.shape[1] // WIDE, enter)
    v = hidden[...]
    normed[...] = (v * inverse_rms(v) * gains[1:2]).astype(bf16)

    def project_q(i):
        queries[:, wide(i)] = nn(normed[...], weights[:, wide(i, inner)]).astype(bf16)

    def project_kv(i):
        kv[:, wide(i)] = nn(enc[...], weights[:, wide(i, 2 * inner)]).astype(bf16)

    loop(inner // WIDE, project_q)
    loop(2 * inner // WIDE, project_kv)
    cross_pairs(0, count, enc_len, queries, kv, mixed, probs, probs_out, out_sems)


def cross_two_body(first, count, enc_len, hidden, queries, kv, mixed_a, *refs):
    pieces, (hidden_out, mixed, probs_out, weights, probs, sems, out_sems) = refs[:10], refs[10:]
    inner = queries.shape[1]
    part = mixed_a.shape[1]
    copies = copy_pieces(pieces, weights, sems, 4 * inner)
    cross_pairs(first, count, enc_len, queries, kv, mixed, probs, probs_out, out_sems)
    wait(copies)

    def leave(i):
        rows = wide(i)
        got = nt(mixed_a[...], weights[rows, pl.ds(0, part)]) + nt(mixed[...], weights[rows, pl.ds(part, inner - part)])
        hidden_out[:, rows] = hidden[:, rows] + got

    loop(hidden.shape[1] // WIDE, leave)


root_two_over_pi = math.sqrt(2.0 / math.pi)


def ffn_one_body(hidden, cot, gains, *refs):
    pieces, (normed, gated, slope, act, low, high, weights, sems) = refs[:10], refs[10:]
    copies = copy_pieces(pieces, weights, sems)
    ff = gated.shape[1]
    v = hidden[...]
    normed[...] = (v * inverse_rms(v) * gains[2:3]).astype(bf16)
    turned = jnp.transpose(cot[...])
    wait(copies)

    def unit(i):
        cols = wide(i)
        gate = nn(normed[...], weights[:, cols])
        up = nn(normed[...], weights[:, wide(i, ff)])
        square = gate * gate
        bend = jnp.tanh(root_two_over_pi * gate * (1.0 + 0.044715 * square))
        half = 0.5 * (1.0 + bend)
        gelu = gate * half
        steep = half + 0.5 * gate * (1.0 - bend * bend) * (root_two_over_pi * (1.0 + 3 * 0.044715 * square))
        units = (gelu * up).astype(bf16)
        gated[:, cols] = units
        slope[:, cols] = (up * steep).astype(bf16)
        act[:, cols] = gelu.astype(bf16)
        part = nn(turned, units)
        low[:, cols] = part[:HALF].astype(bf16)
        high[:, cols] = part[HALF:].astype(bf16)

    loop(ff // WIDE, unit)


def ffn_two_body(cot, normed, slope, act, *refs):
    pieces, (low, high, d_gu, weights, sems) = refs[:10], refs[10:]
    copies = copy_pieces(pieces, weights, sems)
    ff = slope.shape[1]
    turned = jnp.transpose(normed[...])
    wait(copies)

    def unit(i):
        cols, other = wide(i), wide(i, ff)
        d_gated = nn(cot[...], weights[:, cols])
        d_gate = (d_gated * slope[:, cols].astype(f32)).astype(bf16)
        d_up = (d_gated * act[:, cols].astype(f32)).astype(bf16)
        d_gu[:, cols] = d_gate
        d_gu[:, other] = d_up
        part = nn(turned, d_gate)
        low[:, cols] = part[:HALF].astype(bf16)
        high[:, cols] = part[HALF:].astype(bf16)
        part = nn(turned, d_up)
        low[:, other] = part[:HALF].astype(bf16)
        high[:, other] = part[HALF:].astype(bf16)

    loop(ff // WIDE, unit)


def ffn_three_body(hidden, cot, gains, d_gu, *refs):
    pieces, (d_hidden, d_low, d_gain, weights, sems) = refs[:10], refs[10:]
    copies = copy_pieces(pieces, weights, sems)
    wait(copies)

    def back(i):
        d_hidden[:, wide(i)] = nt(d_gu[...], weights[wide(i), :])

    loop(hidden.shape[1] // WIDE, back)
    v = hidden[...]
    d_v, d_g = norm_back(v, gains[2:3], d_hidden[...], inverse_rms(v))
    d_v = d_v + cot[...].astype(f32)
    d_hidden[...] = d_v
    d_low[...] = d_v.astype(bf16)
    d_gain[...] = d_g


def output_body(hidden, gated, perm, *refs):
    pieces, (out, weights, held, sems) = refs[:10], refs[10:]
    copies = copy_pieces(pieces, weights, sems)
    wait(copies)

    def leave(i):
        held[:, wide(i)] = (hidden[:, wide(i)] + nt(gated[...], weights[wide(i), :])).astype(bf16)

    def place(i):
        out[:, wide(i)] = nt(held[...], perm[wide(i), :]).astype(bf16)

    loop(hidden.shape[1] // WIDE, leave)
    loop(hidden.shape[1] // WIDE, place)


def enc_body(d_kv_a, d_kv_b, perm, *refs):
    pieces, (out, weights, held, sems) = refs[:10], refs[10:]
    inner = held.shape[1]
    copies = copy_pieces(pieces, weights, sems, 2 * inner)
    part = d_kv_a.shape[1] // 2
    rest = inner - part
    wait(copies)

    def leave(i):
        rows = wide(i)
        got = nt(d_kv_a[:, pl.ds(0, part)], weights[rows, pl.ds(0, part)])
        got = got + nt(d_kv_b[:, pl.ds(0, rest)], weights[rows, pl.ds(part, rest)])
        got = got + nt(d_kv_a[:, pl.ds(part, part)], weights[rows, pl.ds(inner, part)])
        got = got + nt(d_kv_b[:, pl.ds(rest, rest)], weights[rows, pl.ds(inner + part, rest)])
        held[:, rows] = got.astype(bf16)

    def place(i):
        out[:, wide(i)] = nt(held[...], perm[wide(i), :]).astype(bf16)

    loop(out.shape[1] // WIDE, leave)
    loop(out.shape[1] // WIDE, place)


def attention_back(side, rows, seen, p, d_mixed, mixed, keys, values, d_scores):
    lanes = halves((TILE, TILE))[side]
    d_out = jnp.where(lanes, d_mixed, jnp.zeros_like(d_mixed))
    delta = jnp.sum(d_out.astype(f32) * mixed.astype(f32), axis=-1, keepdims=True)
    d_s = (p.astype(f32) * (nt(d_out, values) - delta)).astype(bf16)
    d_scores[side, rows, pl.ds(0, seen)] = d_s
    return d_s, nn(d_s, keys)


def fetch_probs(probs_in, probs, in_sems):
    copies = []
    for i in range(probs.shape[0] // 2):
        copies.append(pltpu.make_async_copy(probs_in.at[pl.ds(2 * i, 2)], probs.at[pl.ds(2 * i, 2)], in_sems.at[i]))
        copies[-1].start()


def cross_back_pairs(first, count, queries, kv, mixed, d_mixed, probs_in, probs, in_sems, d_q, d_kv, d_scores):
    blocks, inner = queries.shape[0] // TILE, queries.shape[1]

    def pair(i):
        pltpu.make_async_copy(probs_in.at[pl.ds(2 * i, 2)], probs.at[pl.ds(2 * i, 2)], in_sems.at[i]).wait()
        lanes, mine = at((first + i) * TILE, TILE), at(i * TILE, TILE)
        keys, values = kv[:, lanes], kv[:, at(inner + (first + i) * TILE, TILE)]
        d_mix, here = d_mixed[:, lanes], queries[:, lanes]
        both, zero = halves(keys.shape), jnp.zeros_like(keys)
        d_k = d_v = None
        for side in range(2):
            my_keys = jnp.where(both[side], keys, zero)
            for block in range(blocks):
                rows = pl.ds(block * TILE, TILE)
                span = slice(block * TILE, (block + 1) * TILE)
                p = probs[2 * i + side, rows, :]
                _, part = attention_back(side, rows, kv.shape[0], p, d_mix[span], mixed[rows, mine], my_keys, values, d_scores)
                if side == 0:
                    d_q[rows, mine] = part.astype(bf16)
                else:
                    d_q[rows, mine] = (d_q[rows, mine].astype(f32) + part).astype(bf16)
            part_v = tn(probs[2 * i + side], jnp.where(both[side], d_mix, zero))
            part_k = tn(d_scores[side], jnp.where(both[side], here, zero))
            d_v = part_v if side == 0 else d_v + part_v
            d_k = part_k if side == 0 else d_k + part_k
        d_kv[:, mine] = d_k.astype(bf16)
        d_kv[:, at((count + i) * TILE, TILE)] = d_v.astype(bf16)

    loop(count, pair)


def cross_back_one_body(count, d_low, queries, kv, mixed, *refs):
    pieces, probs_in, (d_mixed, d_q, d_kv, weights, probs, d_scores, sems, in_sems) = refs[:10], refs[10], refs[11:]
    inner = queries.shape[1]
    copies = copy_pieces(pieces, weights, sems, 4 * inner)
    fetch_probs(probs_in, probs, in_sems)
    wait(copies)

    def enter(i):
        d_mixed[:, wide(i)] = nn(d_low[...], weights[:, wide(i)]).astype(bf16)

    loop(inner // WIDE, enter)
    cross_back_pairs(0, count, queries, kv, mixed, d_mixed, probs_in, probs, in_sems, d_q, d_kv, d_scores)


def put(low, high, cols, part):
    low[:, cols] = part[:HALF].astype(bf16)
    high[:, cols] = part[HALF:].astype(bf16)


def cross_back_two_body(first, count, *refs):
    (hidden, d_hidden, d_low, enc, gains, normed, queries, kv, mixed_a, mixed_b, one_a, one_b, d_mixed, d_q_a, d_kv_a) = refs[:15]
    pieces, probs_in = refs[15:25], refs[25]
    low, high, d_kv_b, d_out, d_out_low, d_gain, weights, probs, d_q_b, d_scores, sems, in_sems = refs[26:]
    inner = queries.shape[1]
    part = mixed_a.shape[1]
    rest = inner - part
    copies = copy_pieces(pieces, weights, sems, inner)
    fetch_probs(probs_in, probs, in_sems)
    cross_back_pairs(first, count, queries, kv, mixed_b, d_mixed, probs_in, probs, in_sems, d_q_b, d_kv_b, d_scores)
    wait(copies)

    def back(i):
        got = nt(d_q_a[...], weights[wide(i), pl.ds(0, part)]) + nt(d_q_b[...], weights[wide(i), pl.ds(part, rest)])
        d_out[:, wide(i)] = got

    loop(hidden.shape[1] // WIDE, back)
    v = hidden[...]
    d_v, d_g = norm_back(v, gains[1:2], d_out[...], inverse_rms(v))
    d_v = d_v + d_hidden[...]
    d_out[...] = d_v
    d_out_low[...] = d_v.astype(bf16)
    d_gain[...] = d_g
    turned = jnp.transpose(d_out_low[...])
    put(low, high, pl.ds(0, part), nn(turned, one_a[...]))
    put(low, high, pl.ds(part, rest), nn(turned, one_b[...]))
    turned = jnp.transpose(normed[...])
    put(low, high, pl.ds(inner, part), nn(turned, d_q_a[...]))
    put(low, high, pl.ds(inner + part, rest), nn(turned, d_q_b[...]))
    turned = jnp.transpose(enc[...])
    for i in range(2):
        put(low, high, pl.ds((2 + i) * inner, part), nn(turned, d_kv_a[:, pl.ds(i * part, part)]))
        put(low, high, pl.ds((2 + i) * inner + part, rest), nn(turned, d_kv_b[:, pl.ds(i * rest, rest)]))
    turned = jnp.transpose(d_low[...])
    put(low, high, pl.ds(4 * inner, part), nn(turned, mixed_a[...]))
    put(low, high, pl.ds(4 * inner + part, rest), nn(turned, mixed_b[...]))


def self_back_pairs(first, count, qkv, mixed, d_mixed, probs_in, probs, in_sems, d_qkv, d_scores, work, sums):
    tokens, inner = qkv.shape[0], qkv.shape[1] // 3
    blocks = tokens // TILE

    def pair(i):
        pltpu.make_async_copy(probs_in.at[pl.ds(2 * i, 2)], probs.at[pl.ds(2 * i, 2)], in_sems.at[i]).wait()
        lanes, mine = at((first + i) * TILE, TILE), at(i * TILE, TILE)
        here, keys = qkv[:, lanes], qkv[:, at(inner + (first + i) * TILE, TILE)]
        values = qkv[:, at(2 * inner + (first + i) * TILE, TILE)]
        d_mix = d_mixed[:, lanes]
        both, zero = halves(keys.shape), jnp.zeros_like(keys)
        for side in range(2):
            head = 2 * i + side
            my_keys = jnp.where(both[side], keys, zero)
            diagonal = [None] * blocks
            for block in range(blocks):
                rows = pl.ds(block * TILE, TILE)
                span = slice(block * TILE, (block + 1) * TILE)
                seen = (block + 1) * TILE
                p = probs[head, rows, pl.ds(0, seen)]
                d_s, part = attention_back(
                    side, rows, seen, p, d_mix[span], mixed[rows, mine], my_keys[:seen], values[:seen], d_scores
                )
                wider = d_s.astype(f32)
                for j in range(block + 1):
                    tile = wider[:, j * TILE : (j + 1) * TILE]
                    apart = block - j
                    diagonal[apart] = tile if diagonal[apart] is None else diagonal[apart] + tile
                if side == 0:
                    d_qkv[rows, mine] = part.astype(bf16)
                else:
                    d_qkv[rows, mine] = (d_qkv[rows, mine].astype(f32) + part).astype(bf16)
            for apart in range(blocks):
                tile = jnp.concatenate([diagonal[apart], jnp.zeros((TILE, TILE), f32)], axis=1)
                folded = tile[:8]
                for group in range(1, TILE // 8):
                    folded = folded + pltpu.roll(tile[group * 8 : group * 8 + 8], 2 * TILE - 8 * group, 1)
                sums[head * blocks + apart] = folded
            d_o = jnp.where(both[side], d_mix, zero)
            q_o = jnp.where(both[side], here, zero)
            for j in range(blocks):
                start = j * TILE
                rows, out_rows = pl.ds(start, tokens - start), pl.ds(start, TILE)
                part_v = tn(probs[head, rows, pl.ds(start, TILE)], d_o[start:])
                part_k = tn(d_scores[side, rows, pl.ds(start, TILE)], q_o[start:])
                if side == 0:
                    work[0, out_rows, :] = part_v
                    work[1, out_rows, :] = part_k
                else:
                    d_qkv[out_rows, at((count + i) * TILE, TILE)] = (work[1, out_rows, :] + part_k).astype(bf16)
                    d_qkv[out_rows, at((2 * count + i) * TILE, TILE)] = (work[0, out_rows, :] + part_v).astype(bf16)

    loop(count, pair)


def self_back_one_body(count, d_low, normed, qkv, mixed, *refs):
    pieces, probs_in = refs[:10], refs[10]
    low, high, d_mixed, d_qkv, sums, weights, probs, d_scores, work, sems, in_sems = refs[11:]
    inner = qkv.shape[1] // 3
    copies = copy_pieces(pieces, weights, sems)
    fetch_probs(probs_in, probs, in_sems)
    turned = jnp.transpose(normed[...])
    wait(copies)

    def enter(i):
        d_mixed[:, wide(i)] = nn(d_low[...], weights[:, wide(i)]).astype(bf16)

    loop(inner // WIDE, enter)
    self_back_pairs(0, count, qkv, mixed, d_mixed, probs_in, probs, in_sems, d_qkv, d_scores, work, sums)
    part = count * TILE

    def grads(i):
        cols = pl.ds(pl.multiple_of(i * part, TILE), part)
        put(low, high, cols, nn(turned, d_qkv[:, cols]))

    loop(3, grads)


def self_back_two_body(first, count, *refs):
    x, d_hidden, gains, normed, qkv, mixed, gain_c, gain_f, d_mixed, d_qkv_a, perm = refs[:11]
    pieces, probs_in = refs[11:21], refs[21]
    low, high, d_x, sums, weights, probs, d_qkv, d_scores, work, total, sems, in_sems = refs[22:]
    inner = qkv.shape[1] // 3
    copies = copy_pieces(pieces, weights, sems, TILE)
    fetch_probs(probs_in, probs, in_sems)
    turned = jnp.transpose(normed[...])
    self_back_pairs(first, count, qkv, mixed, d_mixed, probs_in, probs, in_sems, d_qkv, d_scores, work, sums)
    wait(copies)
    part, rest = inner - count * TILE, count * TILE

    def back(i):
        got = None
        for j in range(3):
            one = nt(d_qkv_a[:, pl.ds(j * part, part)], weights[wide(i), pl.ds(j * inner, part)])
            got = one if got is None else got + one
            got = got + nt(d_qkv[:, pl.ds(j * rest, rest)], weights[wide(i), pl.ds(j * inner + part, rest)])
        total[:, wide(i)] = got

    loop(x.shape[1] // WIDE, back)
    v = x[...].astype(f32)
    d_v, d_g = norm_back(v, gains[0:1], total[...], inverse_rms(v))
    d_x[...] = (d_v + d_hidden[...]).astype(bf16)
    rows = jnp.concatenate([d_g, gain_c[...], gain_f[...], jnp.zeros((TILE - 3, d_g.shape[1]), f32)], axis=0)
    put(low, high, pl.ds(0, TILE), jnp.transpose(rows))

    def grads(i):
        cols = pl.ds(pl.multiple_of(i * rest, TILE), rest)
        put(low, high, pl.ds(pl.multiple_of(TILE + i * rest, TILE), rest), nn(turned, d_qkv[:, cols]))

    loop(3, grads)


def place_body(value, perm, out):
    def place(i):
        out[:, wide(i)] = nt(value[...], perm[wide(i), :]).astype(bf16)

    loop(out.shape[1] // WIDE, place)


def pack_body(*refs):
    gains, sq, sk, sv, so, cq, ck, cv, co, fg, fu, fo, first, second, third, fourth = refs
    for out, parts in ((first, (gains, sq, sk, sv)), (second, (so, cq, ck, cv, co)), (third, (fg, fu)), (fourth, (fo,))):
        start = 0
        for part in parts:
            out[:, pl.ds(start, part.shape[1])] = part[...]
            start += part.shape[1]


def core_add_body(low, got, own, to_x, to_y, far_x, far_y):
    size = HALF // 4
    total = low[...].astype(f32) + got[...].astype(f32)
    total = total.astype(bf16)
    own[...] = total[:size]
    to_x[...] = total[size : 2 * size]
    to_y[...] = total[2 * size : 3 * size]
    far_x[...] = total[3 * size : 3 * size + size // 2]
    far_y[...] = total[3 * size + size // 2 :]


def core_add(low, got):
    rows, cols = low.shape
    size = rows // 4
    steps = max(n for n in (5, 4, 3, 2, 1) if cols % (n * TILE) == 0)
    block = cols // steps
    sizes = (size, size, size, size // 2, size // 2)
    return pl.pallas_call(
        core_add_body,
        grid=(steps,),
        out_shape=[shape((s, cols), bf16) for s in sizes],
        in_specs=[pl.BlockSpec((rows, block), lambda i: (0, i))] * 2,
        out_specs=[pl.BlockSpec((s, block), lambda i: (0, i)) for s in sizes],
        compiler_params=pltpu.CompilerParams(vmem_limit_bytes=48 * 2**20),
        cost_estimate=pl.CostEstimate(flops=rows * cols, bytes_accessed=6 * rows * cols, transcendentals=0),
        name="core_add",
    )(low, got)


def plane_add_body(to_x, got_x, to_y, got_y, out_x, out_y):
    half = got_x.shape[0]
    out_x[pl.ds(0, half), :] = to_x[pl.ds(0, half), :]
    out_x[pl.ds(half, half), :] = (to_x[pl.ds(half, half), :].astype(f32) + got_x[...].astype(f32)).astype(bf16)
    out_y[pl.ds(0, half), :] = (to_y[pl.ds(0, half), :].astype(f32) + got_y[...].astype(f32)).astype(bf16)
    out_y[pl.ds(half, half), :] = to_y[pl.ds(half, half), :]


def plane_add(to_x, got_x, to_y, got_y):
    return call(
        plane_add_body, "plane_add", [VMEM] * 4, [(shape(to_x.shape, bf16), VMEM)] * 2, [], 2.0, to_x, got_x, to_y, got_y
    )


def own_add_body(own, got_x, got_y, keep, away):
    half = keep.shape[0]
    total = own[...].astype(f32) + got_x[...].astype(f32) + got_y[...].astype(f32)
    keep[...] = total[:half].astype(bf16)
    away[...] = total[half:].astype(bf16)


def own_add(own, got_x, got_y):
    half = shape((own.shape[0] // 2, own.shape[1]), bf16)
    return call(own_add_body, "own_add", [VMEM] * 3, [(half, VMEM)] * 2, [], 2.0, own, got_x, got_y)


def line_add_body(own, got, keep, away):
    half = keep.shape[0]
    total = own[...].astype(f32) + got[...].astype(f32)
    keep[...] = total[:half].astype(bf16)
    away[...] = total[half:].astype(bf16)


def line_add(own, got):
    half = shape((own.shape[0] // 2, own.shape[1]), bf16)
    return call(line_add_body, "line_add", [VMEM] * 2, [(half, VMEM)] * 2, [], 1.5, own, got)


def last_add_body(own, got, *outs):
    start = 0
    for out in outs:
        cols = pl.ds(start, out.shape[1])
        out[...] = own[:, cols].astype(f32) + got[:, cols].astype(f32)
        start += out.shape[1]


def last_add(own, got, widths):
    outs = [(shape((own.shape[0], w), f32), VMEM) for w in widths]
    return call(last_add_body, "last_add", [VMEM] * 2, outs, [], 1.5, own, got)


def bucket_of(distance):
    bucket = np.where(distance < 16, distance, 16)
    for edge in bucket_edges:
        bucket = bucket + (distance >= edge)
    return np.maximum(bucket, 0)


def split_last_body(own_a, got_a, own_b, got_b, gains, *outs):
    part = own_a.shape[1] // 3
    rest = (own_b.shape[1] - TILE) // 3
    gains[...] = own_b[:, pl.ds(0, TILE)].astype(f32) + got_b[:, pl.ds(0, TILE)].astype(f32)
    for i, out in enumerate(outs):
        cols = pl.ds(i * part, part)
        out[:, pl.ds(0, part)] = own_a[:, cols].astype(f32) + got_a[:, cols].astype(f32)
        cols = pl.ds(TILE + i * rest, rest)
        out[:, pl.ds(part, rest)] = own_b[:, cols].astype(f32) + got_b[:, cols].astype(f32)


def layer(
    cube,
    states,
    encoded,
    cotangent,
    dec_lens,
    enc_lens,
    self_query,
    self_key,
    self_value,
    self_out,
    cross_query,
    cross_key,
    cross_value,
    cross_out,
    ffn_gate,
    ffn_up,
    ffn_out,
    gain_self,
    gain_cross,
    gain_ffn,
    table,
):
    _, tokens, width = states.shape
    enc_tokens = encoded.shape[1]
    inner, ff = self_query.shape[1], ffn_gate.shape[1]
    own_rows = self_query.shape[0]
    blocks = tokens // TILE
    pairs = inner // TILE
    early = pairs // 2
    late = pairs - early
    part, rest = early * TILE, late * TILE
    sems = pltpu.SemaphoreType.DMA

    def weight_mem(cols):
        return pltpu.VMEM((width, cols), bf16)

    def mem(*dims):
        return pltpu.VMEM(dims, bf16)

    gains_in = jnp.pad(jnp.stack([gain_self, gain_cross, gain_ffn], axis=1), ((0, 0), (0, TILE - 3)))
    widths = (TILE + 3 * inner, 5 * inner, 2 * ff, ff)
    packed = call(
        pack_body,
        "pack",
        [VMEM] * 12,
        [(shape((own_rows, w), bf16), VMEM) for w in widths],
        [],
        2.0,
        *(gains_in, self_query, self_key, self_value, self_out, cross_query, cross_key, cross_value, cross_out, ffn_gate, ffn_up, ffn_out),
    )
    A, B, C, D = (Gather(cube, p) for p in packed)
    perm = cube.permutation(width)
    x = nn(states[0], perm).astype(bf16)

    lane = np.arange(2 * TILE)
    signed = np.where(lane < TILE, lane, lane - 2 * TILE)
    distance = np.arange(blocks)[:, None] * TILE - signed[None, :]
    chosen = (np.arange(NB)[:, None] == bucket_of(distance).reshape(1, -1)).astype(np.float32)
    lines = lax.dot_general(table, jnp.asarray(chosen, bf16), (((0,), (0,)), ((), ())), preferred_element_type=f32)
    lines = jnp.where(jnp.asarray(distance.reshape(1, -1) >= 0), lines, masked_score)
    lines = lines.reshape(H * blocks, 2 * TILE)
    (bias,) = call(bias_body, "bias", [VMEM], [(shape((H * blocks, TILE, TILE), f32), VMEM)], [], 7.0, lines)
    enc = nn(encoded[0], perm).astype(bf16)
    cot = nn(cotangent[0], perm).astype(bf16)

    token_bf = shape((tokens, width), bf16)
    token_f32 = shape((tokens, width), f32)
    row_f32 = shape((1, width), f32)

    A.line(cube.rest)
    A.own, B.own, C.own, D.own = tie(A.own, B.own, C.own, D.own)
    A.plane()
    B.line(cube.rest[:1])
    A.own, A.over_x, A.over_y, B.own, C.own, D.own, enc, cot, bias = tie(A.own, A.over_x, A.over_y, B.own, C.own, D.own, enc, cot, bias)
    A.far()
    B.line(cube.rest[1:])
    A.far_one, A.far_two, B.own, C.own, D.own = tie(A.far_one, A.far_two, B.own, C.own, D.own)
    A.across()
    B.plane()
    C.line(cube.rest[:1])
    gains, normed_one, qkv, mixed_one_a, probs_one_a = call(
        lambda *refs: self_one_body(early, *refs),
        "self_one",
        [SMEM, VMEM, VMEM] + [ANY] * 10,
        [
            (shape((8, width), f32), VMEM),
            (token_bf, VMEM),
            (shape((tokens, 3 * inner), bf16), VMEM),
            (shape((tokens, part), bf16), VMEM),
            (shape((2 * early, tokens, tokens), bf16), ANY),
        ],
        [weight_mem(widths[0]), mem(2 * early, tokens, tokens), sems((10,)), sems((early,))],
        16.0,
        *(dec_lens, x, bias, *A.pieces),
    )
    qkv, B.own, B.over_x, B.over_y, C.own, D.own = tie(qkv, B.own, B.over_x, B.over_y, C.own, D.own)
    B.far()
    C.line(cube.rest[1:])
    mixed_one_b, probs_one_b = call(
        lambda *refs: self_two_body(early, late, *refs),
        "self_two",
        [SMEM, VMEM, VMEM],
        [(shape((tokens, rest), bf16), VMEM), (shape((2 * late, tokens, tokens), bf16), ANY)],
        [mem(2 * late, tokens, tokens), sems((late,))],
        13.0,
        *(dec_lens, bias, qkv),
    )
    mixed_one_b, B.own, B.over_x, B.over_y, B.far_one, B.far_two, C.own, D.own = tie(
        mixed_one_b, B.own, B.over_x, B.over_y, B.far_one, B.far_two, C.own, D.own
    )
    B.across()
    C.plane()
    D.line(cube.rest[:1])
    hidden_one, normed_two, q_two, kv_two, mixed_two_a, probs_two_a = call(
        lambda *refs: cross_one_body(early, *refs),
        "cross_one",
        [SMEM] + [VMEM] * 5 + [ANY] * 10,
        [
            (token_f32, VMEM),
            (token_bf, VMEM),
            (shape((tokens, inner), bf16), VMEM),
            (shape((enc_tokens, 2 * inner), bf16), VMEM),
            (shape((tokens, part), bf16), VMEM),
            (shape((2 * early, tokens, enc_tokens), bf16), ANY),
        ],
        [weight_mem(4 * inner), mem(2 * early, tokens, enc_tokens), sems((10,)), sems((early,))],
        18.0,
        *(enc_lens, x, mixed_one_a, mixed_one_b, enc, gains, *B.pieces),
    )
    q_two, C.own, C.over_x, C.over_y, D.own = tie(q_two, C.own, C.over_x, C.over_y, D.own)
    C.far()
    D.line(cube.rest[1:])
    hidden_two, mixed_two_b, probs_two_b = call(
        lambda *refs: cross_two_body(early, late, *refs),
        "cross_two",
        [SMEM] + [VMEM] * 4 + [ANY] * 10,
        [(token_f32, VMEM), (shape((tokens, rest), bf16), VMEM), (shape((2 * late, tokens, enc_tokens), bf16), ANY)],
        [weight_mem(inner), mem(2 * late, tokens, enc_tokens), sems((10,)), sems((late,))],
        14.0,
        *(enc_lens, hidden_one, q_two, kv_two, mixed_two_a, *B.pieces),
    )
    hidden_two, C.own, C.over_x, C.over_y, C.far_one, C.far_two, D.own = tie(
        hidden_two, C.own, C.over_x, C.over_y, C.far_one, C.far_two, D.own
    )
    C.across()
    D.plane()
    units = shape((tokens, ff), bf16)
    half_ff = shape((HALF, ff), bf16)
    normed_three, gated, slope, act, fo_low, fo_high = call(
        ffn_one_body,
        "ffn_one",
        [VMEM] * 3 + [ANY] * 10,
        [(token_bf, VMEM)] + [(units, VMEM)] * 3 + [(half_ff, VMEM)] * 2,
        [weight_mem(2 * ff), sems((10,))],
        14.0,
        *(hidden_two, cot, gains, *C.pieces),
    )
    fo_low, fo_high, slope, D.own, D.over_x, D.over_y = tie(fo_low, fo_high, slope, D.own, D.over_x, D.over_y)
    D.far()
    R1 = Reduce(cube, fo_low, fo_high)
    D.across()
    half_gu = shape((HALF, 2 * ff), bf16)
    gu_low, gu_high, d_gu = call(
        ffn_two_body,
        "ffn_two",
        [VMEM] * 4 + [ANY] * 10,
        [(half_gu, VMEM), (half_gu, VMEM), (shape((tokens, 2 * ff), bf16), VMEM)],
        [weight_mem(ff), sems((10,))],
        14.0,
        *(cot, normed_three, slope, act, *D.pieces),
    )
    R1.got, gu_low, gu_high, d_gu = tie(R1.got, gu_low, gu_high, d_gu)
    R1.far()
    R2 = Reduce(cube, gu_low, gu_high)
    d_hidden_two, d_low_two, gain_f = call(
        ffn_three_body,
        "ffn_three",
        [VMEM] * 4 + [ANY] * 10,
        [(token_f32, VMEM), (token_bf, VMEM), (row_f32, VMEM)],
        [weight_mem(2 * ff), sems((10,))],
        8.0,
        *(hidden_two, cot, gains, d_gu, *C.pieces),
    )
    R1.got_x, R1.got_y, R2.got, d_low_two = tie(R1.got_x, R1.got_y, R2.got, d_low_two)
    R1.plane()
    R2.far()
    d_mixed_two, d_q_a, d_kv_a = call(
        lambda *refs: cross_back_one_body(early, *refs),
        "cross_back_one",
        [VMEM] * 4 + [ANY] * 11,
        [
            (shape((tokens, inner), bf16), VMEM),
            (shape((tokens, part), bf16), VMEM),
            (shape((enc_tokens, 2 * part), bf16), VMEM),
        ],
        [
            weight_mem(inner),
            mem(2 * early, tokens, enc_tokens),
            mem(2, tokens, enc_tokens),
            sems((10,)),
            sems((early,)),
        ],
        14.0,
        *(d_low_two, q_two, kv_two, mixed_two_a, *B.pieces, probs_two_a),
    )
    R1.got_x, R1.got_y, R2.got_x, R2.got_y, d_mixed_two = tie(R1.got_x, R1.got_y, R2.got_x, R2.got_y, d_mixed_two)
    R1.line()
    R2.plane()
    half_cross = shape((HALF, 5 * inner), bf16)
    cross_low, cross_high, d_kv_b, d_hidden_one, d_low_one, gain_c = call(
        lambda *refs: cross_back_two_body(early, late, *refs),
        "cross_back_two",
        [VMEM] * 15 + [ANY] * 11,
        [
            (half_cross, VMEM),
            (half_cross, VMEM),
            (shape((enc_tokens, 2 * rest), bf16), VMEM),
            (token_f32, VMEM),
            (token_bf, VMEM),
            (row_f32, VMEM),
        ],
        [
            weight_mem(inner),
            mem(2 * late, tokens, enc_tokens),
            mem(tokens, rest),
            mem(2, tokens, enc_tokens),
            sems((10,)),
            sems((late,)),
        ],
        20.0,
        *(hidden_one, d_hidden_two, d_low_two, enc, gains, normed_two, q_two, kv_two, mixed_two_a, mixed_two_b),
        *(mixed_one_a, mixed_one_b, d_mixed_two, d_q_a, d_kv_a, *B.pieces, probs_two_b),
    )
    R1.got, R2.got_x, R2.got_y, cross_low, cross_high, d_low_one = tie(
        R1.got, R2.got_x, R2.got_y, cross_low, cross_high, d_low_one
    )
    R3 = Reduce(cube, cross_low, cross_high)
    R1.rest()
    R2.line()
    (output,) = call(
        output_body,
        "output",
        [VMEM] * 3 + [ANY] * 10,
        [(token_bf, VMEM)],
        [weight_mem(ff), mem(tokens, width), sems((10,))],
        7.0,
        *(tie(hidden_two, cross_low)[0], gated, perm, *D.pieces),
    )
    R3.got, output, d_low_one = tie(R3.got, output, d_low_one)
    R3.far()
    half_a = shape((HALF, 3 * part), bf16)
    sums_a_shape = shape((2 * early * blocks, 8, 2 * TILE), f32)
    self_low_a, self_high_a, d_mixed_one, d_qkv_a, sums_a = call(
        lambda *refs: self_back_one_body(early, *refs),
        "self_back_one",
        [VMEM] * 4 + [ANY] * 11,
        [
            (half_a, VMEM),
            (half_a, VMEM),
            (shape((tokens, inner), bf16), VMEM),
            (shape((tokens, 3 * part), bf16), VMEM),
            (sums_a_shape, VMEM),
        ],
        [
            weight_mem(inner),
            mem(2 * early, tokens, tokens),
            mem(2, tokens, tokens),
            pltpu.VMEM((2, tokens, TILE), f32),
            sems((10,)),
            sems((early,)),
        ],
        16.0,
        *(d_low_one, normed_one, qkv, mixed_one_a, *B.pieces, probs_one_a),
    )
    R1.got, R2.got, R3.got_x, R3.got_y, self_low_a, self_high_a, d_qkv_a = tie(
        R1.got, R2.got, R3.got_x, R3.got_y, self_low_a, self_high_a, d_qkv_a
    )
    R4 = Reduce(cube, self_low_a, self_high_a)
    R3.plane()
    R2.rest()
    (g_fo,) = R1.last((ff,))
    half_b = shape((HALF, TILE + 3 * rest), bf16)
    sums_b_shape = shape((2 * late * blocks, 8, 2 * TILE), f32)
    self_low_b, self_high_b, d_x, sums_b = call(
        lambda *refs: self_back_two_body(early, late, *refs),
        "self_back_two",
        [VMEM] * 11 + [ANY] * 11,
        [(half_b, VMEM), (half_b, VMEM), (token_bf, VMEM), (sums_b_shape, VMEM)],
        [
            weight_mem(3 * inner),
            mem(2 * late, tokens, tokens),
            mem(tokens, 3 * rest),
            mem(2, tokens, tokens),
            pltpu.VMEM((2, tokens, TILE), f32),
            pltpu.VMEM((tokens, width), f32),
            sems((10,)),
            sems((late,)),
        ],
        18.0,
        *(x, d_hidden_one, gains, normed_one, qkv, mixed_one_b, gain_c, gain_f, d_mixed_one, d_qkv_a, perm),
        *(*A.pieces, probs_one_b),
    )
    R4.got, R3.got_x, R3.got_y, R2.got, self_low_b, self_high_b, d_x, sums_b = tie(
        R4.got, R3.got_x, R3.got_y, R2.got, self_low_b, self_high_b, d_x, sums_b
    )
    R5 = Reduce(cube, self_low_b, self_high_b)
    R4.far()
    R3.line()
    (grad_enc,) = call(
        enc_body,
        "grad_encoded",
        [VMEM] * 3 + [ANY] * 10,
        [(shape((enc_tokens, width), bf16), VMEM)],
        [weight_mem(2 * inner), mem(enc_tokens, width), sems((10,))],
        7.0,
        *(tie(d_kv_a, sums_b)[0], d_kv_b, perm, *B.pieces),
    )
    R5.far()
    R4.plane()
    R3.rest()
    (grad_states,) = call(place_body, "grad_states", [VMEM] * 2, [(token_bf, VMEM)], [], 3.0, d_x, perm)
    g_fg, g_fu = R2.last((ff, ff))

    apart = distance[:, None, :] + np.arange(8)[None, :, None]
    counted = (np.arange(NB)[:, None] == bucket_of(apart).reshape(1, -1)) & (apart.reshape(1, -1) >= 0)
    sums = jnp.concatenate([sums_a, sums_b], axis=0).reshape(H, blocks * 16 * TILE)
    table_part = lax.dot_general(
        jnp.asarray(counted.astype(np.float32)), sums, (((1,), (1,)), ((), ())), precision=lax.Precision.HIGHEST
    )
    grad_table = cube.all_sum(table_part)

    R5.plane()
    R4.line()
    g_so, g_cq, g_ck, g_cv, g_co = R3.last((inner,) * 5)
    R5.line()
    R4.rest()
    R5.rest()
    sizes = (TILE, inner, inner, inner)
    g_gains, g_sq, g_sk, g_sv = call(
        split_last_body,
        "last_self",
        [VMEM] * 4,
        [(shape((own_rows, w), f32), VMEM) for w in sizes],
        [],
        1.5,
        *(R4.own, R4.got, R5.own, R5.got),
    )
    return (
        output[None],
        grad_states[None],
        grad_enc[None],
        g_sq,
        g_sk,
        g_sv,
        g_so,
        g_cq,
        g_ck,
        g_cv,
        g_co,
        g_fg,
        g_fu,
        g_fo,
        g_gains[:, 0],
        g_gains[:, 1],
        g_gains[:, 2],
        grad_table,
    )


def solution(mesh):
    cube = Cube(mesh)
    both = ("gx", "gy")
    row, flat, one = P(both, None, None), P(both, None), P(both)
    in_specs = (row, row, row, one, one) + (flat,) * 11 + (one,) * 3 + (P(),)
    out_specs = (row, row, row) + (flat,) * 11 + (one,) * 3 + (P(),)

    def per_device(*args):
        return layer(cube, *args)

    return jax.shard_map(per_device, mesh=mesh, in_specs=in_specs, out_specs=out_specs, check_vma=False)
```

```python
import math

import jax
import jax.numpy as jnp
import numpy as np
from jax import lax
from jax.experimental import pallas as pl
from jax.experimental.pallas import tpu as pltpu
from jax.sharding import PartitionSpec as P

H = 12
HD = 64
NB = 32

norm_eps = 1e-06
masked_score = -1000000000.0
bucket_edges = [int(math.ceil(16 * 8 ** (power / 16.0))) for power in range(1, 16)]

bf16 = jnp.bfloat16
f32 = jnp.float32


class Cube:
    def __init__(self, mesh):
        self.nx, self.ny = mesh.shape["gx"], mesh.shape["gy"]
        self.n = self.nx * self.ny
        self.core, self.y, self.x = ("gx", 1), ("gx", 2), ("gy", 1)
        self.rest = []
        bit = self.ny // 2
        while bit > 1:
            self.rest.append(("gy", bit))
            bit //= 2
        bit = self.nx // 2
        while bit > 2:
            self.rest.append(("gx", bit))
            bit //= 2

    def send(self, value, step):
        axis, bit = step
        size = self.nx if axis == "gx" else self.ny
        return lax.ppermute(value, axis, [(i, i ^ bit) for i in range(size)])

    def owners(self):
        mask_x, mask_y = np.zeros(self.n, np.int32), np.zeros(self.n, np.int32)
        for place in range(self.n):
            steps = []
            inner, block = place % (self.n // 8), (place // (self.n // 8)) % 4
            for at_bit, step in enumerate(self.rest):
                if (inner >> at_bit) & 1:
                    steps.append(step)
            if block & 1:
                steps.append(self.x)
            if block & 2:
                steps.append(self.y)
            if place >= self.n // 2:
                steps.append(self.core)
            for axis, bit in steps:
                if axis == "gx":
                    mask_x[place] ^= bit
                else:
                    mask_y[place] ^= bit
        gx, gy = lax.axis_index("gx"), lax.axis_index("gy")
        return (gx ^ jnp.asarray(mask_x)) * self.ny + (gy ^ jnp.asarray(mask_y))

    def permutation(self, width):
        rows = width // self.n
        feature = (self.owners()[:, None] * rows + jnp.arange(rows, dtype=jnp.int32)).reshape(1, width)
        return (jnp.arange(width, dtype=jnp.int32)[:, None] == feature).astype(bf16)

    def all_sum(self, value):
        for step in [self.core, self.x, self.y] + self.rest:
            value = value + self.send(value, step)
        return value


class Gather:
    def __init__(self, cube, packed):
        self.cube, self.held = cube, [packed]

    def line(self, step):
        own = jnp.concatenate(self.held, axis=0)
        self.held = [own, self.cube.send(own, step)]

    def plane(self):
        own = jnp.concatenate(self.held, axis=0)
        self.held = [own, self.cube.send(own, self.cube.x), self.cube.send(own, self.cube.y)]

    def far(self):
        own, over_x, over_y = self.held
        half = own.shape[0] // 2
        far_one, far_two = self.cube.send(over_y[:half], self.cube.x), self.cube.send(over_x[half:], self.cube.y)
        near = stack(own, over_x, over_y)
        self.held = [near, far_one, far_two, self.cube.send(near, self.cube.core)]

    def across(self):
        self.held = self.held + [self.cube.send(v, self.cube.core) for v in self.held[1:3]]


class Reduce:
    def __init__(self, cube, low, high):
        self.cube, self.held = cube, []
        self.more(low, high)

    def more(self, low, high):
        self.held = self.held + [low, self.cube.send(high, self.cube.core)]

    def far(self):
        cube = self.cube
        own, to_x, to_y, far_x, far_y = core_add(*self.held)
        self.held = [own, to_x, cube.send(far_y, cube.y), to_y, cube.send(far_x, cube.x)]

    def plane(self):
        cube = self.cube
        to_x, to_y = plane_add(*self.held[1:])
        self.held = [self.held[0], cube.send(to_x, cube.x), cube.send(to_y, cube.y)]

    def line(self):
        own, away = own_add(*self.held)
        self.held = [own, self.cube.send(away, self.cube.rest[-1])]

    def rest(self):
        for step in self.cube.rest[-2::-1]:
            own, away = line_add(*self.held)
            self.held = [own, self.cube.send(away, step)]

    def last(self, widths):
        return last_add(*self.held, widths)


class Order:
    def __init__(self, token):
        self.token = token

    def __call__(self, values, *transfers):
        held = [v for t in transfers for v in t.held]
        out = list(lax.optimization_barrier((self.token, *values, *held)))
        self.token, place = out[0], 1 + len(values)
        for t in transfers:
            t.held = out[place : place + len(t.held)]
            place += len(t.held)
        return out[1 : 1 + len(values)]


TILE = 128
HALF = 384


def nn(left, right):
    return lax.dot_general(left, right, (((1,), (0,)), ((), ())), preferred_element_type=f32)


def nt(left, right):
    return lax.dot_general(left, right, (((1,), (1,)), ((), ())), preferred_element_type=f32)


def tn(left, right):
    return lax.dot_general(left, right, (((0,), (0,)), ((), ())), preferred_element_type=f32)


def at(start, size):
    return pl.ds(start, size)


VMEM = pl.BlockSpec(memory_space=pltpu.VMEM)
SMEM = pl.BlockSpec(memory_space=pltpu.SMEM)
FAR = pl.BlockSpec(memory_space=pltpu.HBM)


def shape(dims, kind):
    return jax.ShapeDtypeStruct(dims, kind)


def near(dims, kind):
    return pltpu.VMEM(dims, kind)


def in_bytes(spec, dims, kind):
    if spec.memory_space is not pltpu.VMEM:
        return 0
    rows = math.prod(dims[:-1])
    return -(-rows // 16) * 16 * max(dims[-1], TILE) * jnp.dtype(kind).itemsize


def call(body, name, ins, outs, scratch, cost, *args, spare=6):
    held = sum(in_bytes(spec, a.shape, a.dtype) for spec, a in zip(ins, args))
    held += sum(in_bytes(spec, o.shape, o.dtype) for o, spec in outs)
    held += sum(in_bytes(VMEM, s.shape, s.dtype) for s in scratch if getattr(s, "memory_space", None) is pltpu.VMEM)
    return pl.pallas_call(
        body,
        out_shape=[o[0] for o in outs],
        in_specs=ins,
        out_specs=[o[1] for o in outs],
        scratch_shapes=scratch,
        compiler_params=pltpu.CompilerParams(vmem_limit_bytes=held + spare * 2**20),
        cost_estimate=pl.CostEstimate(flops=0, bytes_accessed=int(cost * 3.6e4), transcendentals=0),
        name=name,
    )(*args)


def halves(value):
    lane = lax.broadcasted_iota(jnp.int32, value, 1)
    return (lane < HD, lane >= HD)


def inverse_rms(v):
    return lax.rsqrt(jnp.mean(v * v, axis=-1, keepdims=True) + norm_eps)


def norm_back(v, gain, dy, r):
    scaled = dy * gain
    mean = jnp.mean(scaled * v, axis=-1, keepdims=True)
    d_v = (scaled - v * (mean * (r * r))) * r
    return d_v, jnp.sum(dy * (v * r), axis=0, keepdims=True)


def softmax_rows(scores):
    top = jnp.max(scores, axis=-1, keepdims=True)
    expo = jnp.exp(scores - top)
    return (expo * (1.0 / jnp.sum(expo, axis=-1, keepdims=True))).astype(bf16)


def bias_body(lines, out):
    def one(i, _):
        line = lines[pl.ds(i, 1), :]
        wide = jnp.broadcast_to(line, (TILE, 2 * TILE))
        out[i] = pltpu.roll(wide, 0, 1, stride=1, stride_axis=0)[:, :TILE]
        return 0

    lax.fori_loop(0, out.shape[0], one, 0)


def copy_pieces(pieces, weights, sems, start=0):
    copies, row, cols = [], 0, weights.shape[1]
    for i, piece in enumerate(pieces):
        size = piece.shape[0]
        source = piece.at[:, pl.ds(start, cols)]
        copies.append(pltpu.make_async_copy(source, weights.at[pl.ds(row, size), :], sems.at[i]))
        copies[-1].start()
        row += size
    return copies


def wait(copies):
    for copy in copies:
        copy.wait()


def loop(count, body):
    for i in range(count):
        body(i)


WIDE = 2 * TILE


def wide(i, start=0):
    return pl.ds(start + i * WIDE, WIDE)


def self_pairs(first, count, dec_len, bias, qkv, mixed, probs_out, probs, out_sems):
    tokens, inner = qkv.shape[0], qkv.shape[1] // 3
    blocks = tokens // TILE
    places = lax.broadcasted_iota(jnp.int32, (1, tokens), 1)
    limit = jnp.where(places < dec_len[0], 0.0, masked_score)

    def pair(i):
        lanes = at(i * TILE, TILE)
        keys = qkv[:, at(inner + i * TILE, TILE)]
        values = qkv[:, at(2 * inner + i * TILE, TILE)]
        both = halves((TILE, TILE))
        for block in range(blocks):
            rows = pl.ds(block * TILE, TILE)
            seen = (block + 1) * TILE
            queries = qkv[rows, lanes]
            result = None
            for side in range(2):
                mine = jnp.where(both[side], queries, jnp.zeros_like(queries))
                scores = nt(mine, keys[:seen])
                strip = [bias[(2 * (first + i) + side) * blocks + block - j] for j in range(block + 1)]
                strip = strip[0] if block == 0 else jnp.concatenate(strip, axis=1)
                p = softmax_rows(scores + strip + limit[:, :seen])
                probs[2 * i + side, rows, pl.ds(0, seen)] = p
                got = nn(p, values[:seen])
                result = got if side == 0 else jnp.where(both[0], result, got)
            mixed[rows, at(i * TILE, TILE)] = result.astype(bf16)
        pltpu.make_async_copy(probs.at[pl.ds(2 * i, 2)], probs_out.at[pl.ds(2 * i, 2)], out_sems.at[i]).start()

    loop(count, pair)
    for i in range(count):
        pltpu.make_async_copy(probs.at[pl.ds(2 * i, 2)], probs_out.at[pl.ds(2 * i, 2)], out_sems.at[i]).wait()


def self_enter_body(x, *refs):
    pieces, (gains, normed, qkv_a, qkv_b, weights, sems) = refs[:6], refs[6:]
    copies = copy_pieces(pieces, weights, sems)
    xs = x[...].astype(f32)
    scaled = xs * inverse_rms(xs)
    wait(copies)
    gain_rows = jnp.transpose(weights[:, :TILE].astype(f32))
    gains[...] = gain_rows[:8]
    normed[...] = (scaled * gain_rows[0:1]).astype(bf16)
    start = TILE
    for out in (qkv_a, qkv_b):
        third = out.shape[1] // 3
        for i in range(3):
            out[:, pl.ds(i * third, third)] = nn(normed[...], weights[:, pl.ds(start, third)]).astype(bf16)
            start += third


def cross_pairs(first, count, enc_len, queries, kv, mixed, probs, probs_out, out_sems):
    blocks, inner = queries.shape[0] // TILE, queries.shape[1]
    places = lax.broadcasted_iota(jnp.int32, (1, kv.shape[0]), 1)
    limit = jnp.where(places < enc_len[0], 0.0, masked_score)

    def pair(i):
        lanes = at((first + i) * TILE, TILE)
        keys = kv[:, lanes]
        values = kv[:, at(inner + (first + i) * TILE, TILE)]
        both = halves((TILE, TILE))
        for block in range(blocks):
            rows = pl.ds(block * TILE, TILE)
            here = queries[rows, lanes]
            result = None
            for side in range(2):
                mine = jnp.where(both[side], here, jnp.zeros_like(here))
                p = softmax_rows(nt(mine, keys) + limit)
                probs[2 * i + side, rows, :] = p
                got = nn(p, values)
                result = got if side == 0 else jnp.where(both[0], result, got)
            mixed[rows, at(i * TILE, TILE)] = result.astype(bf16)
        pltpu.make_async_copy(probs.at[pl.ds(2 * i, 2)], probs_out.at[pl.ds(2 * i, 2)], out_sems.at[i]).start()

    loop(count, pair)
    for i in range(count):
        pltpu.make_async_copy(probs.at[pl.ds(2 * i, 2)], probs_out.at[pl.ds(2 * i, 2)], out_sems.at[i]).wait()


def cross_one_body(count, enc_len, x, mixed_a, mixed_b, enc, gains, *refs):
    pieces, (hidden, normed, queries, kv, mixed, probs_out, weights, probs, sems, out_sems) = refs[:6], refs[6:]
    copies = copy_pieces(pieces, weights, sems)
    inner = queries.shape[1]
    part = mixed_a.shape[1]
    wait(copies)

    def enter(i):
        rows = wide(i)
        got = nt(mixed_a[...], weights[rows, pl.ds(0, part)]) + nt(mixed_b[...], weights[rows, pl.ds(part, inner - part)])
        hidden[:, rows] = x[:, rows].astype(f32) + got

    loop(hidden.shape[1] // WIDE, enter)
    v = hidden[...]
    normed[...] = (v * inverse_rms(v) * gains[1:2]).astype(bf16)

    def project_q(i):
        queries[:, wide(i)] = nn(normed[...], weights[:, wide(i, inner)]).astype(bf16)

    def project_kv(i):
        kv[:, wide(i)] = nn(enc[...], weights[:, wide(i, 2 * inner)]).astype(bf16)

    loop(inner // WIDE, project_q)
    loop(2 * inner // WIDE, project_kv)
    cross_pairs(0, count, enc_len, queries, kv, mixed, probs, probs_out, out_sems)


def cross_two_body(first, count, enc_len, hidden, queries, kv, mixed_a, *refs):
    pieces, (hidden_out, mixed, probs_out, weights, probs, sems, out_sems) = refs[:6], refs[6:]
    inner = queries.shape[1]
    part = mixed_a.shape[1]
    copies = copy_pieces(pieces, weights, sems, 4 * inner)
    cross_pairs(first, count, enc_len, queries, kv, mixed, probs, probs_out, out_sems)
    wait(copies)

    def leave(i):
        rows = wide(i)
        got = nt(mixed_a[...], weights[rows, pl.ds(0, part)]) + nt(mixed[...], weights[rows, pl.ds(part, inner - part)])
        hidden_out[:, rows] = hidden[:, rows] + got

    loop(hidden.shape[1] // WIDE, leave)


root_two_over_pi = math.sqrt(2.0 / math.pi)


def ffn_one_body(hidden, cot, gains, *refs):
    pieces, (normed, gated, slope, act, low, high, weights, sems) = refs[:6], refs[6:]
    copies = copy_pieces(pieces, weights, sems)
    ff = gated.shape[1]
    v = hidden[...]
    normed[...] = (v * inverse_rms(v) * gains[2:3]).astype(bf16)
    turned = jnp.transpose(cot[...])
    wait(copies)

    def unit(i):
        cols = wide(i)
        gate = nn(normed[...], weights[:, cols])
        up = nn(normed[...], weights[:, wide(i, ff)])
        square = gate * gate
        bend = jnp.tanh(root_two_over_pi * gate * (1.0 + 0.044715 * square))
        half = 0.5 * (1.0 + bend)
        gelu = gate * half
        steep = half + 0.5 * gate * (1.0 - bend * bend) * (root_two_over_pi * (1.0 + 3 * 0.044715 * square))
        units = (gelu * up).astype(bf16)
        gated[:, cols] = units
        slope[:, cols] = (up * steep).astype(bf16)
        act[:, cols] = gelu.astype(bf16)
        part = nn(turned, units)
        low[:, cols] = part[:HALF].astype(bf16)
        high[:, cols] = part[HALF:].astype(bf16)

    loop(ff // WIDE, unit)


def ffn_two_body(cot, normed, slope, act, *refs):
    pieces, (low, high, d_gu, weights, sems) = refs[:6], refs[6:]
    copies = copy_pieces(pieces, weights, sems)
    ff = slope.shape[1]
    turned = jnp.transpose(normed[...])
    wait(copies)

    def unit(i):
        cols, other = wide(i), wide(i, ff)
        d_gated = nn(cot[...], weights[:, cols])
        d_gate = (d_gated * slope[:, cols].astype(f32)).astype(bf16)
        d_up = (d_gated * act[:, cols].astype(f32)).astype(bf16)
        d_gu[:, cols] = d_gate
        d_gu[:, other] = d_up
        part = nn(turned, d_gate)
        low[:, cols] = part[:HALF].astype(bf16)
        high[:, cols] = part[HALF:].astype(bf16)
        part = nn(turned, d_up)
        low[:, other] = part[:HALF].astype(bf16)
        high[:, other] = part[HALF:].astype(bf16)

    loop(ff // WIDE, unit)


def ffn_three_body(hidden, cot, gains, d_gu, *refs):
    pieces, (d_hidden, d_low, d_gain, weights, sems) = refs[:6], refs[6:]
    copies = copy_pieces(pieces, weights, sems)
    wait(copies)

    def back(i):
        d_hidden[:, wide(i)] = nt(d_gu[...], weights[wide(i), :])

    loop(hidden.shape[1] // WIDE, back)
    v = hidden[...]
    d_v, d_g = norm_back(v, gains[2:3], d_hidden[...], inverse_rms(v))
    d_v = d_v + cot[...].astype(f32)
    d_hidden[...] = d_v
    d_low[...] = d_v.astype(bf16)
    d_gain[...] = d_g


def output_body(hidden, gated, perm, *refs):
    pieces, (out, weights, held, sems) = refs[:6], refs[6:]
    copies = copy_pieces(pieces, weights, sems)
    wait(copies)

    def leave(i):
        held[:, wide(i)] = (hidden[:, wide(i)] + nt(gated[...], weights[wide(i), :])).astype(bf16)

    def place(i):
        out[:, wide(i)] = nt(held[...], perm[wide(i), :]).astype(bf16)

    loop(hidden.shape[1] // WIDE, leave)
    loop(hidden.shape[1] // WIDE, place)


def enc_body(d_kv_a, d_kv_b, perm, *refs):
    pieces, (out, weights, held, sems) = refs[:6], refs[6:]
    inner = held.shape[1]
    copies = copy_pieces(pieces, weights, sems, 2 * inner)
    part = d_kv_a.shape[1] // 2
    rest = inner - part
    wait(copies)

    def leave(i):
        rows = wide(i)
        got = nt(d_kv_a[:, pl.ds(0, part)], weights[rows, pl.ds(0, part)])
        got = got + nt(d_kv_b[:, pl.ds(0, rest)], weights[rows, pl.ds(part, rest)])
        got = got + nt(d_kv_a[:, pl.ds(part, part)], weights[rows, pl.ds(inner, part)])
        got = got + nt(d_kv_b[:, pl.ds(rest, rest)], weights[rows, pl.ds(inner + part, rest)])
        held[:, rows] = got.astype(bf16)

    def place(i):
        out[:, wide(i)] = nt(held[...], perm[wide(i), :]).astype(bf16)

    loop(out.shape[1] // WIDE, leave)
    loop(out.shape[1] // WIDE, place)


def attention_back(side, rows, seen, p, d_mixed, mixed, keys, values, d_scores):
    lanes = halves((TILE, TILE))[side]
    d_out = jnp.where(lanes, d_mixed, jnp.zeros_like(d_mixed))
    delta = jnp.sum(d_out.astype(f32) * mixed.astype(f32), axis=-1, keepdims=True)
    d_s = (p.astype(f32) * (nt(d_out, values) - delta)).astype(bf16)
    d_scores[side, rows, pl.ds(0, seen)] = d_s
    return d_s, nn(d_s, keys)


def fetch_probs(probs_in, probs, in_sems):
    copies = []
    for i in range(probs.shape[0] // 2):
        copies.append(pltpu.make_async_copy(probs_in.at[pl.ds(2 * i, 2)], probs.at[pl.ds(2 * i, 2)], in_sems.at[i]))
        copies[-1].start()


def cross_back_pairs(first, count, queries, kv, mixed, d_mixed, probs_in, probs, in_sems, d_q, d_kv, d_scores):
    blocks, inner = queries.shape[0] // TILE, queries.shape[1]

    def pair(i):
        pltpu.make_async_copy(probs_in.at[pl.ds(2 * i, 2)], probs.at[pl.ds(2 * i, 2)], in_sems.at[i]).wait()
        lanes, mine = at((first + i) * TILE, TILE), at(i * TILE, TILE)
        keys, values = kv[:, lanes], kv[:, at(inner + (first + i) * TILE, TILE)]
        d_mix, here = d_mixed[:, lanes], queries[:, lanes]
        both, zero = halves(keys.shape), jnp.zeros_like(keys)
        d_k = d_v = None
        for side in range(2):
            my_keys = jnp.where(both[side], keys, zero)
            for block in range(blocks):
                rows = pl.ds(block * TILE, TILE)
                span = slice(block * TILE, (block + 1) * TILE)
                p = probs[2 * i + side, rows, :]
                _, part = attention_back(side, rows, kv.shape[0], p, d_mix[span], mixed[rows, mine], my_keys, values, d_scores)
                if side == 0:
                    d_q[rows, mine] = part.astype(bf16)
                else:
                    d_q[rows, mine] = (d_q[rows, mine].astype(f32) + part).astype(bf16)
            part_v = tn(probs[2 * i + side], jnp.where(both[side], d_mix, zero))
            part_k = tn(d_scores[side], jnp.where(both[side], here, zero))
            d_v = part_v if side == 0 else d_v + part_v
            d_k = part_k if side == 0 else d_k + part_k
        d_kv[:, mine] = d_k.astype(bf16)
        d_kv[:, at((count + i) * TILE, TILE)] = d_v.astype(bf16)

    loop(count, pair)


def cross_back_one_body(count, d_low, queries, kv, mixed, *refs):
    pieces, probs_in, (d_mixed, d_q, d_kv, weights, probs, d_scores, sems, in_sems) = refs[:6], refs[6], refs[7:]
    inner = queries.shape[1]
    copies = copy_pieces(pieces, weights, sems, 4 * inner)
    fetch_probs(probs_in, probs, in_sems)
    wait(copies)

    def enter(i):
        d_mixed[:, wide(i)] = nn(d_low[...], weights[:, wide(i)]).astype(bf16)

    loop(inner // WIDE, enter)
    cross_back_pairs(0, count, queries, kv, mixed, d_mixed, probs_in, probs, in_sems, d_q, d_kv, d_scores)


def put(low, high, cols, part):
    low[:, cols] = part[:HALF].astype(bf16)
    high[:, cols] = part[HALF:].astype(bf16)


def cross_back_two_body(first, count, *refs):
    hidden, d_hidden, gains, queries, kv, mixed, d_mixed, d_q_a = refs[:8]
    pieces, probs_in = refs[8:14], refs[14]
    d_q, d_kv, d_out, d_out_low, d_gain, weights, probs, d_scores, sems, in_sems = refs[15:]
    inner = queries.shape[1]
    part = d_q_a.shape[1]
    rest = inner - part
    copies = copy_pieces(pieces, weights, sems, inner)
    fetch_probs(probs_in, probs, in_sems)
    cross_back_pairs(first, count, queries, kv, mixed, d_mixed, probs_in, probs, in_sems, d_q, d_kv, d_scores)
    wait(copies)

    def back(i):
        got = nt(d_q_a[...], weights[wide(i), pl.ds(0, part)]) + nt(d_q[...], weights[wide(i), pl.ds(part, rest)])
        d_out[:, wide(i)] = got

    loop(hidden.shape[1] // WIDE, back)
    v = hidden[...]
    d_v, d_g = norm_back(v, gains[1:2], d_out[...], inverse_rms(v))
    d_v = d_v + d_hidden[...]
    d_out[...] = d_v
    d_out_low[...] = d_v.astype(bf16)
    d_gain[...] = d_g


def cross_grads_body(d_one, one_a, one_b, normed, d_q_a, d_q_b, enc, d_kv_a, d_kv_b, d_two, two_a, two_b, low, high):
    part, rest = one_a.shape[1], one_b.shape[1]
    k_a, v_a = d_kv_a.at[:, pl.ds(0, part)], d_kv_a.at[:, pl.ds(part, part)]
    k_b, v_b = d_kv_b.at[:, pl.ds(0, rest)], d_kv_b.at[:, pl.ds(rest, rest)]
    start = 0
    for left, rights in (
        (d_one, (one_a, one_b)),
        (normed, (d_q_a, d_q_b)),
        (enc, (k_a, k_b, v_a, v_b)),
        (d_two, (two_a, two_b)),
    ):
        turned = jnp.transpose(left[...])
        for right in rights:
            put(low, high, pl.ds(start, right.shape[1]), nn(turned, right[...]))
            start += right.shape[1]


def self_back_pairs(first, count, qkv, mixed, d_mixed, probs_in, probs, in_sems, d_qkv, d_scores, work, sums, counted):
    tokens, inner = qkv.shape[0], qkv.shape[1] // 3
    blocks = tokens // TILE

    def pair(i):
        pltpu.make_async_copy(probs_in.at[pl.ds(2 * i, 2)], probs.at[pl.ds(2 * i, 2)], in_sems.at[i]).wait()
        lanes, mine = at((first + i) * TILE, TILE), at(i * TILE, TILE)
        here, keys = qkv[:, mine], qkv[:, at(inner + i * TILE, TILE)]
        values = qkv[:, at(2 * inner + i * TILE, TILE)]
        d_mix = d_mixed[:, lanes]
        both, zero = halves(keys.shape), jnp.zeros_like(keys)
        for side in range(2):
            head = 2 * i + side
            my_keys = jnp.where(both[side], keys, zero)
            diagonal = [None] * blocks
            for block in range(blocks):
                rows = pl.ds(block * TILE, TILE)
                span = slice(block * TILE, (block + 1) * TILE)
                seen = (block + 1) * TILE
                p = probs[head, rows, pl.ds(0, seen)]
                d_s, part = attention_back(
                    side, rows, seen, p, d_mix[span], mixed[rows, mine], my_keys[:seen], values[:seen], d_scores
                )
                wider = d_s.astype(f32)
                for j in range(block + 1):
                    tile = wider[:, j * TILE : (j + 1) * TILE]
                    apart = block - j
                    diagonal[apart] = tile if diagonal[apart] is None else diagonal[apart] + tile
                if side == 0:
                    d_qkv[rows, mine] = part.astype(bf16)
                else:
                    d_qkv[rows, mine] = (d_qkv[rows, mine].astype(f32) + part).astype(bf16)
            for apart in range(blocks):
                tile = jnp.concatenate([diagonal[apart], jnp.zeros((TILE, TILE), f32)], axis=1)
                folded = tile[:8]
                for group in range(1, TILE // 8):
                    folded = folded + pltpu.roll(tile[group * 8 : group * 8 + 8], 2 * TILE - 8 * group, 1)
                for s in range(8):
                    sums[s, pl.ds(apart * 8 + head, 1), :] = folded[s : s + 1]
            d_o = jnp.where(both[side], d_mix, zero)
            q_o = jnp.where(both[side], here, zero)
            for j in range(blocks):
                start = j * TILE
                rows, out_rows = pl.ds(start, tokens - start), pl.ds(start, TILE)
                part_v = tn(probs[head, rows, pl.ds(start, TILE)], d_o[start:])
                part_k = tn(d_scores[side, rows, pl.ds(start, TILE)], q_o[start:])
                if side == 0:
                    work[0, out_rows, :] = part_v
                    work[1, out_rows, :] = part_k
                else:
                    d_qkv[out_rows, at((count + i) * TILE, TILE)] = (work[1, out_rows, :] + part_k).astype(bf16)
                    d_qkv[out_rows, at((2 * count + i) * TILE, TILE)] = (work[0, out_rows, :] + part_v).astype(bf16)

    loop(count, pair)
    lines = sums[0]
    for s in range(1, 8):
        lines = lines + pltpu.roll(sums[s], 2 * TILE - s, 1)
    table = None
    for apart in range(blocks):
        here = lax.dot_general(
            lines[apart * 8 : apart * 8 + 8],
            counted[apart],
            (((1,), (0,)), ((), ())),
            precision=lax.Precision.HIGHEST,
            preferred_element_type=f32,
        )
        table = here if table is None else table + here
    return table


def self_back_one_body(count, d_low, normed, qkv, mixed, counted, *refs):
    pieces, probs_in = refs[:6], refs[6]
    low, high, d_mixed, d_qkv, table, weights, probs, d_scores, work, sums, sems, in_sems = refs[7:]
    copies = copy_pieces(pieces, weights, sems)
    fetch_probs(probs_in, probs, in_sems)
    turned = jnp.transpose(normed[...])
    wait(copies)

    def enter(i):
        d_mixed[:, wide(i)] = nn(d_low[...], weights[:, wide(i)]).astype(bf16)

    loop(d_mixed.shape[1] // WIDE, enter)
    sums[...] = jnp.zeros_like(sums)
    table[...] = self_back_pairs(
        0, count, qkv, mixed, d_mixed, probs_in, probs, in_sems, d_qkv, d_scores, work, sums, counted
    )
    part = count * TILE

    def grads(i):
        cols = pl.ds(i * part, part)
        put(low, high, cols, nn(turned, d_qkv[:, cols]))

    loop(3, grads)


def self_back_two_body(first, count, *refs):
    x, d_hidden, gains, normed, qkv, mixed, gain_c, gain_f, d_mixed, d_qkv_a, counted, table_a, spread = refs[:13]
    pieces, probs_in = refs[13:19], refs[19]
    low, high, d_x, table, weights, probs, d_qkv, d_scores, work, sums, total, sems, in_sems = refs[20:]
    copies = copy_pieces(pieces, weights, sems, TILE)
    fetch_probs(probs_in, probs, in_sems)
    turned = jnp.transpose(normed[...])
    sums[...] = jnp.zeros_like(sums)
    table[pl.ds(0, 8), :] = table_a[...]
    table[pl.ds(8, 8), :] = self_back_pairs(
        first, count, qkv, mixed, d_mixed, probs_in, probs, in_sems, d_qkv, d_scores, work, sums, counted
    )
    wait(copies)
    rest = count * TILE
    start = d_qkv_a.shape[1]
    head = low.shape[1] - 3 * rest

    def back(i):
        got = nt(d_qkv_a[...], weights[wide(i), pl.ds(0, start)])
        total[:, wide(i)] = got + nt(d_qkv[...], weights[wide(i), pl.ds(start, 3 * rest)])

    loop(x.shape[1] // WIDE, back)
    v = x[...].astype(f32)
    d_v, d_g = norm_back(v, gains[0:1], total[...], inverse_rms(v))
    d_x[...] = (d_v + d_hidden[...]).astype(bf16)
    rows = jnp.concatenate([d_g, gain_c[...], gain_f[...], jnp.zeros((TILE - 3, d_g.shape[1]), f32)], axis=0)
    found = table[...].astype(bf16)
    per_row = spread.shape[0]
    parts = []
    for j in range(per_row):
        left, right = jnp.zeros((16, j * NB), bf16), jnp.zeros((16, head - (j + 1) * NB), bf16)
        wider = ([left] if j else []) + [found] + ([right] if right.shape[1] else [])
        parts.append(nn(spread[j], jnp.concatenate(wider, axis=1)))
    side = jnp.transpose(rows)
    if head == TILE:
        lane = lax.broadcasted_iota(jnp.int32, side.shape, 1)
        side = jnp.where(lane < HD, sum(parts), pltpu.roll(side, HD, 1))
    else:
        side = jnp.concatenate([sum(parts), side], axis=1)[:, :head]
    put(low, high, pl.ds(0, head), side)

    def grads(i):
        cols = pl.ds(i * rest, rest)
        put(low, high, pl.ds(head + i * rest, rest), nn(turned, d_qkv[:, cols]))

    loop(3, grads)


def place_body(value, perm, out):
    def place(i):
        out[:, wide(i)] = nt(value[...], perm[wide(i), :]).astype(bf16)

    loop(out.shape[1] // WIDE, place)


def stack_body(one, two, three, out, sems):
    copies, row = [], 0
    for i, value in enumerate((one, two, three)):
        copies.append(pltpu.make_async_copy(value, out.at[pl.ds(row, value.shape[0]), :], sems.at[i]))
        copies[-1].start()
        row += value.shape[0]
    wait(copies)


def stack(*values):
    rows, cols = sum(v.shape[0] for v in values), values[0].shape[1]
    out = [(shape((rows, cols), bf16), FAR)]
    return call(stack_body, "stack", [FAR] * 3, out, [pltpu.SemaphoreType.DMA((3,))], 1.0, *values, spare=2)[0]


def pack_body(part, *refs):
    gain_s, gain_c, gain_f, sq, sk, sv, so, cq, ck, cv, co, fg, fu, fo, early, second, third, fourth, sems = refs
    inner = sq.shape[1]
    rest = inner - part
    moves = [(v.at[:, pl.ds(0, part)], early, TILE + i * part) for i, v in enumerate((sq, sk, sv))]
    moves += [(v.at[:, pl.ds(part, rest)], early, TILE + 3 * part + i * rest) for i, v in enumerate((sq, sk, sv))]
    moves += [(v, second, i * inner) for i, v in enumerate((so, cq, ck, cv, co))]
    moves += [(fg, third, 0), (fu, third, fg.shape[1]), (fo, fourth, 0)]
    copies = []
    for i, (source, out, start) in enumerate(moves):
        copies.append(pltpu.make_async_copy(source, out.at[:, pl.ds(start, source.shape[1])], sems.at[i]))
        copies[-1].start()
    count = gain_s.shape[1]
    rows = jnp.concatenate([gain_s[...], gain_c[...], gain_f[...], jnp.zeros((TILE - 3, count), bf16)], axis=0).astype(f32)
    rows = jnp.concatenate([rows, jnp.zeros((TILE, TILE - count), f32)], axis=1)
    early[:, pl.ds(0, TILE)] = jnp.transpose(rows)[:count].astype(bf16)
    wait(copies)


def core_add_body(split, *refs):
    outs = refs[-5:]

    def add(low, got):
        size = HALF // 4
        total = (low[...].astype(f32) + got[...].astype(f32)).astype(bf16)
        starts = (0, size, 2 * size, 3 * size, 3 * size + size // 2)
        for out, start in zip(outs, starts):
            out[...] = total[start : start + out.shape[0]]

    if split is None:
        add(*refs[:2])
    else:
        step = pl.program_id(0)
        pl.when(step < split)(lambda: add(*refs[:2]))
        pl.when(step >= split)(lambda: add(*refs[2:4]))


def core_add(*pairs):
    rows = pairs[0].shape[0]
    cols = [pairs[i].shape[1] for i in range(0, len(pairs), 2)]
    size = rows // 4
    block = max(n * TILE for n in range(1, 7) if all(c % (n * TILE) == 0 for c in cols))
    split = None if len(cols) == 1 else cols[0] // block
    sizes = (size, size, size, size // 2, size // 2)
    first = pl.BlockSpec((rows, block), lambda i: (0, i if split is None else jnp.minimum(i, split - 1)))
    second = pl.BlockSpec((rows, block), lambda i: (0, jnp.maximum(i - split, 0)))
    total = sum(cols)
    return pl.pallas_call(
        lambda *refs: core_add_body(split, *refs),
        grid=(total // block,),
        out_shape=[shape((s, total), bf16) for s in sizes],
        in_specs=[first, first] if split is None else [first, first, second, second],
        out_specs=[pl.BlockSpec((s, block), lambda i: (0, i)) for s in sizes],
        compiler_params=pltpu.CompilerParams(vmem_limit_bytes=16 * 2**20),
        cost_estimate=pl.CostEstimate(flops=0, bytes_accessed=1024, transcendentals=0),
        name="core_add",
    )(*pairs)


def plane_add_body(to_x, got_x, to_y, got_y, out_x, out_y):
    half = got_x.shape[0]
    out_x[pl.ds(0, half), :] = to_x[pl.ds(0, half), :]
    out_x[pl.ds(half, half), :] = (to_x[pl.ds(half, half), :].astype(f32) + got_x[...].astype(f32)).astype(bf16)
    out_y[pl.ds(0, half), :] = (to_y[pl.ds(0, half), :].astype(f32) + got_y[...].astype(f32)).astype(bf16)
    out_y[pl.ds(half, half), :] = to_y[pl.ds(half, half), :]


def plane_add(to_x, got_x, to_y, got_y):
    return call(
        plane_add_body, "plane_add", [VMEM] * 4, [(shape(to_x.shape, bf16), VMEM)] * 2, [], 2.0, to_x, got_x, to_y, got_y
    )


def own_add_body(own, got_x, got_y, keep, away):
    half = keep.shape[0]
    total = own[...].astype(f32) + got_x[...].astype(f32) + got_y[...].astype(f32)
    keep[...] = total[:half].astype(bf16)
    away[...] = total[half:].astype(bf16)


def own_add(own, got_x, got_y):
    half = shape((own.shape[0] // 2, own.shape[1]), bf16)
    return call(own_add_body, "own_add", [VMEM] * 3, [(half, VMEM)] * 2, [], 2.0, own, got_x, got_y)


def line_add_body(own, got, keep, away):
    half = keep.shape[0]
    total = own[...].astype(f32) + got[...].astype(f32)
    keep[...] = total[:half].astype(bf16)
    away[...] = total[half:].astype(bf16)


def line_add(own, got):
    half = shape((own.shape[0] // 2, own.shape[1]), bf16)
    return call(line_add_body, "line_add", [VMEM] * 2, [(half, VMEM)] * 2, [], 1.5, own, got)


def last_add_body(own, got, *outs):
    start = 0
    for out in outs:
        cols = pl.ds(start, out.shape[1])
        out[...] = own[:, cols].astype(f32) + got[:, cols].astype(f32)
        start += out.shape[1]


def last_add(own, got, widths):
    outs = [(shape((own.shape[0], w), f32), VMEM) for w in widths]
    return call(last_add_body, "last_add", [VMEM] * 2, outs, [], 1.5, own, got)


def bucket_of(distance):
    bucket = np.where(distance < 16, distance, 16)
    for edge in bucket_edges:
        bucket = bucket + (distance >= edge)
    return np.maximum(bucket, 0)


def split_last_body(own_a, got_a, own_b, got_b, side, *outs):
    head = side.shape[1]
    rest = (own_b.shape[1] - head) // 3
    part = outs[0].shape[1] - rest
    side[...] = own_b[:, pl.ds(0, head)].astype(f32) + got_b[:, pl.ds(0, head)].astype(f32)
    for i, out in enumerate(outs[:3]):
        cols = pl.ds(own_a.shape[1] - (3 - i) * part, part)
        out[:, pl.ds(0, part)] = own_a[:, cols].astype(f32) + got_a[:, cols].astype(f32)
        cols = pl.ds(head + i * rest, rest)
        out[:, pl.ds(part, rest)] = own_b[:, cols].astype(f32) + got_b[:, cols].astype(f32)
    for i, out in enumerate(outs[3:]):
        cols = pl.ds(i * out.shape[1], out.shape[1])
        out[...] = own_a[:, cols].astype(f32) + got_a[:, cols].astype(f32)


def layer(
    cube,
    states,
    encoded,
    cotangent,
    dec_lens,
    enc_lens,
    self_query,
    self_key,
    self_value,
    self_out,
    cross_query,
    cross_key,
    cross_value,
    cross_out,
    ffn_gate,
    ffn_up,
    ffn_out,
    gain_self,
    gain_cross,
    gain_ffn,
    table,
):
    _, tokens, width = states.shape
    enc_tokens = encoded.shape[1]
    inner, ff = self_query.shape[1], ffn_gate.shape[1]
    own_rows = self_query.shape[0]
    blocks = tokens // TILE
    pairs = inner // TILE
    early = pairs // 2
    late = pairs - early
    part, rest = early * TILE, late * TILE
    sems = pltpu.SemaphoreType.DMA
    fence = Order(dec_lens)

    def weight_mem(cols):
        return pltpu.VMEM((width, cols), bf16)

    def mem(*dims):
        return pltpu.VMEM(dims, bf16)

    widths = (TILE + 3 * inner, 5 * inner, 2 * ff, ff)
    packed = call(
        lambda *refs: pack_body(part, *refs),
        "pack",
        [VMEM] * 3 + [FAR] * 11,
        [(shape((own_rows, w), bf16), VMEM) for w in widths],
        [sems((14,))],
        2.0,
        *(gain_self.reshape(1, -1), gain_cross.reshape(1, -1), gain_ffn.reshape(1, -1)),
        *(self_query, self_key, self_value, self_out, cross_query, cross_key, cross_value, cross_out, ffn_gate, ffn_up, ffn_out),
        spare=60,
    )
    A, B, C, D = (Gather(cube, p) for p in packed)
    lines_of = cube.rest
    for step in lines_of[:-1]:
        A.line(step)
    perm = cube.permutation(width)

    lane = np.arange(2 * TILE)
    signed = np.where(lane < TILE, lane, lane - 2 * TILE)
    distance = np.arange(blocks)[:, None] * TILE - signed[None, :]
    chosen = (np.arange(NB)[:, None] == bucket_of(distance).reshape(1, -1)).astype(np.float32)
    lines = lax.dot_general(table, jnp.asarray(chosen, bf16), (((0,), (0,)), ((), ())), preferred_element_type=f32)
    lines = jnp.where(jnp.asarray(distance.reshape(1, -1) >= 0), lines, masked_score)
    lines = lines.reshape(H * blocks, 2 * TILE)
    counted = (bucket_of(distance)[:, :, None] == np.arange(NB)) & (distance >= 0)[:, :, None]
    counted = jnp.asarray(counted.astype(np.float32))

    token_bf = shape((tokens, width), bf16)
    token_f32 = shape((tokens, width), f32)
    row_f32 = shape((1, width), f32)

    (bias,) = call(bias_body, "bias", [VMEM], [(shape((H * blocks, TILE, TILE), f32), VMEM)], [], 5.0, lines)
    bias, perm = fence([bias, perm], A)
    A.line(lines_of[-1])
    x = nn(states[0], perm).astype(bf16)
    enc = nn(encoded[0], perm).astype(bf16)
    cot = nn(cotangent[0], perm).astype(bf16)
    x, enc, cot = fence([x, enc, cot], A, B)
    A.plane()
    for step in lines_of[:-1]:
        B.line(step)
    fence([], A, B)
    A.far()
    B.line(lines_of[-1])
    fence([], A)
    A.across()
    (x,) = fence([x], A, B, C)
    B.plane()
    for step in lines_of[:-1]:
        C.line(step)
    gains, normed_one, qkv_a, qkv_b = call(
        self_enter_body,
        "self_enter",
        [VMEM] + [FAR] * 6,
        [
            (shape((8, width), f32), VMEM),
            (token_bf, VMEM),
            (shape((tokens, 3 * part), bf16), VMEM),
            (shape((tokens, 3 * rest), bf16), VMEM),
        ],
        [weight_mem(widths[0]), sems((10,))],
        6.0,
        *(x, *A.held),
    )
    gains, normed_one, qkv_a, qkv_b = fence([gains, normed_one, qkv_a, qkv_b], D)
    for step in lines_of[:-1]:
        D.line(step)

    def self_heads(first, count, qkv):
        return call(
            lambda *refs: self_pairs(first, count, *refs),
            "self_heads",
            [SMEM, VMEM, VMEM],
            [(shape((tokens, count * TILE), bf16), VMEM), (shape((2 * count, tokens, tokens), bf16), FAR)],
            [mem(2 * count, tokens, tokens), sems((count,))],
            8.0,
            *(dec_lens, bias, qkv),
        )

    mixed_one_a, probs_one_a = self_heads(0, early, qkv_a)
    mixed_one_a, probs_one_a, qkv_b = fence([mixed_one_a, probs_one_a, qkv_b], B, C, D)
    B.far()
    C.line(lines_of[-1])
    D.line(lines_of[-1])
    mixed_one_b, probs_one_b = self_heads(early, late, qkv_b)
    mixed_one_b, probs_one_b = fence([mixed_one_b, probs_one_b], B, C)
    B.across()
    C.plane()
    (mixed_one_b,) = fence([mixed_one_b], B, D)
    D.plane()
    hidden_one, normed_two, q_two, kv_two, mixed_two_a, probs_two_a = call(
        lambda *refs: cross_one_body(early, *refs),
        "cross_one",
        [SMEM] + [VMEM] * 5 + [FAR] * 6,
        [
            (token_f32, VMEM),
            (token_bf, VMEM),
            (shape((tokens, inner), bf16), VMEM),
            (shape((enc_tokens, 2 * inner), bf16), VMEM),
            (shape((tokens, part), bf16), VMEM),
            (shape((2 * early, tokens, enc_tokens), bf16), FAR),
        ],
        [weight_mem(4 * inner), mem(2 * early, tokens, enc_tokens), sems((10,)), sems((early,))],
        13.0,
        *(enc_lens, x, mixed_one_a, mixed_one_b, enc, gains, *B.held),
    )
    hidden_one, normed_two, q_two, kv_two, mixed_two_a, probs_two_a = fence(
        [hidden_one, normed_two, q_two, kv_two, mixed_two_a, probs_two_a], C
    )
    C.far()
    hidden_two, mixed_two_b, probs_two_b = call(
        lambda *refs: cross_two_body(early, late, *refs),
        "cross_two",
        [SMEM] + [VMEM] * 4 + [FAR] * 6,
        [(token_f32, VMEM), (shape((tokens, rest), bf16), VMEM), (shape((2 * late, tokens, enc_tokens), bf16), FAR)],
        [weight_mem(inner), mem(2 * late, tokens, enc_tokens), sems((10,)), sems((late,))],
        10.0,
        *(enc_lens, hidden_one, q_two, kv_two, mixed_two_a, *B.held),
    )
    hidden_two, mixed_two_b, probs_two_b = fence([hidden_two, mixed_two_b, probs_two_b], C, D)
    C.across()
    D.far()
    (hidden_two,) = fence([hidden_two], C)
    units = shape((tokens, ff), bf16)
    near_units = near((tokens, ff), bf16)
    half_ff = shape((HALF, ff), bf16)
    normed_three, gated, slope, act, fo_low, fo_high = call(
        ffn_one_body,
        "ffn_one",
        [VMEM] * 3 + [FAR] * 6,
        [(token_bf, VMEM), (units, VMEM), (near_units, VMEM), (near_units, VMEM)] + [(half_ff, VMEM)] * 2,
        [weight_mem(2 * ff), sems((10,))],
        10.0,
        *(hidden_two, cot, gains, *C.held),
    )
    fo_low, fo_high, normed_three, gated, slope, act = fence([fo_low, fo_high, normed_three, gated, slope, act], D)
    D.across()
    R1 = Reduce(cube, fo_low, fo_high)
    slope, act = fence([slope, act], D)
    half_gu = shape((HALF, 2 * ff), bf16)
    gu_low, gu_high, d_gu = call(
        ffn_two_body,
        "ffn_two",
        [VMEM] * 4 + [FAR] * 6,
        [(half_gu, VMEM), (half_gu, VMEM), (near((tokens, 2 * ff), bf16), VMEM)],
        [weight_mem(ff), sems((10,))],
        10.0,
        *(cot, normed_three, slope, act, *D.held),
    )
    gu_low, gu_high, d_gu = fence([gu_low, gu_high, d_gu], R1)
    R1.more(gu_low, gu_high)
    d_hidden_two, d_low_two, gain_f = call(
        ffn_three_body,
        "ffn_three",
        [VMEM] * 4 + [FAR] * 6,
        [(token_f32, VMEM), (token_bf, VMEM), (row_f32, VMEM)],
        [weight_mem(2 * ff), sems((10,))],
        5.0,
        *(hidden_two, cot, gains, d_gu, *C.held),
    )
    d_hidden_two, d_low_two, gain_f = fence([d_hidden_two, d_low_two, gain_f], R1)
    R1.far()
    d_mixed_two, d_q_a, d_kv_a = call(
        lambda *refs: cross_back_one_body(early, *refs),
        "cross_back_one",
        [VMEM] * 4 + [FAR] * 7,
        [
            (shape((tokens, inner), bf16), VMEM),
            (shape((tokens, part), bf16), VMEM),
            (shape((enc_tokens, 2 * part), bf16), VMEM),
        ],
        [
            weight_mem(inner),
            mem(2 * early, tokens, enc_tokens),
            mem(2, tokens, enc_tokens),
            sems((10,)),
            sems((early,)),
        ],
        8.0,
        *(d_low_two, q_two, kv_two, mixed_two_a, *B.held, probs_two_a),
    )
    d_mixed_two, d_q_a, d_kv_a = fence([d_mixed_two, d_q_a, d_kv_a], R1)
    R1.plane()
    d_q_b, d_kv_b, d_hidden_one, d_low_one, gain_c = call(
        lambda *refs: cross_back_two_body(early, late, *refs),
        "cross_back_two",
        [VMEM] * 8 + [FAR] * 7,
        [
            (shape((tokens, rest), bf16), VMEM),
            (shape((enc_tokens, 2 * rest), bf16), VMEM),
            (token_f32, VMEM),
            (token_bf, VMEM),
            (row_f32, VMEM),
        ],
        [
            weight_mem(inner),
            mem(2 * late, tokens, enc_tokens),
            mem(2, tokens, enc_tokens),
            sems((10,)),
            sems((late,)),
        ],
        8.0,
        *(hidden_one, d_hidden_two, gains, q_two, kv_two, mixed_two_b, d_mixed_two, d_q_a, *B.held, probs_two_b),
    )
    d_q_b, d_kv_b, d_hidden_one, d_low_one, gain_c = fence([d_q_b, d_kv_b, d_hidden_one, d_low_one, gain_c])
    half_cross = shape((HALF, 5 * inner), bf16)
    cross_low, cross_high = call(
        cross_grads_body,
        "cross_grads",
        [VMEM] * 12,
        [(half_cross, VMEM)] * 2,
        [],
        9.0,
        *(d_low_one, mixed_one_a, mixed_one_b, normed_two, d_q_a, d_q_b, enc, d_kv_a, d_kv_b, d_low_two, mixed_two_a, mixed_two_b),
    )
    d_low_one, cross_low, cross_high = fence([d_low_one, cross_low, cross_high])
    half_a = shape((HALF, 3 * part), bf16)
    self_low_a, self_high_a, d_mixed_one, d_qkv_a, table_a = call(
        lambda *refs: self_back_one_body(early, *refs),
        "self_back_one",
        [VMEM] * 5 + [FAR] * 7,
        [
            (half_a, VMEM),
            (half_a, VMEM),
            (shape((tokens, inner), bf16), VMEM),
            (shape((tokens, 3 * part), bf16), VMEM),
            (shape((8, NB), f32), VMEM),
        ],
        [
            weight_mem(inner),
            mem(2 * early, tokens, tokens),
            mem(2, tokens, tokens),
            pltpu.VMEM((2, tokens, TILE), f32),
            pltpu.VMEM((8, 8 * blocks, 2 * TILE), f32),
            sems((10,)),
            sems((early,)),
        ],
        9.0,
        *(d_low_one, normed_one, qkv_a, mixed_one_a, counted, *B.held, probs_one_a),
    )
    self_low_a, self_high_a, d_qkv_a, d_mixed_one, table_a, cross_low, cross_high, d_kv_b = fence(
        [self_low_a, self_high_a, d_qkv_a, d_mixed_one, table_a, cross_low, cross_high, d_kv_b], R1
    )
    R1.line()
    R3 = Reduce(cube, cross_low, cross_high)
    R3.more(self_low_a, self_high_a)
    (grad_enc,) = call(
        enc_body,
        "grad_encoded",
        [VMEM] * 3 + [FAR] * 6,
        [(shape((enc_tokens, width), bf16), VMEM)],
        [weight_mem(2 * inner), mem(enc_tokens, width), sems((10,))],
        5.0,
        *(d_kv_a, d_kv_b, perm, *B.held),
    )
    d_qkv_a, grad_enc = fence([d_qkv_a, grad_enc], R3)
    R3.far()
    per_row = -(-H // own_rows)
    head_cols = TILE if per_row * NB <= HD else per_row * NB + TILE
    placed = np.zeros((per_row, width, 16), np.float32)
    for h in range(H):
        slot = h if h < 2 * early else 8 + h - 2 * early
        placed[h % per_row, h // per_row :: own_rows, slot] = 1.0
    half_b = shape((HALF, head_cols + 3 * rest), bf16)
    self_low_b, self_high_b, d_x, table_sum = call(
        lambda *refs: self_back_two_body(early, late, *refs),
        "self_back_two",
        [VMEM] * 13 + [FAR] * 7,
        [(half_b, VMEM), (half_b, VMEM), (token_bf, VMEM), (shape((16, NB), f32), VMEM)],
        [
            weight_mem(3 * inner),
            mem(2 * late, tokens, tokens),
            mem(tokens, 3 * rest),
            mem(2, tokens, tokens),
            pltpu.VMEM((2, tokens, TILE), f32),
            pltpu.VMEM((8, 8 * blocks, 2 * TILE), f32),
            pltpu.VMEM((tokens, width), f32),
            sems((10,)),
            sems((late,)),
        ],
        12.0,
        *(x, d_hidden_one, gains, normed_one, qkv_b, mixed_one_b, gain_c, gain_f, d_mixed_one, d_qkv_a, counted, table_a),
        jnp.asarray(placed, bf16),
        *(*A.held, probs_one_b),
    )
    self_low_b, self_high_b, d_x = fence([self_low_b, self_high_b, d_x], R3, R1)
    R5 = Reduce(cube, self_low_b, self_high_b)
    R3.plane()
    R1.rest()
    (grad_states,) = call(place_body, "grad_states", [VMEM] * 2, [(token_bf, VMEM)], [], 2.0, d_x, perm)
    gated, grad_states = fence([gated, grad_states], R5)
    R5.far()
    (output,) = call(
        output_body,
        "output",
        [VMEM] * 3 + [FAR] * 6,
        [(token_bf, VMEM)],
        [weight_mem(ff), mem(tokens, width), sems((10,))],
        6.0,
        *(hidden_two, gated, perm, *D.held),
    )
    (output,) = fence([output], R3)
    R3.line()
    fence([], R5, R1)
    R5.plane()
    g_fo, g_fg, g_fu = R1.last((ff, ff, ff))
    (g_fo,) = fence([g_fo], R5)
    R5.line()
    fence([], R3)
    R3.rest()
    fence([], R5)
    R5.rest()
    fence([], R3, R5)
    sizes = (head_cols,) + (inner,) * 8
    side, g_sq, g_sk, g_sv, g_so, g_cq, g_ck, g_cv, g_co = call(
        split_last_body,
        "last_self",
        [VMEM] * 4,
        [(shape((own_rows, w), f32), VMEM) for w in sizes],
        [],
        1.5,
        *(*R3.held, *R5.held),
    )
    heads = [side[h // per_row, (h % per_row) * NB : (h % per_row + 1) * NB] for h in range(H)]
    if per_row == 1:
        grad_table = side[:H, :NB].T
    else:
        grad_table = jnp.stack(heads, axis=1)
    first_gain = HD if head_cols == TILE else per_row * NB
    g_gains = side[:, first_gain : first_gain + 3]
    return (
        output[None],
        grad_states[None],
        grad_enc[None],
        g_sq,
        g_sk,
        g_sv,
        g_so,
        g_cq,
        g_ck,
        g_cv,
        g_co,
        g_fg,
        g_fu,
        g_fo,
        g_gains[:, 0],
        g_gains[:, 1],
        g_gains[:, 2],
        grad_table,
    )


def solution(mesh):
    cube = Cube(mesh)
    both = ("gx", "gy")
    row, flat, one = P(both, None, None), P(both, None), P(both)
    in_specs = (row, row, row, one, one) + (flat,) * 11 + (one,) * 3 + (P(),)
    out_specs = (row, row, row) + (flat,) * 11 + (one,) * 3 + (P(),)

    def per_device(*args):
        return layer(cube, *args)

    return jax.shard_map(per_device, mesh=mesh, in_specs=in_specs, out_specs=out_specs, check_vma=False)
```

```python
import math

import jax
import jax.numpy as jnp
import numpy as np
from jax import lax
from jax.experimental import pallas as pl
from jax.experimental.pallas import tpu as pltpu
from jax.sharding import PartitionSpec as P

H = 12
HD = 64
NB = 32

norm_eps = 1e-06
masked_score = -1000000000.0
bucket_edges = [int(math.ceil(16 * 8 ** (power / 16.0))) for power in range(1, 16)]

bf16 = jnp.bfloat16
f32 = jnp.float32


class Cube:
    def __init__(self, mesh):
        self.nx, self.ny = mesh.shape["gx"], mesh.shape["gy"]
        self.n = self.nx * self.ny
        self.core, self.y, self.x = ("gx", 1), ("gx", 2), ("gy", 1)
        self.rest = []
        bit = self.ny // 2
        while bit > 1:
            self.rest.append(("gy", bit))
            bit //= 2
        bit = self.nx // 2
        while bit > 2:
            self.rest.append(("gx", bit))
            bit //= 2

    def send(self, value, step):
        axis, bit = step
        size = self.nx if axis == "gx" else self.ny
        return lax.ppermute(value, axis, [(i, i ^ bit) for i in range(size)])

    def owners(self):
        mask_x, mask_y = np.zeros(self.n, np.int32), np.zeros(self.n, np.int32)
        for place in range(self.n):
            steps = []
            inner, block = place % (self.n // 8), (place // (self.n // 8)) % 4
            for at_bit, step in enumerate(self.rest):
                if (inner >> at_bit) & 1:
                    steps.append(step)
            if block & 1:
                steps.append(self.x)
            if block & 2:
                steps.append(self.y)
            if place >= self.n // 2:
                steps.append(self.core)
            for axis, bit in steps:
                if axis == "gx":
                    mask_x[place] ^= bit
                else:
                    mask_y[place] ^= bit
        gx, gy = lax.axis_index("gx"), lax.axis_index("gy")
        return (gx ^ jnp.asarray(mask_x)) * self.ny + (gy ^ jnp.asarray(mask_y))

    def permutation(self, width):
        rows = width // self.n
        feature = (self.owners()[:, None] * rows + jnp.arange(rows, dtype=jnp.int32)).reshape(1, width)
        return (jnp.arange(width, dtype=jnp.int32)[:, None] == feature).astype(bf16)

    def all_sum(self, value):
        for step in [self.core, self.x, self.y] + self.rest:
            value = value + self.send(value, step)
        return value


class Gather:
    def __init__(self, cube, packed):
        self.cube, self.held = cube, [packed]

    def line(self, step):
        own = jnp.concatenate(self.held, axis=0)
        self.held = [own, self.cube.send(own, step)]

    def split(self, cols):
        own = jnp.concatenate(self.held, axis=0)
        return Gather(self.cube, own[:, :cols]), Gather(self.cube, own[:, cols:])

    def plane(self):
        own = jnp.concatenate(self.held, axis=0)
        self.held = [own, self.cube.send(own, self.cube.x), self.cube.send(own, self.cube.y)]

    def far(self):
        own, over_x, over_y = self.held
        half = own.shape[0] // 2
        far_one, far_two = self.cube.send(over_y[:half], self.cube.x), self.cube.send(over_x[half:], self.cube.y)
        near = stack(own, over_x, over_y)
        self.held = [near, far_one, far_two, self.cube.send(near, self.cube.core)]

    def across(self):
        self.held = self.held + [self.cube.send(v, self.cube.core) for v in self.held[1:3]]


class Reduce:
    def __init__(self, cube, low, high):
        self.cube, self.held = cube, []
        self.more(low, high)

    def more(self, low, high, parts=1):
        rows = high.shape[0] // parts
        got = [self.cube.send(high[i * rows : (i + 1) * rows], self.cube.core) for i in range(parts)]
        self.held = self.held + [low] + got
        self.parts = parts

    def far(self):
        cube = self.cube
        own, to_x, to_y, far_x, far_y = core_add(*self.held)
        self.held = [own, to_x, cube.send(far_y, cube.y), to_y, cube.send(far_x, cube.x)]

    def plane(self):
        cube = self.cube
        to_x, to_y = plane_add(*self.held[1:])
        self.held = [self.held[0], cube.send(to_x, cube.x), cube.send(to_y, cube.y)]

    def line(self):
        own, away = own_add(*self.held)
        self.held = [own, self.cube.send(away, self.cube.rest[-1])]

    def rest(self):
        for step in self.cube.rest[-2::-1]:
            own, away = line_add(*self.held)
            self.held = [own, self.cube.send(away, step)]

    def last(self, widths):
        return last_add(*self.held, widths)


class Order:
    def __init__(self, token):
        self.token = token

    def __call__(self, values, *transfers):
        held = [v for t in transfers for v in t.held]
        out = list(lax.optimization_barrier((self.token, *values, *held)))
        self.token, place = out[0], 1 + len(values)
        for t in transfers:
            t.held = out[place : place + len(t.held)]
            place += len(t.held)
        return out[1 : 1 + len(values)]


TILE = 128
HALF = 384


def nn(left, right):
    return lax.dot_general(left, right, (((1,), (0,)), ((), ())), preferred_element_type=f32)


def nt(left, right):
    return lax.dot_general(left, right, (((1,), (1,)), ((), ())), preferred_element_type=f32)


def tn(left, right):
    return lax.dot_general(left, right, (((0,), (0,)), ((), ())), preferred_element_type=f32)


def at(start, size):
    return pl.ds(start, size)


VMEM = pl.BlockSpec(memory_space=pltpu.VMEM)
SMEM = pl.BlockSpec(memory_space=pltpu.SMEM)
FAR = pl.BlockSpec(memory_space=pltpu.HBM)


def shape(dims, kind):
    return jax.ShapeDtypeStruct(dims, kind)


def near(dims, kind):
    return pltpu.VMEM(dims, kind)


def in_bytes(spec, dims, kind):
    if spec.memory_space is not pltpu.VMEM:
        return 0
    rows = math.prod(dims[:-1])
    return -(-rows // 16) * 16 * max(dims[-1], TILE) * jnp.dtype(kind).itemsize


def call(body, name, ins, outs, scratch, cost, *args, spare=6):
    held = sum(in_bytes(spec, a.shape, a.dtype) for spec, a in zip(ins, args))
    held += sum(in_bytes(spec, o.shape, o.dtype) for o, spec in outs)
    held //= 2
    held += sum(in_bytes(VMEM, s.shape, s.dtype) for s in scratch if getattr(s, "memory_space", None) is pltpu.VMEM)
    return pl.pallas_call(
        body,
        out_shape=[pltpu.HBM(o.shape, o.dtype) if spec is FAR else o for o, spec in outs],
        in_specs=ins,
        out_specs=[o[1] for o in outs],
        scratch_shapes=scratch,
        compiler_params=pltpu.CompilerParams(vmem_limit_bytes=held + spare * 2**20),
        cost_estimate=pl.CostEstimate(flops=0, bytes_accessed=int(cost * 3.6e4), transcendentals=0),
        name=name,
    )(*args)


def halves(value):
    lane = lax.broadcasted_iota(jnp.int32, value, 1)
    return (lane < HD, lane >= HD)


def inverse_rms(v):
    return lax.rsqrt(jnp.mean(v * v, axis=-1, keepdims=True) + norm_eps)


def norm_back(v, gain, dy, r):
    scaled = dy * gain
    mean = jnp.mean(scaled * v, axis=-1, keepdims=True)
    d_v = (scaled - v * (mean * (r * r))) * r
    return d_v, jnp.sum(dy * (v * r), axis=0, keepdims=True)


def softmax_rows(scores):
    top = jnp.max(scores, axis=-1, keepdims=True)
    expo = jnp.exp(scores - top)
    return (expo * (1.0 / jnp.sum(expo, axis=-1, keepdims=True))).astype(bf16)


def bias_body(lines, out):
    def one(i, _):
        line = lines[pl.ds(i, 1), :]
        wide = jnp.broadcast_to(line, (TILE, 2 * TILE))
        out[i] = pltpu.roll(wide, 0, 1, stride=1, stride_axis=0)[:, :TILE]
        return 0

    lax.fori_loop(0, out.shape[0], one, 0)


def copy_pieces(pieces, weights, sems, start=0):
    copies, row, cols = [], 0, weights.shape[1]
    for i, piece in enumerate(pieces):
        size = piece.shape[0]
        source = piece.at[:, pl.ds(start, cols)]
        copies.append(pltpu.make_async_copy(source, weights.at[pl.ds(row, size), :], sems.at[i]))
        copies[-1].start()
        row += size
    return copies


def wait(copies):
    for copy in copies:
        copy.wait()


def loop(count, body):
    for i in range(count):
        body(i)


def put_halves(value, low, high, start):
    cols = pl.ds(start, value.shape[1])
    low[:, cols] = value[:HALF].astype(bf16)
    high[:, cols] = value[HALF:].astype(bf16)


WIDE = 2 * TILE


def wide(i, start=0):
    return pl.ds(start + i * WIDE, WIDE)


def self_pairs(first, count, dec_len, bias, qkv, mixed, probs_out, probs, out_sems):
    tokens, inner = qkv.shape[0], qkv.shape[1] // 3
    blocks = tokens // TILE
    places = lax.broadcasted_iota(jnp.int32, (1, tokens), 1)
    limit = jnp.where(places < dec_len[0], 0.0, masked_score)
    apart = jnp.full((TILE, TILE), masked_score, f32)
    both = halves((WIDE, TILE))

    def pair(i):
        lanes = at(i * TILE, TILE)
        keys = qkv[:, at(inner + i * TILE, TILE)]
        values = qkv[:, at(2 * inner + i * TILE, TILE)]
        scores = {}
        for block in range(tokens // WIDE):
            seen = (block + 1) * WIDE
            queries = qkv[pl.ds(block * WIDE, WIDE), lanes]
            for side in range(2):
                mine = jnp.where(both[side], queries, jnp.zeros_like(queries))
                head = (2 * (first + i) + side) * blocks
                strips = []
                for row in (2 * block, 2 * block + 1):
                    tiles = [bias[head + row - j] if row >= j else apart for j in range(seen // TILE)]
                    strips.append(jnp.concatenate(tiles, axis=1))
                scores[block, side] = nt(mine, keys[:seen]) + jnp.concatenate(strips, axis=0) + limit[:, :seen]
        for block in range(tokens // WIDE):
            rows, seen = pl.ds(block * WIDE, WIDE), (block + 1) * WIDE
            got = []
            for side in range(2):
                p = softmax_rows(scores[block, side])
                probs[2 * i + side, rows, pl.ds(0, seen)] = p
                got.append(nn(p, values[:seen]))
            mixed[rows, lanes] = jnp.where(both[0], got[0], got[1]).astype(bf16)
        pltpu.make_async_copy(probs.at[pl.ds(2 * i, 2)], probs_out.at[pl.ds(2 * i, 2)], out_sems.at[i]).start()

    loop(count, pair)
    for i in range(count):
        pltpu.make_async_copy(probs.at[pl.ds(2 * i, 2)], probs_out.at[pl.ds(2 * i, 2)], out_sems.at[i]).wait()


def self_enter_body(x, *refs):
    pieces, (gains, normed, qkv_a, qkv_b, weights, sems) = refs[:6], refs[6:]
    copies = copy_pieces(pieces, weights, sems)
    xs = x[...].astype(f32)
    scaled = xs * inverse_rms(xs)
    wait(copies)
    gain_rows = jnp.transpose(weights[:, :TILE].astype(f32))
    gains[...] = gain_rows[:8]
    normed[...] = (scaled * gain_rows[0:1]).astype(bf16)
    start = TILE
    for out in (qkv_a, qkv_b):
        third = out.shape[1] // 3
        for i in range(3):
            out[:, pl.ds(i * third, third)] = nn(normed[...], weights[:, pl.ds(start, third)]).astype(bf16)
            start += third


def cross_pairs(first, count, enc_len, queries, kv, mixed, probs, probs_out, out_sems):
    inner = queries.shape[1]
    places = lax.broadcasted_iota(jnp.int32, (1, kv.shape[0]), 1)
    limit = jnp.where(places < enc_len[0], 0.0, masked_score)
    both = halves((queries.shape[0], TILE))

    def pair(i):
        lanes = at((first + i) * TILE, TILE)
        keys = kv[:, lanes]
        values = kv[:, at(inner + (first + i) * TILE, TILE)]
        here = queries[:, lanes]
        scores = [nt(jnp.where(both[side], here, jnp.zeros_like(here)), keys) + limit for side in range(2)]
        got = []
        for side in range(2):
            p = softmax_rows(scores[side])
            probs[2 * i + side] = p
            got.append(nn(p, values))
        mixed[:, at(i * TILE, TILE)] = jnp.where(both[0], got[0], got[1]).astype(bf16)
        pltpu.make_async_copy(probs.at[pl.ds(2 * i, 2)], probs_out.at[pl.ds(2 * i, 2)], out_sems.at[i]).start()

    loop(count, pair)
    for i in range(count):
        pltpu.make_async_copy(probs.at[pl.ds(2 * i, 2)], probs_out.at[pl.ds(2 * i, 2)], out_sems.at[i]).wait()


def cross_one_body(count, enc_len, x, mixed_a, mixed_b, enc, gains, *refs):
    pieces, (hidden, normed, queries, kv, mixed, probs_out, weights, probs, sems, out_sems) = refs[:6], refs[6:]
    inner = queries.shape[1]
    copies = copy_pieces(pieces, weights, sems, TILE + 3 * inner)
    part = mixed_a.shape[1]
    wait(copies)

    def enter(i):
        rows = wide(i)
        got = nt(mixed_a[...], weights[rows, pl.ds(0, part)]) + nt(mixed_b[...], weights[rows, pl.ds(part, inner - part)])
        hidden[:, rows] = x[:, rows].astype(f32) + got

    loop(hidden.shape[1] // WIDE, enter)
    v = hidden[...]
    normed[...] = (v * inverse_rms(v) * gains[1:2]).astype(bf16)

    def project_q(i):
        queries[:, wide(i)] = nn(normed[...], weights[:, wide(i, inner)]).astype(bf16)

    def project_kv(i):
        kv[:, wide(i)] = nn(enc[...], weights[:, wide(i, 2 * inner)]).astype(bf16)

    loop(inner // WIDE, project_q)
    loop(2 * inner // WIDE, project_kv)
    cross_pairs(0, count, enc_len, queries, kv, mixed, probs, probs_out, out_sems)


def cross_two_body(first, count, enc_len, hidden, queries, kv, mixed_a, *refs):
    pieces, (hidden_out, mixed, probs_out, weights, probs, sems, out_sems) = refs[:6], refs[6:]
    inner = queries.shape[1]
    part = mixed_a.shape[1]
    copies = copy_pieces(pieces, weights, sems, TILE + 7 * inner)
    cross_pairs(first, count, enc_len, queries, kv, mixed, probs, probs_out, out_sems)
    wait(copies)

    def leave(i):
        rows = wide(i)
        got = nt(mixed_a[...], weights[rows, pl.ds(0, part)]) + nt(mixed[...], weights[rows, pl.ds(part, inner - part)])
        hidden_out[:, rows] = hidden[:, rows] + got

    loop(hidden.shape[1] // WIDE, leave)


root_two_over_pi = math.sqrt(2.0 / math.pi)


def ffn_one_body(hidden, gains, *refs):
    pieces, (normed, slope, act, gated, weights, sems) = refs[:6], refs[6:]
    copies = copy_pieces(pieces, weights, sems)
    ff = gated.shape[1]
    v = hidden[...]
    normed[...] = (v * inverse_rms(v) * gains[2:3]).astype(bf16)
    wait(copies)

    def unit(i):
        cols = wide(i)
        gate = nn(normed[...], weights[:, cols])
        up = nn(normed[...], weights[:, wide(i, ff)])
        square = gate * gate
        bend = jnp.tanh(root_two_over_pi * gate * (1.0 + 0.044715 * square))
        half = 0.5 * (1.0 + bend)
        gelu = gate * half
        steep = half + 0.5 * gate * (1.0 - bend * bend) * (root_two_over_pi * (1.0 + 3 * 0.044715 * square))
        units = (gelu * up).astype(bf16)
        gated[:, cols] = units
        slope[:, cols] = (up * steep).astype(bf16)
        act[:, cols] = gelu.astype(bf16)

    loop(ff // WIDE, unit)


def ffn_grad_body(cot, gated, low, high):
    turned = jnp.transpose(cot[...])
    for i in range(gated.shape[1] // WIDE):
        put_halves(nn(turned, gated[:, wide(i)]), low, high, i * WIDE)


def ffn_two_body(cot, normed, slope, act, *refs):
    pieces, (d_gu, low, high, weights, sems) = refs[:6], refs[6:]
    ff = slope.shape[1]
    copies = copy_pieces(pieces, weights, sems, 2 * ff)
    turned = jnp.transpose(normed[...])
    wait(copies)

    def unit(i):
        cols, other = wide(i), wide(i, ff)
        d_gated = nn(cot[...], weights[:, cols])
        d_gate = (d_gated * slope[:, cols].astype(f32)).astype(bf16)
        d_up = (d_gated * act[:, cols].astype(f32)).astype(bf16)
        d_gu[:, cols] = d_gate
        d_gu[:, other] = d_up
        put_halves(nn(turned, d_gate), low, high, i * WIDE)
        put_halves(nn(turned, d_up), low, high, ff + i * WIDE)

    loop(ff // WIDE, unit)


def ffn_three_body(hidden, cot, gains, d_gu, *refs):
    pieces, (d_hidden, d_low, d_gain, weights, sems) = refs[:6], refs[6:]
    copies = copy_pieces(pieces, weights, sems)
    wait(copies)

    def back(i):
        d_hidden[:, wide(i)] = nt(d_gu[...], weights[wide(i), :])

    loop(hidden.shape[1] // WIDE, back)
    v = hidden[...]
    d_v, d_g = norm_back(v, gains[2:3], d_hidden[...], inverse_rms(v))
    d_v = d_v + cot[...].astype(f32)
    d_hidden[...] = d_v
    d_low[...] = d_v.astype(bf16)
    d_gain[...] = d_g


def output_body(hidden, gated, perm, *refs):
    pieces, (out, weights, held, sems) = refs[:6], refs[6:]
    copies = copy_pieces(pieces, weights, sems, 2 * gated.shape[1])
    wait(copies)

    def leave(i):
        held[:, wide(i)] = (hidden[:, wide(i)] + nt(gated[...], weights[wide(i), :])).astype(bf16)

    def place(i):
        out[:, wide(i)] = nt(held[...], perm[wide(i), :]).astype(bf16)

    loop(hidden.shape[1] // WIDE, leave)
    loop(hidden.shape[1] // WIDE, place)


def enc_body(d_kv_a, d_kv_b, perm, *refs):
    pieces, (out, weights, held, sems) = refs[:6], refs[6:]
    inner = held.shape[1]
    copies = copy_pieces(pieces, weights, sems, TILE + 5 * inner)
    part = d_kv_a.shape[1] // 2
    rest = inner - part
    wait(copies)

    def leave(i):
        rows = wide(i)
        got = nt(d_kv_a[:, pl.ds(0, part)], weights[rows, pl.ds(0, part)])
        got = got + nt(d_kv_b[:, pl.ds(0, rest)], weights[rows, pl.ds(part, rest)])
        got = got + nt(d_kv_a[:, pl.ds(part, part)], weights[rows, pl.ds(inner, part)])
        got = got + nt(d_kv_b[:, pl.ds(rest, rest)], weights[rows, pl.ds(inner + part, rest)])
        held[:, rows] = got.astype(bf16)

    def place(i):
        out[:, wide(i)] = nt(held[...], perm[wide(i), :]).astype(bf16)

    loop(out.shape[1] // WIDE, leave)
    loop(out.shape[1] // WIDE, place)


def fetch_probs(probs_in, probs, in_sems):
    copies = []
    for i in range(probs.shape[0] // 2):
        copies.append(pltpu.make_async_copy(probs_in.at[pl.ds(2 * i, 2)], probs.at[pl.ds(2 * i, 2)], in_sems.at[i]))
        copies[-1].start()


def cross_back_pairs(first, count, queries, kv, mixed, d_mixed, probs_in, probs, in_sems, d_q, d_kv):
    inner = queries.shape[1]
    both = halves((queries.shape[0], TILE))

    def part_of(value):
        return [jnp.where(lanes, value, jnp.zeros_like(value)) for lanes in both]

    def pair(i):
        pltpu.make_async_copy(probs_in.at[pl.ds(2 * i, 2)], probs.at[pl.ds(2 * i, 2)], in_sems.at[i]).wait()
        lanes, mine = at((first + i) * TILE, TILE), at(i * TILE, TILE)
        keys, values = part_of(kv[:, lanes]), kv[:, at(inner + (first + i) * TILE, TILE)]
        d_outs, here = part_of(d_mixed[:, lanes]), part_of(queries[:, lanes])
        d_probs = [nt(d_outs[side], values) for side in range(2)]
        result = mixed[:, mine].astype(f32)
        d_here = d_k = d_v = None
        for side in range(2):
            p = probs[2 * i + side]
            delta = jnp.sum(d_outs[side].astype(f32) * result, axis=-1, keepdims=True)
            d_s = (p.astype(f32) * (d_probs[side] - delta)).astype(bf16)
            parts = nn(d_s, keys[side]), tn(d_s, here[side]), tn(p, d_outs[side])
            d_here = parts[0] if side == 0 else d_here + parts[0]
            d_k = parts[1] if side == 0 else d_k + parts[1]
            d_v = parts[2] if side == 0 else d_v + parts[2]
        d_q[:, mine] = d_here.astype(bf16)
        d_kv[:, mine] = d_k.astype(bf16)
        d_kv[:, at((count + i) * TILE, TILE)] = d_v.astype(bf16)

    loop(count, pair)


def cross_back_one_body(count, d_low, queries, kv, mixed, *refs):
    pieces, probs_in, (d_mixed, d_q, d_kv, weights, probs, sems, in_sems) = refs[:6], refs[6], refs[7:]
    inner = queries.shape[1]
    copies = copy_pieces(pieces, weights, sems, TILE + 7 * inner)
    fetch_probs(probs_in, probs, in_sems)
    wait(copies)

    def enter(i):
        d_mixed[:, wide(i)] = nn(d_low[...], weights[:, wide(i)]).astype(bf16)

    loop(inner // WIDE, enter)
    cross_back_pairs(0, count, queries, kv, mixed, d_mixed, probs_in, probs, in_sems, d_q, d_kv)


def cross_back_two_body(first, count, *refs):
    hidden, d_hidden, gains, queries, kv, mixed, d_mixed, d_q_a = refs[:8]
    pieces, probs_in = refs[8:14], refs[14]
    d_q, d_kv, d_out, d_out_low, d_gain, weights, probs, sems, in_sems = refs[15:]
    inner = queries.shape[1]
    part = d_q_a.shape[1]
    rest = inner - part
    copies = copy_pieces(pieces, weights, sems, TILE + 4 * inner)
    fetch_probs(probs_in, probs, in_sems)
    cross_back_pairs(first, count, queries, kv, mixed, d_mixed, probs_in, probs, in_sems, d_q, d_kv)
    wait(copies)

    def back(i):
        got = nt(d_q_a[...], weights[wide(i), pl.ds(0, part)]) + nt(d_q[...], weights[wide(i), pl.ds(part, rest)])
        d_out[:, wide(i)] = got

    loop(hidden.shape[1] // WIDE, back)
    v = hidden[...]
    d_v, d_g = norm_back(v, gains[1:2], d_out[...], inverse_rms(v))
    d_v = d_v + d_hidden[...]
    d_out[...] = d_v
    d_out_low[...] = d_v.astype(bf16)
    d_gain[...] = d_g


def cross_grads_body(d_one, one_a, one_b, normed, d_q_a, d_q_b, enc, d_kv_a, d_kv_b, d_two, two_a, two_b, low, high):
    part, rest = one_a.shape[1], one_b.shape[1]
    k_a, v_a = d_kv_a.at[:, pl.ds(0, part)], d_kv_a.at[:, pl.ds(part, part)]
    k_b, v_b = d_kv_b.at[:, pl.ds(0, rest)], d_kv_b.at[:, pl.ds(rest, rest)]
    start = 0
    for left, rights in (
        (d_one, (one_a, one_b)),
        (normed, (d_q_a, d_q_b)),
        (enc, (k_a, k_b, v_a, v_b)),
        (d_two, (two_a, two_b)),
    ):
        turned = jnp.transpose(left[...])
        for right in rights:
            put_halves(nn(turned, right[...]), low, high, start)
            start += right.shape[1]


def self_back_pairs(first, count, qkv, mixed, d_mixed, probs_in, probs, in_sems, d_qkv, sums, counted):
    tokens, inner = qkv.shape[0], qkv.shape[1] // 3
    blocks, wides = tokens // TILE, tokens // WIDE
    both = halves((tokens, TILE))

    def part_of(value):
        return [jnp.where(lanes, value, jnp.zeros_like(value)) for lanes in both]

    def pair(i):
        pltpu.make_async_copy(probs_in.at[pl.ds(2 * i, 2)], probs.at[pl.ds(2 * i, 2)], in_sems.at[i]).wait()
        mine = at(i * TILE, TILE)
        here, keys = part_of(qkv[:, mine]), part_of(qkv[:, at(inner + i * TILE, TILE)])
        values = qkv[:, at(2 * inner + i * TILE, TILE)]
        d_outs = part_of(d_mixed[:, at((first + i) * TILE, TILE)])
        result = mixed[:, mine].astype(f32)
        d_probs = {}
        for side in range(2):
            for block in range(wides):
                span = slice(block * WIDE, (block + 1) * WIDE)
                d_probs[side, block] = nt(d_outs[side][span], values[: span.stop])
        d_here, d_k, d_v = [None] * wides, [None] * wides, [None] * wides
        for side in range(2):
            head = 2 * i + side
            delta = jnp.sum(d_outs[side].astype(f32) * result, axis=-1, keepdims=True)
            diagonal = [None] * blocks
            for block in range(wides):
                span = slice(block * WIDE, (block + 1) * WIDE)
                p = probs[head, pl.ds(span.start, WIDE), pl.ds(0, span.stop)]
                d_s = (p.astype(f32) * (d_probs[side, block] - delta[span])).astype(bf16)
                part = nn(d_s, keys[side][: span.stop])
                d_here[block] = part if side == 0 else d_here[block] + part
                for j in range(block + 1):
                    cols = slice(j * WIDE, (j + 1) * WIDE)
                    part = tn(d_s[:, cols], here[side][span])
                    d_k[j] = part if d_k[j] is None else d_k[j] + part
                    part = tn(p[:, cols], d_outs[side][span])
                    d_v[j] = part if d_v[j] is None else d_v[j] + part
                wider = d_s.astype(f32)
                for row in range(2):
                    for j in range(2 * block + row + 1):
                        tile = wider[row * TILE : (row + 1) * TILE, j * TILE : (j + 1) * TILE]
                        apart = 2 * block + row - j
                        diagonal[apart] = tile if diagonal[apart] is None else diagonal[apart] + tile
            for apart in range(blocks):
                tile = jnp.concatenate([diagonal[apart], jnp.zeros((TILE, TILE), f32)], axis=1)
                folded = tile[:8]
                for group in range(1, TILE // 8):
                    folded = folded + pltpu.roll(tile[group * 8 : group * 8 + 8], 2 * TILE - 8 * group, 1)
                for s in range(8):
                    sums[s, pl.ds(apart * 8 + head, 1), :] = folded[s : s + 1]
        for block in range(wides):
            rows = pl.ds(block * WIDE, WIDE)
            d_qkv[rows, mine] = d_here[block].astype(bf16)
            d_qkv[rows, at((count + i) * TILE, TILE)] = d_k[block].astype(bf16)
            d_qkv[rows, at((2 * count + i) * TILE, TILE)] = d_v[block].astype(bf16)

    loop(count, pair)
    lines = sums[0]
    for s in range(1, 8):
        lines = lines + pltpu.roll(sums[s], 2 * TILE - s, 1)
    table = None
    for apart in range(blocks):
        here = lax.dot_general(
            lines[apart * 8 : apart * 8 + 8],
            counted[apart],
            (((1,), (0,)), ((), ())),
            precision=lax.Precision.HIGHEST,
            preferred_element_type=f32,
        )
        table = here if table is None else table + here
    return table


def self_back_one_body(count, d_low, normed, qkv, mixed, counted, *refs):
    pieces, probs_in = refs[:6], refs[6]
    d_mixed, d_qkv, table, low, high, weights, probs, sums, sems, in_sems = refs[7:]
    copies = copy_pieces(pieces, weights, sems, TILE + 3 * weights.shape[1])
    fetch_probs(probs_in, probs, in_sems)
    turned = jnp.transpose(normed[...])
    wait(copies)

    def enter(i):
        d_mixed[:, wide(i)] = nn(d_low[...], weights[:, wide(i)]).astype(bf16)

    loop(d_mixed.shape[1] // WIDE, enter)
    sums[...] = jnp.zeros_like(sums)
    table[...] = self_back_pairs(
        0, count, qkv, mixed, d_mixed, probs_in, probs, in_sems, d_qkv, sums, counted
    )
    part = count * TILE

    def grads(i):
        put_halves(nn(turned, d_qkv[:, pl.ds(i * part, part)]), low, high, i * part)

    loop(3, grads)


def self_back_two_body(first, count, qkv, mixed, d_mixed, counted, table_a, probs_in, *refs):
    d_qkv, table, probs, sums, in_sems = refs
    fetch_probs(probs_in, probs, in_sems)
    sums[...] = jnp.zeros_like(sums)
    table[pl.ds(0, 8), :] = table_a[...]
    table[pl.ds(8, 8), :] = self_back_pairs(
        first, count, qkv, mixed, d_mixed, probs_in, probs, in_sems, d_qkv, sums, counted
    )


def self_back_three_body(count, x, d_hidden, gains, normed, gain_c, gain_f, d_qkv_a, d_qkv, table, spread, *refs):
    pieces, (d_x, low, high, weights, total, sems) = refs[:6], refs[6:]
    copies = copy_pieces(pieces, weights, sems, TILE)
    turned = jnp.transpose(normed[...])
    rest = count * TILE
    start = d_qkv_a.shape[1]
    head = low.shape[1] - 3 * rest

    def grads(i):
        put_halves(nn(turned, d_qkv[:, pl.ds(i * rest, rest)]), low, high, head + i * rest)

    loop(3, grads)
    wait(copies)

    def back(i):
        got = nt(d_qkv_a[...], weights[wide(i), pl.ds(0, start)])
        total[:, wide(i)] = got + nt(d_qkv[...], weights[wide(i), pl.ds(start, 3 * rest)])

    loop(x.shape[1] // WIDE, back)
    v = x[...].astype(f32)
    d_v, d_g = norm_back(v, gains[0:1], total[...], inverse_rms(v))
    d_x[...] = (d_v + d_hidden[...]).astype(bf16)
    rows = jnp.concatenate([d_g, gain_c[...], gain_f[...], jnp.zeros((TILE - 3, d_g.shape[1]), f32)], axis=0)
    found = table[...].astype(bf16)
    per_row = spread.shape[0]
    parts = []
    for j in range(per_row):
        left, right = jnp.zeros((16, j * NB), bf16), jnp.zeros((16, head - (j + 1) * NB), bf16)
        wider = ([left] if j else []) + [found] + ([right] if right.shape[1] else [])
        parts.append(nn(spread[j], jnp.concatenate(wider, axis=1)))
    side = jnp.transpose(rows)
    if head == TILE:
        lane = lax.broadcasted_iota(jnp.int32, side.shape, 1)
        side = jnp.where(lane < HD, sum(parts), pltpu.roll(side, HD, 1))
    else:
        side = jnp.concatenate([sum(parts), side], axis=1)[:, :head]
    put_halves(side, low, high, 0)


def place_body(value, perm, out):
    def place(i):
        out[:, wide(i)] = nt(value[...], perm[wide(i), :]).astype(bf16)

    loop(out.shape[1] // WIDE, place)


def stack_body(one, two, three, out, sems):
    copies, row = [], 0
    for i, value in enumerate((one, two, three)):
        copies.append(pltpu.make_async_copy(value, out.at[pl.ds(row, value.shape[0]), :], sems.at[i]))
        copies[-1].start()
        row += value.shape[0]
    wait(copies)


def stack(*values):
    rows, cols = sum(v.shape[0] for v in values), values[0].shape[1]
    out = [(shape((rows, cols), bf16), FAR)]
    return call(stack_body, "stack", [FAR] * 3, out, [pltpu.SemaphoreType.DMA((3,))], 1.0, *values, spare=2)[0]


def pack_body(part, *refs):
    gain_s, gain_c, gain_f, sq, sk, sv, so, cq, ck, cv, co, fg, fu, fo, early, third, sems = refs
    inner = sq.shape[1]
    rest = inner - part
    moves = [(v.at[:, pl.ds(0, part)], early, TILE + i * part) for i, v in enumerate((sq, sk, sv))]
    moves += [(v.at[:, pl.ds(part, rest)], early, TILE + 3 * part + i * rest) for i, v in enumerate((sq, sk, sv))]
    moves += [(v, early, TILE + (3 + i) * inner) for i, v in enumerate((so, cq, ck, cv, co))]
    moves += [(fg, third, 0), (fu, third, fg.shape[1]), (fo, third, 2 * fg.shape[1])]
    copies = []
    for i, (source, out, start) in enumerate(moves):
        copies.append(pltpu.make_async_copy(source, out.at[:, pl.ds(start, source.shape[1])], sems.at[i]))
        copies[-1].start()
    count = gain_s.shape[1]
    rows = jnp.concatenate([gain_s[...], gain_c[...], gain_f[...], jnp.zeros((TILE - 3, count), bf16)], axis=0).astype(f32)
    rows = jnp.concatenate([rows, jnp.zeros((TILE, TILE - count), f32)], axis=1)
    early[:, pl.ds(0, TILE)] = jnp.transpose(rows)[:count].astype(bf16)
    wait(copies)


def core_add_large_body(block, *refs):
    count = 4 if len(refs) > 12 else 2
    ins, outs, (lows, gots, sums, in_sems, out_sems) = refs[:count], refs[count:-5], refs[-5:]
    blocks = []
    for low, got in zip(ins[::2], ins[1::2]):
        blocks += [(low, got, i * block) for i in range(low.shape[1] // block)]
    copies = []
    for i, (low, got, start) in enumerate(blocks):
        cols = pl.ds(i * block, block)
        copies.append([])
        for j, (source, to) in enumerate(((low, lows), (got, gots))):
            copies[-1].append(pltpu.make_async_copy(source.at[:, pl.ds(start, block)], to.at[:, cols], in_sems.at[2 * i + j]))
            copies[-1][-1].start()
    leaving = []
    for i in range(len(blocks)):
        cols = pl.ds(i * block, block)
        wait(copies[i])
        sums[:, cols] = (lows[:, cols].astype(f32) + gots[:, cols].astype(f32)).astype(bf16)
        row = 0
        for j, out in enumerate(outs):
            size = out.shape[0]
            leaving.append(pltpu.make_async_copy(sums.at[pl.ds(row, size), cols], out.at[:, cols], out_sems.at[5 * i + j]))
            leaving[-1].start()
            row += size
    wait(leaving)


def core_add_large(*pairs):
    rows = pairs[0].shape[0]
    cols = [pairs[i].shape[1] for i in range(0, len(pairs), 2)]
    size = rows // 4
    total = sum(cols)
    block = max(n * TILE for n in range(1, 9) if all(c % (n * TILE) == 0 for c in cols))
    count = total // block
    sizes = (size, size, size, size // 2, size // 2)
    return call(
        lambda *refs: core_add_large_body(block, *refs),
        "core_add_large",
        [FAR] * len(pairs),
        [(shape((s, total), bf16), FAR) for s in sizes],
        [pltpu.VMEM((rows, total), bf16)] * 3 + [pltpu.SemaphoreType.DMA((2 * count,)), pltpu.SemaphoreType.DMA((5 * count,))],
        4.0,
        *pairs,
        spare=3,
    )


def core_add_body(split, *refs):
    outs = refs[-5:]

    def add(low, *gots):
        size = HALF // 4
        got = gots[0][...] if len(gots) == 1 else jnp.concatenate([g[...] for g in gots], axis=0)
        total = (low[...].astype(f32) + got.astype(f32)).astype(bf16)
        starts = (0, size, 2 * size, 3 * size, 3 * size + size // 2)
        for out, start in zip(outs, starts):
            out[...] = total[start : start + out.shape[0]]

    if split is None:
        add(*refs[:2])
    else:
        step = pl.program_id(0)
        pl.when(step < split)(lambda: add(*refs[:2]))
        pl.when(step >= split)(lambda: add(*refs[2:-5]))


def core_add(*pairs):
    rows = pairs[0].shape[0]
    cols = [pairs[0].shape[1]] + ([pairs[2].shape[1]] if len(pairs) > 2 else [])
    if sum(cols) > 5000:
        return core_add_large(*pairs)
    size = rows // 4
    block = max(n * TILE for n in range(1, 7) if all(c % (n * TILE) == 0 for c in cols))
    split = None if len(cols) == 1 else cols[0] // block
    sizes = (size, size, size, size // 2, size // 2)
    first = pl.BlockSpec((rows, block), lambda i: (0, i if split is None else jnp.minimum(i, split - 1)))
    second = pl.BlockSpec((rows, block), lambda i: (0, jnp.maximum(i - split, 0)))
    parted = pl.BlockSpec((rows // max(len(pairs) - 3, 1), block), lambda i: (0, jnp.maximum(i - split, 0)))
    total = sum(cols)
    return pl.pallas_call(
        lambda *refs: core_add_body(split, *refs),
        grid=(total // block,),
        out_shape=[shape((s, total), bf16) for s in sizes],
        in_specs=[first, first] if split is None else [first, first, second] + [parted] * (len(pairs) - 3),
        out_specs=[pl.BlockSpec((s, block), lambda i: (0, i)) for s in sizes],
        compiler_params=pltpu.CompilerParams(vmem_limit_bytes=16 * 2**20),
        cost_estimate=pl.CostEstimate(flops=0, bytes_accessed=1024, transcendentals=0),
        name="core_add",
    )(*pairs)


def plane_add_body(to_x, got_x, to_y, got_y, out_x, out_y):
    half = got_x.shape[0]
    out_x[pl.ds(0, half), :] = to_x[pl.ds(0, half), :]
    out_x[pl.ds(half, half), :] = (to_x[pl.ds(half, half), :].astype(f32) + got_x[...].astype(f32)).astype(bf16)
    out_y[pl.ds(0, half), :] = (to_y[pl.ds(0, half), :].astype(f32) + got_y[...].astype(f32)).astype(bf16)
    out_y[pl.ds(half, half), :] = to_y[pl.ds(half, half), :]


def plane_add(to_x, got_x, to_y, got_y):
    return call(
        plane_add_body, "plane_add", [VMEM] * 4, [(shape(to_x.shape, bf16), VMEM)] * 2, [], 2.0, to_x, got_x, to_y, got_y
    )


def own_add_body(own, got_x, got_y, keep, away):
    half = keep.shape[0]
    total = own[...].astype(f32) + got_x[...].astype(f32) + got_y[...].astype(f32)
    keep[...] = total[:half].astype(bf16)
    away[...] = total[half:].astype(bf16)


def own_add(own, got_x, got_y):
    half = shape((own.shape[0] // 2, own.shape[1]), bf16)
    return call(own_add_body, "own_add", [VMEM] * 3, [(half, VMEM)] * 2, [], 2.0, own, got_x, got_y)


def line_add_body(own, got, keep, away):
    half = keep.shape[0]
    total = own[...].astype(f32) + got[...].astype(f32)
    keep[...] = total[:half].astype(bf16)
    away[...] = total[half:].astype(bf16)


def line_add(own, got):
    half = shape((own.shape[0] // 2, own.shape[1]), bf16)
    return call(line_add_body, "line_add", [VMEM] * 2, [(half, VMEM)] * 2, [], 1.5, own, got)


def last_add_body(own, got, *outs):
    start = 0
    for out in outs:
        cols = pl.ds(start, out.shape[1])
        out[...] = own[:, cols].astype(f32) + got[:, cols].astype(f32)
        start += out.shape[1]


def last_add(own, got, widths):
    outs = [(shape((own.shape[0], w), f32), VMEM) for w in widths]
    return call(last_add_body, "last_add", [VMEM] * 2, outs, [], 1.5, own, got)


def bucket_of(distance):
    bucket = np.where(distance < 16, distance, 16)
    for edge in bucket_edges:
        bucket = bucket + (distance >= edge)
    return np.maximum(bucket, 0)


def split_last_body(own_a, got_a, own_b, got_b, side, *outs):
    head = side.shape[1]
    rest = (own_b.shape[1] - head) // 3
    part = outs[0].shape[1] - rest
    side[...] = own_b[:, pl.ds(0, head)].astype(f32) + got_b[:, pl.ds(0, head)].astype(f32)
    for i, out in enumerate(outs[:3]):
        cols = pl.ds(own_a.shape[1] - (3 - i) * part, part)
        out[:, pl.ds(0, part)] = own_a[:, cols].astype(f32) + got_a[:, cols].astype(f32)
        cols = pl.ds(head + i * rest, rest)
        out[:, pl.ds(part, rest)] = own_b[:, cols].astype(f32) + got_b[:, cols].astype(f32)
    for i, out in enumerate(outs[3:]):
        cols = pl.ds(i * out.shape[1], out.shape[1])
        out[...] = own_a[:, cols].astype(f32) + got_a[:, cols].astype(f32)


def layer(
    cube,
    states,
    encoded,
    cotangent,
    dec_lens,
    enc_lens,
    self_query,
    self_key,
    self_value,
    self_out,
    cross_query,
    cross_key,
    cross_value,
    cross_out,
    ffn_gate,
    ffn_up,
    ffn_out,
    gain_self,
    gain_cross,
    gain_ffn,
    table,
):
    _, tokens, width = states.shape
    enc_tokens = encoded.shape[1]
    inner, ff = self_query.shape[1], ffn_gate.shape[1]
    own_rows = self_query.shape[0]
    blocks = tokens // TILE
    pairs = inner // TILE
    early = pairs // 2
    late = pairs - early
    part, rest = early * TILE, late * TILE
    sems = pltpu.SemaphoreType.DMA
    fence = Order(dec_lens)

    def weight_mem(cols):
        return pltpu.VMEM((width, cols), bf16)

    def mem(*dims):
        return pltpu.VMEM(dims, bf16)

    widths = (TILE + 8 * inner, 3 * ff)
    second = TILE + 3 * inner
    packed = call(
        lambda *refs: pack_body(part, *refs),
        "pack",
        [VMEM] * 3 + [FAR] * 11,
        [(shape((own_rows, w), bf16), VMEM) for w in widths],
        [sems((14,))],
        2.0,
        *(gain_self.reshape(1, -1), gain_cross.reshape(1, -1), gain_ffn.reshape(1, -1)),
        *(self_query, self_key, self_value, self_out, cross_query, cross_key, cross_value, cross_out, ffn_gate, ffn_up, ffn_out),
        spare=60,
    )
    A, C = (Gather(cube, p) for p in packed)
    lines_of = cube.rest
    for step in lines_of[:-1]:
        A.line(step)
    perm = cube.permutation(width)

    lane = np.arange(2 * TILE)
    signed = np.where(lane < TILE, lane, lane - 2 * TILE)
    distance = np.arange(blocks)[:, None] * TILE - signed[None, :]
    chosen = (np.arange(NB)[:, None] == bucket_of(distance).reshape(1, -1)).astype(np.float32)
    lines = lax.dot_general(table, jnp.asarray(chosen, bf16), (((0,), (0,)), ((), ())), preferred_element_type=f32)
    lines = jnp.where(jnp.asarray(distance.reshape(1, -1) >= 0), lines, masked_score)
    lines = lines.reshape(H * blocks, 2 * TILE)
    counted = (bucket_of(distance)[:, :, None] == np.arange(NB)) & (distance >= 0)[:, :, None]
    counted = jnp.asarray(counted.astype(np.float32))

    token_bf = shape((tokens, width), bf16)
    token_f32 = shape((tokens, width), f32)
    row_f32 = shape((1, width), f32)

    (bias,) = call(bias_body, "bias", [VMEM], [(shape((H * blocks, TILE, TILE), f32), VMEM)], [], 5.0, lines)
    bias, perm = fence([bias, perm], A)
    A.line(lines_of[-1])
    x = nn(states[0], perm).astype(bf16)
    enc = nn(encoded[0], perm).astype(bf16)
    cot = nn(cotangent[0], perm).astype(bf16)
    x, enc, cot = fence([x, enc, cot], A, C)
    A.plane()
    for step in lines_of[:-1]:
        C.line(step)
    fence([], A, C)
    A.far()
    C.line(lines_of[-1])
    fence([], A, C)
    A.across()
    C.plane()
    (x,) = fence([x], A)
    gains, normed_one, qkv_a, qkv_b = call(
        self_enter_body,
        "self_enter",
        [VMEM] + [FAR] * 6,
        [
            (shape((8, width), f32), VMEM),
            (token_bf, VMEM),
            (shape((tokens, 3 * part), bf16), VMEM),
            (shape((tokens, 3 * rest), bf16), VMEM),
        ],
        [weight_mem(second), sems((10,))],
        6.0,
        *(x, *A.held),
    )

    def self_heads(first, count, qkv):
        return call(
            lambda *refs: self_pairs(first, count, *refs),
            "self_heads",
            [SMEM, VMEM, VMEM],
            [(shape((tokens, count * TILE), bf16), VMEM), (shape((2 * count, tokens, tokens), bf16), FAR)],
            [mem(2 * count, tokens, tokens), sems((count,))],
            8.0,
            *(dec_lens, bias, qkv),
        )

    mixed_one_a, probs_one_a = self_heads(0, early, qkv_a)
    mixed_one_a, qkv_b = fence([mixed_one_a, qkv_b])
    mixed_one_b, probs_one_b = self_heads(early, late, qkv_b)
    (mixed_one_b,) = fence([mixed_one_b])
    hidden_one, normed_two, q_two, kv_two, mixed_two_a, probs_two_a = call(
        lambda *refs: cross_one_body(early, *refs),
        "cross_one",
        [SMEM] + [VMEM] * 5 + [FAR] * 6,
        [
            (token_f32, VMEM),
            (token_bf, VMEM),
            (shape((tokens, inner), bf16), VMEM),
            (shape((enc_tokens, 2 * inner), bf16), VMEM),
            (shape((tokens, part), bf16), VMEM),
            (shape((2 * early, tokens, enc_tokens), bf16), FAR),
        ],
        [weight_mem(4 * inner), mem(2 * early, tokens, enc_tokens), sems((10,)), sems((early,))],
        13.0,
        *(enc_lens, x, mixed_one_a, mixed_one_b, enc, gains, *A.held),
    )
    hidden_one, normed_two, q_two, kv_two, mixed_two_a, probs_two_a = fence(
        [hidden_one, normed_two, q_two, kv_two, mixed_two_a, probs_two_a], C
    )
    C.far()
    hidden_two, mixed_two_b, probs_two_b = call(
        lambda *refs: cross_two_body(early, late, *refs),
        "cross_two",
        [SMEM] + [VMEM] * 4 + [FAR] * 6,
        [(token_f32, VMEM), (shape((tokens, rest), bf16), VMEM), (shape((2 * late, tokens, enc_tokens), bf16), FAR)],
        [weight_mem(inner), mem(2 * late, tokens, enc_tokens), sems((10,)), sems((late,))],
        10.0,
        *(enc_lens, hidden_one, q_two, kv_two, mixed_two_a, *A.held),
    )
    (hidden_two,) = fence([hidden_two], C)
    C.across()
    (hidden_two,) = fence([hidden_two], C)
    units = shape((tokens, ff), bf16)
    near_units = near((tokens, ff), bf16)
    half_ff = shape((HALF, ff), bf16)
    normed_three, slope, act, gated = call(
        ffn_one_body,
        "ffn_one",
        [VMEM] * 2 + [FAR] * 6,
        [(token_bf, VMEM), (near_units, VMEM), (near_units, VMEM), (units, VMEM)],
        [weight_mem(2 * ff), sems((6,))],
        10.0,
        *(hidden_two, gains, *C.held),
    )
    normed_three, gated, slope, act = fence([normed_three, gated, slope, act])
    fo_low, fo_high = call(
        ffn_grad_body, "ffn_grad", [VMEM] * 2, [(half_ff, VMEM)] * 2, [], 4.0, cot, gated
    )
    fo_low, fo_high, slope, act = fence([fo_low, fo_high, slope, act])
    R1 = Reduce(cube, fo_low, fo_high)
    half_gu = shape((HALF, 2 * ff), bf16)
    d_gu, gu_low, gu_high = call(
        ffn_two_body,
        "ffn_two",
        [VMEM] * 4 + [FAR] * 6,
        [(near((tokens, 2 * ff), bf16), VMEM), (half_gu, VMEM), (half_gu, VMEM)],
        [weight_mem(ff), sems((6,))],
        10.0,
        *(cot, normed_three, slope, act, *C.held),
    )
    gu_low, gu_high, d_gu = fence([gu_low, gu_high, d_gu], R1)
    R1.more(gu_low, gu_high)
    d_hidden_two, d_low_two, gain_f = call(
        ffn_three_body,
        "ffn_three",
        [VMEM] * 4 + [FAR] * 6,
        [(token_f32, VMEM), (token_bf, VMEM), (row_f32, VMEM)],
        [weight_mem(2 * ff), sems((10,))],
        5.0,
        *(hidden_two, cot, gains, d_gu, *C.held),
    )
    d_hidden_two, d_low_two, gain_f = fence([d_hidden_two, d_low_two, gain_f], R1)
    R1.far()
    d_mixed_two, d_q_a, d_kv_a = call(
        lambda *refs: cross_back_one_body(early, *refs),
        "cross_back_one",
        [VMEM] * 4 + [FAR] * 7,
        [
            (shape((tokens, inner), bf16), VMEM),
            (shape((tokens, part), bf16), VMEM),
            (shape((enc_tokens, 2 * part), bf16), VMEM),
        ],
        [
            weight_mem(inner),
            mem(2 * early, tokens, enc_tokens),
            sems((10,)),
            sems((early,)),
        ],
        8.0,
        *(d_low_two, q_two, kv_two, mixed_two_a, *A.held, probs_two_a),
    )
    d_mixed_two, d_q_a, d_kv_a = fence([d_mixed_two, d_q_a, d_kv_a], R1)
    R1.plane()
    d_q_b, d_kv_b, d_hidden_one, d_low_one, gain_c = call(
        lambda *refs: cross_back_two_body(early, late, *refs),
        "cross_back_two",
        [VMEM] * 8 + [FAR] * 7,
        [
            (shape((tokens, rest), bf16), VMEM),
            (shape((enc_tokens, 2 * rest), bf16), VMEM),
            (token_f32, VMEM),
            (token_bf, VMEM),
            (row_f32, VMEM),
        ],
        [
            weight_mem(inner),
            mem(2 * late, tokens, enc_tokens),
            sems((10,)),
            sems((late,)),
        ],
        8.0,
        *(hidden_one, d_hidden_two, gains, q_two, kv_two, mixed_two_b, d_mixed_two, d_q_a, *A.held, probs_two_b),
    )
    d_q_b, d_kv_b, d_hidden_one, d_low_one, gain_c = fence([d_q_b, d_kv_b, d_hidden_one, d_low_one, gain_c])
    half_a = shape((HALF, 3 * part), bf16)
    d_mixed_one, d_qkv_a, table_a, self_low_a, self_high_a = call(
        lambda *refs: self_back_one_body(early, *refs),
        "self_back_one",
        [VMEM] * 5 + [FAR] * 7,
        [
            (shape((tokens, inner), bf16), VMEM),
            (shape((tokens, 3 * part), bf16), VMEM),
            (shape((8, NB), f32), VMEM),
            (half_a, VMEM),
            (half_a, VMEM),
        ],
        [
            weight_mem(inner),
            mem(2 * early, tokens, tokens),
            pltpu.VMEM((8, 8 * blocks, 2 * TILE), f32),
            sems((6,)),
            sems((early,)),
        ],
        9.0,
        *(d_low_one, normed_one, qkv_a, mixed_one_a, counted, *A.held, probs_one_a),
    )
    self_low_a, self_high_a, d_qkv_a, d_mixed_one, table_a, d_q_b, d_low_two = fence(
        [self_low_a, self_high_a, d_qkv_a, d_mixed_one, table_a, d_q_b, d_low_two]
    )
    half_cross = shape((HALF, 5 * inner), bf16)
    cross_low, cross_high = call(
        cross_grads_body,
        "cross_grads",
        [VMEM] * 12,
        [(half_cross, VMEM)] * 2,
        [],
        9.0,
        *(d_low_one, mixed_one_a, mixed_one_b, normed_two, d_q_a, d_q_b, enc, d_kv_a, d_kv_b, d_low_two, mixed_two_a, mixed_two_b),
    )
    cross_low, cross_high, d_kv_b = fence([cross_low, cross_high, d_kv_b], R1)
    R1.line()
    R3 = Reduce(cube, cross_low, cross_high)
    R3.more(self_low_a, self_high_a)
    (grad_enc,) = call(
        enc_body,
        "grad_encoded",
        [VMEM] * 3 + [FAR] * 6,
        [(shape((enc_tokens, width), bf16), VMEM)],
        [weight_mem(2 * inner), mem(enc_tokens, width), sems((10,))],
        5.0,
        *(d_kv_a, d_kv_b, perm, *A.held),
    )
    d_qkv_a, grad_enc = fence([d_qkv_a, grad_enc], R3)
    R3.far()
    per_row = -(-H // own_rows)
    head_cols = TILE if per_row * NB <= HD else per_row * NB + TILE
    placed = np.zeros((per_row, width, 16), np.float32)
    for h in range(H):
        slot = h if h < 2 * early else 8 + h - 2 * early
        placed[h % per_row, h // per_row :: own_rows, slot] = 1.0
    half_b = shape((HALF, head_cols + 3 * rest), bf16)
    d_qkv_b, table_sum = call(
        lambda *refs: self_back_two_body(early, late, *refs),
        "self_back_two",
        [VMEM] * 5 + [FAR],
        [(shape((tokens, 3 * rest), bf16), VMEM), (shape((16, NB), f32), VMEM)],
        [
            mem(2 * late, tokens, tokens),
            pltpu.VMEM((8, 8 * blocks, 2 * TILE), f32),
            sems((late,)),
        ],
        7.0,
        *(qkv_b, mixed_one_b, d_mixed_one, counted, table_a, probs_one_b),
    )
    d_qkv_b, table_sum = fence([d_qkv_b, table_sum], R3, R1)
    R3.plane()
    R1.rest()
    d_x, self_low_b, self_high_b = call(
        lambda *refs: self_back_three_body(late, *refs),
        "self_back_three",
        [VMEM] * 10 + [FAR] * 6,
        [(token_bf, VMEM), (half_b, VMEM), (half_b, VMEM)],
        [
            weight_mem(3 * inner),
            pltpu.VMEM((tokens, width), f32),
            sems((6,)),
        ],
        5.0,
        *(x, d_hidden_one, gains, normed_one, gain_c, gain_f, d_qkv_a, d_qkv_b, table_sum, jnp.asarray(placed, bf16)),
        *A.held,
    )
    self_low_b, self_high_b, d_x, gated = fence([self_low_b, self_high_b, d_x, gated])
    (grad_states,) = call(place_body, "grad_states", [VMEM] * 2, [(token_bf, VMEM)], [], 2.0, d_x, perm)
    (output,) = call(
        output_body,
        "output",
        [VMEM] * 3 + [FAR] * 6,
        [(token_bf, VMEM)],
        [weight_mem(ff), mem(tokens, width), sems((10,))],
        6.0,
        *(hidden_two, gated, perm, *C.held),
    )
    output, grad_states, self_high_b = fence([output, grad_states, self_high_b], R3, R1)
    R5 = Reduce(cube, self_low_b, self_high_b)
    R3.line()
    g_fo, g_fg, g_fu = R1.last((ff, ff, ff))
    (g_fo,) = fence([g_fo], R5)
    R5.far()
    fence([], R5)
    R5.plane()
    fence([], R3)
    R3.rest()
    fence([], R5)
    R5.line()
    fence([], R5)
    R5.rest()
    fence([], R3, R5)
    sizes = (head_cols,) + (inner,) * 8
    side, g_sq, g_sk, g_sv, g_so, g_cq, g_ck, g_cv, g_co = call(
        split_last_body,
        "last_self",
        [VMEM] * 4,
        [(shape((own_rows, w), f32), VMEM) for w in sizes],
        [],
        1.5,
        *(*R3.held, *R5.held),
    )
    heads = [side[h // per_row, (h % per_row) * NB : (h % per_row + 1) * NB] for h in range(H)]
    if per_row == 1:
        grad_table = side[:H, :NB].T
    else:
        grad_table = jnp.stack(heads, axis=1)
    first_gain = HD if head_cols == TILE else per_row * NB
    g_gains = side[:, first_gain : first_gain + 3]
    return (
        output[None],
        grad_states[None],
        grad_enc[None],
        g_sq,
        g_sk,
        g_sv,
        g_so,
        g_cq,
        g_ck,
        g_cv,
        g_co,
        g_fg,
        g_fu,
        g_fo,
        g_gains[:, 0],
        g_gains[:, 1],
        g_gains[:, 2],
        grad_table,
    )


def solution(mesh):
    cube = Cube(mesh)
    both = ("gx", "gy")
    row, flat, one = P(both, None, None), P(both, None), P(both)
    in_specs = (row, row, row, one, one) + (flat,) * 11 + (one,) * 3 + (P(),)
    out_specs = (row, row, row) + (flat,) * 11 + (one,) * 3 + (P(),)

    def per_device(*args):
        return layer(cube, *args)

    return jax.shard_map(per_device, mesh=mesh, in_specs=in_specs, out_specs=out_specs, check_vma=False)
```

```python
import math

import jax
import jax.numpy as jnp
import numpy as np
from jax import lax
from jax.experimental import pallas as pl
from jax.experimental.pallas import tpu as pltpu
from jax.sharding import PartitionSpec as P

H = 12
HD = 64
NB = 32

norm_eps = 1e-06
masked_score = -1000000000.0
bucket_edges = [int(math.ceil(16 * 8 ** (power / 16.0))) for power in range(1, 16)]

bf16 = jnp.bfloat16
f32 = jnp.float32


class Cube:
    def __init__(self, mesh):
        self.nx, self.ny = mesh.shape["gx"], mesh.shape["gy"]
        self.n = self.nx * self.ny
        self.core, self.y, self.x = ("gx", 1), ("gx", 2), ("gy", 1)
        self.rest = []
        bit = self.ny // 2
        while bit > 1:
            self.rest.append(("gy", bit))
            bit //= 2
        bit = self.nx // 2
        while bit > 2:
            self.rest.append(("gx", bit))
            bit //= 2

    def send(self, value, step):
        axis, bit = step
        size = self.nx if axis == "gx" else self.ny
        return lax.ppermute(value, axis, [(i, i ^ bit) for i in range(size)])

    def owners(self):
        mask_x, mask_y = np.zeros(self.n, np.int32), np.zeros(self.n, np.int32)
        for place in range(self.n):
            steps = []
            inner, block = place % (self.n // 8), (place // (self.n // 8)) % 4
            for at_bit, step in enumerate(self.rest):
                if (inner >> at_bit) & 1:
                    steps.append(step)
            if block & 1:
                steps.append(self.x)
            if block & 2:
                steps.append(self.y)
            if place >= self.n // 2:
                steps.append(self.core)
            for axis, bit in steps:
                if axis == "gx":
                    mask_x[place] ^= bit
                else:
                    mask_y[place] ^= bit
        gx, gy = lax.axis_index("gx"), lax.axis_index("gy")
        return (gx ^ jnp.asarray(mask_x)) * self.ny + (gy ^ jnp.asarray(mask_y))

    def permutation(self, width):
        rows = width // self.n
        feature = (self.owners()[:, None] * rows + jnp.arange(rows, dtype=jnp.int32)).reshape(1, width)
        return (jnp.arange(width, dtype=jnp.int32)[:, None] == feature).astype(bf16)

    def all_sum(self, value):
        for step in [self.core, self.x, self.y] + self.rest:
            value = value + self.send(value, step)
        return value


class Gather:
    def __init__(self, cube, packed):
        self.cube, self.held = cube, [packed]

    def line(self, step):
        own = jnp.concatenate(self.held, axis=0)
        self.held = [own, self.cube.send(own, step)]

    def split(self, cols):
        own = jnp.concatenate(self.held, axis=0)
        return Gather(self.cube, own[:, :cols]), Gather(self.cube, own[:, cols:])

    def plane(self):
        own = jnp.concatenate(self.held, axis=0)
        self.held = [own, self.cube.send(own, self.cube.x), self.cube.send(own, self.cube.y)]

    def far(self):
        own, over_x, over_y = self.held
        half = own.shape[0] // 2
        far_one, far_two = self.cube.send(over_y[:half], self.cube.x), self.cube.send(over_x[half:], self.cube.y)
        near = stack(own, over_x, over_y)
        self.held = [near, far_one, far_two, self.cube.send(near, self.cube.core)]

    def across(self):
        self.held = self.held + [self.cube.send(v, self.cube.core) for v in self.held[1:3]]


class Reduce:
    def __init__(self, cube, low, high):
        self.cube, self.held = cube, []
        self.more(low, high)

    def more(self, low, high, parts=1):
        rows = high.shape[0] // parts
        got = [self.cube.send(high[i * rows : (i + 1) * rows], self.cube.core) for i in range(parts)]
        self.held = self.held + [low] + got
        self.parts = parts

    def far(self):
        cube = self.cube
        own, to_x, to_y, far_x, far_y = core_add(*self.held)
        self.held = [own, to_x, cube.send(far_y, cube.y), to_y, cube.send(far_x, cube.x)]

    def plane(self):
        cube = self.cube
        to_x, to_y = plane_add(*self.held[1:])
        self.held = [self.held[0], cube.send(to_x, cube.x), cube.send(to_y, cube.y)]

    def line(self):
        own, away = own_add(*self.held)
        self.held = [own, self.cube.send(away, self.cube.rest[-1])]

    def rest(self):
        for step in self.cube.rest[-2::-1]:
            own, away = line_add(*self.held)
            self.held = [own, self.cube.send(away, step)]

    def last(self, widths):
        return last_add(*self.held, widths)


class Order:
    def __init__(self, token):
        self.token = token

    def __call__(self, values, *transfers):
        held = [v for t in transfers for v in t.held]
        out = list(lax.optimization_barrier((self.token, *values, *held)))
        self.token, place = out[0], 1 + len(values)
        for t in transfers:
            t.held = out[place : place + len(t.held)]
            place += len(t.held)
        return out[1 : 1 + len(values)]


TILE = 128
HALF = 384


def nn(left, right):
    return lax.dot_general(left, right, (((1,), (0,)), ((), ())), preferred_element_type=f32)


def nt(left, right):
    return lax.dot_general(left, right, (((1,), (1,)), ((), ())), preferred_element_type=f32)


def tn(left, right):
    return lax.dot_general(left, right, (((0,), (0,)), ((), ())), preferred_element_type=f32)


def at(start, size):
    return pl.ds(start, size)


VMEM = pl.BlockSpec(memory_space=pltpu.VMEM)
SMEM = pl.BlockSpec(memory_space=pltpu.SMEM)
FAR = pl.BlockSpec(memory_space=pltpu.HBM)


def shape(dims, kind):
    return jax.ShapeDtypeStruct(dims, kind)


def near(dims, kind):
    return pltpu.VMEM(dims, kind)


def in_bytes(spec, dims, kind):
    if spec.memory_space is not pltpu.VMEM:
        return 0
    rows = math.prod(dims[:-1])
    return -(-rows // 16) * 16 * max(dims[-1], TILE) * jnp.dtype(kind).itemsize


def call(body, name, ins, outs, scratch, cost, *args, spare=6):
    held = sum(in_bytes(spec, a.shape, a.dtype) for spec, a in zip(ins, args))
    held += sum(in_bytes(spec, o.shape, o.dtype) for o, spec in outs)
    held //= 2
    held += sum(in_bytes(VMEM, s.shape, s.dtype) for s in scratch if getattr(s, "memory_space", None) is pltpu.VMEM)
    return pl.pallas_call(
        body,
        out_shape=[pltpu.HBM(o.shape, o.dtype) if spec is FAR else o for o, spec in outs],
        in_specs=ins,
        out_specs=[o[1] for o in outs],
        scratch_shapes=scratch,
        compiler_params=pltpu.CompilerParams(vmem_limit_bytes=held + spare * 2**20),
        cost_estimate=pl.CostEstimate(flops=0, bytes_accessed=int(cost * 3.6e4), transcendentals=0),
        name=name,
    )(*args)


def halves(value):
    lane = lax.broadcasted_iota(jnp.int32, value, 1)
    return (lane < HD, lane >= HD)


def inverse_rms(v):
    return lax.rsqrt(jnp.mean(v * v, axis=-1, keepdims=True) + norm_eps)


def norm_back(v, gain, dy, r):
    scaled = dy * gain
    mean = jnp.mean(scaled * v, axis=-1, keepdims=True)
    d_v = (scaled - v * (mean * (r * r))) * r
    return d_v, jnp.sum(dy * (v * r), axis=0, keepdims=True)


def softmax_rows(scores):
    top = jnp.max(scores, axis=-1, keepdims=True)
    expo = jnp.exp(scores - top)
    return (expo * (1.0 / jnp.sum(expo, axis=-1, keepdims=True))).astype(bf16)


def bias_body(lines, out):
    def one(i, _):
        line = lines[pl.ds(i, 1), :]
        wide = jnp.broadcast_to(line, (TILE, 2 * TILE))
        out[i] = pltpu.roll(wide, 0, 1, stride=1, stride_axis=0)[:, :TILE]
        return 0

    lax.fori_loop(0, out.shape[0], one, 0)


def copy_pieces(pieces, weights, sems, start=0):
    copies, row, cols = [], 0, weights.shape[1]
    for i, piece in enumerate(pieces):
        size = piece.shape[0]
        source = piece.at[:, pl.ds(start, cols)]
        copies.append(pltpu.make_async_copy(source, weights.at[pl.ds(row, size), :], sems.at[i]))
        copies[-1].start()
        row += size
    return copies


def wait(copies):
    for copy in copies:
        copy.wait()


def loop(count, body):
    for i in range(count):
        body(i)


def put_halves(value, low, high, start):
    cols = pl.ds(start, value.shape[1])
    low[:, cols] = value[:HALF].astype(bf16)
    high[:, cols] = value[HALF:].astype(bf16)


WIDE = 2 * TILE


def wide(i, start=0):
    return pl.ds(start + i * WIDE, WIDE)


def self_pairs(first, count, dec_len, bias, qkv, mixed, probs_out, probs, out_sems):
    tokens, inner = qkv.shape[0], qkv.shape[1] // 3
    blocks = tokens // TILE
    places = lax.broadcasted_iota(jnp.int32, (1, tokens), 1)
    limit = jnp.where(places < dec_len[0], 0.0, masked_score)
    apart = jnp.full((TILE, TILE), masked_score, f32)
    both = halves((WIDE, TILE))

    def pair(i):
        lanes = at(i * TILE, TILE)
        keys = qkv[:, at(inner + i * TILE, TILE)]
        values = qkv[:, at(2 * inner + i * TILE, TILE)]
        scores = {}
        for block in range(tokens // WIDE):
            seen = (block + 1) * WIDE
            queries = qkv[pl.ds(block * WIDE, WIDE), lanes]
            for side in range(2):
                mine = jnp.where(both[side], queries, jnp.zeros_like(queries))
                head = (2 * (first + i) + side) * blocks
                strips = []
                for row in (2 * block, 2 * block + 1):
                    tiles = [bias[head + row - j] if row >= j else apart for j in range(seen // TILE)]
                    strips.append(jnp.concatenate(tiles, axis=1))
                scores[block, side] = nt(mine, keys[:seen]) + jnp.concatenate(strips, axis=0) + limit[:, :seen]
        for block in range(tokens // WIDE):
            rows, seen = pl.ds(block * WIDE, WIDE), (block + 1) * WIDE
            got = []
            for side in range(2):
                p = softmax_rows(scores[block, side])
                probs[2 * i + side, rows, pl.ds(0, seen)] = p
                got.append(nn(p, values[:seen]))
            mixed[rows, lanes] = jnp.where(both[0], got[0], got[1]).astype(bf16)
        pltpu.make_async_copy(probs.at[pl.ds(2 * i, 2)], probs_out.at[pl.ds(2 * i, 2)], out_sems.at[i]).start()

    loop(count, pair)
    for i in range(count):
        pltpu.make_async_copy(probs.at[pl.ds(2 * i, 2)], probs_out.at[pl.ds(2 * i, 2)], out_sems.at[i]).wait()


def self_enter_body(x, *refs):
    pieces, (gains, normed, qkv_a, qkv_b, weights, sems) = refs[:6], refs[6:]
    copies = copy_pieces(pieces, weights, sems)
    xs = x[...].astype(f32)
    scaled = xs * inverse_rms(xs)
    wait(copies)
    gain_rows = jnp.transpose(weights[:, :TILE].astype(f32))
    gains[...] = gain_rows[:8]
    normed[...] = (scaled * gain_rows[0:1]).astype(bf16)
    start = TILE
    for out in (qkv_a, qkv_b):
        third = out.shape[1] // 3
        for i in range(3):
            out[:, pl.ds(i * third, third)] = nn(normed[...], weights[:, pl.ds(start, third)]).astype(bf16)
            start += third


def cross_pairs(first, count, enc_len, queries, kv, mixed, probs, probs_out, out_sems):
    inner = queries.shape[1]
    places = lax.broadcasted_iota(jnp.int32, (1, kv.shape[0]), 1)
    limit = jnp.where(places < enc_len[0], 0.0, masked_score)
    both = halves((queries.shape[0], TILE))

    def pair(i):
        lanes = at((first + i) * TILE, TILE)
        keys = kv[:, lanes]
        values = kv[:, at(inner + (first + i) * TILE, TILE)]
        here = queries[:, lanes]
        scores = [nt(jnp.where(both[side], here, jnp.zeros_like(here)), keys) + limit for side in range(2)]
        got = []
        for side in range(2):
            p = softmax_rows(scores[side])
            probs[2 * i + side] = p
            got.append(nn(p, values))
        mixed[:, at(i * TILE, TILE)] = jnp.where(both[0], got[0], got[1]).astype(bf16)
        pltpu.make_async_copy(probs.at[pl.ds(2 * i, 2)], probs_out.at[pl.ds(2 * i, 2)], out_sems.at[i]).start()

    loop(count, pair)
    for i in range(count):
        pltpu.make_async_copy(probs.at[pl.ds(2 * i, 2)], probs_out.at[pl.ds(2 * i, 2)], out_sems.at[i]).wait()


def cross_one_body(count, enc_len, x, mixed_a, mixed_b, enc, gains, *refs):
    pieces, (hidden, normed, queries, kv, mixed, probs_out, weights, probs, sems, out_sems) = refs[:6], refs[6:]
    inner = queries.shape[1]
    copies = copy_pieces(pieces, weights, sems, TILE + 3 * inner)
    part = mixed_a.shape[1]
    wait(copies)

    def enter(i):
        rows = wide(i)
        got = nt(mixed_a[...], weights[rows, pl.ds(0, part)]) + nt(mixed_b[...], weights[rows, pl.ds(part, inner - part)])
        hidden[:, rows] = x[:, rows].astype(f32) + got

    loop(hidden.shape[1] // WIDE, enter)
    v = hidden[...]
    normed[...] = (v * inverse_rms(v) * gains[1:2]).astype(bf16)

    def project_q(i):
        queries[:, wide(i)] = nn(normed[...], weights[:, wide(i, inner)]).astype(bf16)

    def project_kv(i):
        kv[:, wide(i)] = nn(enc[...], weights[:, wide(i, 2 * inner)]).astype(bf16)

    loop(inner // WIDE, project_q)
    loop(2 * inner // WIDE, project_kv)
    cross_pairs(0, count, enc_len, queries, kv, mixed, probs, probs_out, out_sems)


def cross_two_body(first, count, enc_len, hidden, queries, kv, mixed_a, *refs):
    pieces, (hidden_out, mixed, probs_out, weights, probs, sems, out_sems) = refs[:6], refs[6:]
    inner = queries.shape[1]
    part = mixed_a.shape[1]
    copies = copy_pieces(pieces, weights, sems, TILE + 7 * inner)
    cross_pairs(first, count, enc_len, queries, kv, mixed, probs, probs_out, out_sems)
    wait(copies)

    def leave(i):
        rows = wide(i)
        got = nt(mixed_a[...], weights[rows, pl.ds(0, part)]) + nt(mixed[...], weights[rows, pl.ds(part, inner - part)])
        hidden_out[:, rows] = hidden[:, rows] + got

    loop(hidden.shape[1] // WIDE, leave)


root_two_over_pi = math.sqrt(2.0 / math.pi)


def ffn_one_body(hidden, gains, *refs):
    pieces, (normed, slope, act, gated, weights, sems) = refs[:6], refs[6:]
    copies = copy_pieces(pieces, weights, sems)
    ff = gated.shape[1]
    v = hidden[...]
    normed[...] = (v * inverse_rms(v) * gains[2:3]).astype(bf16)
    wait(copies)

    def unit(i):
        cols = wide(i)
        gate = nn(normed[...], weights[:, cols])
        up = nn(normed[...], weights[:, wide(i, ff)])
        square = gate * gate
        bend = jnp.tanh(root_two_over_pi * gate * (1.0 + 0.044715 * square))
        half = 0.5 * (1.0 + bend)
        gelu = gate * half
        steep = half + 0.5 * gate * (1.0 - bend * bend) * (root_two_over_pi * (1.0 + 3 * 0.044715 * square))
        units = (gelu * up).astype(bf16)
        gated[:, cols] = units
        slope[:, cols] = (up * steep).astype(bf16)
        act[:, cols] = gelu.astype(bf16)

    loop(ff // WIDE, unit)


def ffn_grad_body(cot, gated, low, high):
    turned = jnp.transpose(cot[...])
    for i in range(gated.shape[1] // WIDE):
        put_halves(nn(turned, gated[:, wide(i)]), low, high, i * WIDE)


def ffn_two_body(cot, normed, slope, act, *refs):
    pieces, (d_gu, low, high, weights, sems) = refs[:6], refs[6:]
    ff = slope.shape[1]
    copies = copy_pieces(pieces, weights, sems, 2 * ff)
    turned = jnp.transpose(normed[...])
    wait(copies)

    def unit(i):
        cols, other = wide(i), wide(i, ff)
        d_gated = nn(cot[...], weights[:, cols])
        d_gate = (d_gated * slope[:, cols].astype(f32)).astype(bf16)
        d_up = (d_gated * act[:, cols].astype(f32)).astype(bf16)
        d_gu[:, cols] = d_gate
        d_gu[:, other] = d_up
        put_halves(nn(turned, d_gate), low, high, i * WIDE)
        put_halves(nn(turned, d_up), low, high, ff + i * WIDE)

    loop(ff // WIDE, unit)


def ffn_three_body(hidden, cot, gains, d_gu, *refs):
    pieces, (d_hidden, d_low, d_gain, weights, sems) = refs[:6], refs[6:]
    copies = copy_pieces(pieces, weights, sems)
    wait(copies)

    def back(i):
        d_hidden[:, wide(i)] = nt(d_gu[...], weights[wide(i), :])

    loop(hidden.shape[1] // WIDE, back)
    v = hidden[...]
    d_v, d_g = norm_back(v, gains[2:3], d_hidden[...], inverse_rms(v))
    d_v = d_v + cot[...].astype(f32)
    d_hidden[...] = d_v
    d_low[...] = d_v.astype(bf16)
    d_gain[...] = d_g


def output_body(hidden, gated, perm, *refs):
    pieces, (out, weights, held, sems) = refs[:6], refs[6:]
    copies = copy_pieces(pieces, weights, sems, 2 * gated.shape[1])
    wait(copies)

    def leave(i):
        held[:, wide(i)] = (hidden[:, wide(i)] + nt(gated[...], weights[wide(i), :])).astype(bf16)

    def place(i):
        out[:, wide(i)] = nt(held[...], perm[wide(i), :]).astype(bf16)

    loop(hidden.shape[1] // WIDE, leave)
    loop(hidden.shape[1] // WIDE, place)


def enc_body(d_kv_a, d_kv_b, perm, *refs):
    pieces, (out, weights, held, sems) = refs[:6], refs[6:]
    inner = held.shape[1]
    copies = copy_pieces(pieces, weights, sems, TILE + 5 * inner)
    part = d_kv_a.shape[1] // 2
    rest = inner - part
    wait(copies)

    def leave(i):
        rows = wide(i)
        got = nt(d_kv_a[:, pl.ds(0, part)], weights[rows, pl.ds(0, part)])
        got = got + nt(d_kv_b[:, pl.ds(0, rest)], weights[rows, pl.ds(part, rest)])
        got = got + nt(d_kv_a[:, pl.ds(part, part)], weights[rows, pl.ds(inner, part)])
        got = got + nt(d_kv_b[:, pl.ds(rest, rest)], weights[rows, pl.ds(inner + part, rest)])
        held[:, rows] = got.astype(bf16)

    def place(i):
        out[:, wide(i)] = nt(held[...], perm[wide(i), :]).astype(bf16)

    loop(out.shape[1] // WIDE, leave)
    loop(out.shape[1] // WIDE, place)


def fetch_probs(probs_in, probs, in_sems):
    copies = []
    for i in range(probs.shape[0] // 2):
        copies.append(pltpu.make_async_copy(probs_in.at[pl.ds(2 * i, 2)], probs.at[pl.ds(2 * i, 2)], in_sems.at[i]))
        copies[-1].start()


def cross_back_pairs(first, count, queries, kv, mixed, d_mixed, probs_in, probs, in_sems, d_q, d_kv):
    inner = queries.shape[1]
    both = halves((queries.shape[0], TILE))

    def part_of(value):
        return [jnp.where(lanes, value, jnp.zeros_like(value)) for lanes in both]

    def pair(i):
        pltpu.make_async_copy(probs_in.at[pl.ds(2 * i, 2)], probs.at[pl.ds(2 * i, 2)], in_sems.at[i]).wait()
        lanes, mine = at((first + i) * TILE, TILE), at(i * TILE, TILE)
        keys, values = part_of(kv[:, lanes]), kv[:, at(inner + (first + i) * TILE, TILE)]
        d_outs, here = part_of(d_mixed[:, lanes]), part_of(queries[:, lanes])
        d_probs = [nt(d_outs[side], values) for side in range(2)]
        result = mixed[:, mine].astype(f32)
        d_here = d_k = d_v = None
        for side in range(2):
            p = probs[2 * i + side]
            delta = jnp.sum(d_outs[side].astype(f32) * result, axis=-1, keepdims=True)
            d_s = (p.astype(f32) * (d_probs[side] - delta)).astype(bf16)
            parts = nn(d_s, keys[side]), tn(d_s, here[side]), tn(p, d_outs[side])
            d_here = parts[0] if side == 0 else d_here + parts[0]
            d_k = parts[1] if side == 0 else d_k + parts[1]
            d_v = parts[2] if side == 0 else d_v + parts[2]
        d_q[:, mine] = d_here.astype(bf16)
        d_kv[:, mine] = d_k.astype(bf16)
        d_kv[:, at((count + i) * TILE, TILE)] = d_v.astype(bf16)

    loop(count, pair)


def cross_back_one_body(count, d_low, queries, kv, mixed, *refs):
    pieces, probs_in, (d_mixed, d_q, d_kv, weights, probs, sems, in_sems) = refs[:6], refs[6], refs[7:]
    inner = queries.shape[1]
    copies = copy_pieces(pieces, weights, sems, TILE + 7 * inner)
    fetch_probs(probs_in, probs, in_sems)
    wait(copies)

    def enter(i):
        d_mixed[:, wide(i)] = nn(d_low[...], weights[:, wide(i)]).astype(bf16)

    loop(inner // WIDE, enter)
    cross_back_pairs(0, count, queries, kv, mixed, d_mixed, probs_in, probs, in_sems, d_q, d_kv)


def cross_back_two_body(first, count, *refs):
    hidden, d_hidden, gains, queries, kv, mixed, d_mixed, d_q_a = refs[:8]
    pieces, probs_in = refs[8:14], refs[14]
    d_q, d_kv, d_out, d_out_low, d_gain, weights, probs, sems, in_sems = refs[15:]
    inner = queries.shape[1]
    part = d_q_a.shape[1]
    rest = inner - part
    copies = copy_pieces(pieces, weights, sems, TILE + 4 * inner)
    fetch_probs(probs_in, probs, in_sems)
    cross_back_pairs(first, count, queries, kv, mixed, d_mixed, probs_in, probs, in_sems, d_q, d_kv)
    wait(copies)

    def back(i):
        got = nt(d_q_a[...], weights[wide(i), pl.ds(0, part)]) + nt(d_q[...], weights[wide(i), pl.ds(part, rest)])
        d_out[:, wide(i)] = got

    loop(hidden.shape[1] // WIDE, back)
    v = hidden[...]
    d_v, d_g = norm_back(v, gains[1:2], d_out[...], inverse_rms(v))
    d_v = d_v + d_hidden[...]
    d_out[...] = d_v
    d_out_low[...] = d_v.astype(bf16)
    d_gain[...] = d_g


def cross_grads_body(d_one, one_a, one_b, normed, d_q_a, d_q_b, enc, d_kv_a, d_kv_b, d_two, two_a, two_b, low, high):
    part, rest = one_a.shape[1], one_b.shape[1]
    k_a, v_a = d_kv_a.at[:, pl.ds(0, part)], d_kv_a.at[:, pl.ds(part, part)]
    k_b, v_b = d_kv_b.at[:, pl.ds(0, rest)], d_kv_b.at[:, pl.ds(rest, rest)]
    start = 0
    for left, rights in (
        (d_one, (one_a, one_b)),
        (normed, (d_q_a, d_q_b)),
        (enc, (k_a, k_b, v_a, v_b)),
        (d_two, (two_a, two_b)),
    ):
        turned = jnp.transpose(left[...])
        for right in rights:
            put_halves(nn(turned, right[...]), low, high, start)
            start += right.shape[1]


def self_back_pairs(first, count, qkv, mixed, d_mixed, probs_in, probs, in_sems, d_qkv, sums, counted):
    tokens, inner = qkv.shape[0], qkv.shape[1] // 3
    blocks, wides = tokens // TILE, tokens // WIDE
    both = halves((tokens, TILE))

    def part_of(value):
        return [jnp.where(lanes, value, jnp.zeros_like(value)) for lanes in both]

    def pair(i):
        pltpu.make_async_copy(probs_in.at[pl.ds(2 * i, 2)], probs.at[pl.ds(2 * i, 2)], in_sems.at[i]).wait()
        mine = at(i * TILE, TILE)
        here, keys = part_of(qkv[:, mine]), part_of(qkv[:, at(inner + i * TILE, TILE)])
        values = qkv[:, at(2 * inner + i * TILE, TILE)]
        d_outs = part_of(d_mixed[:, at((first + i) * TILE, TILE)])
        result = mixed[:, mine].astype(f32)
        d_probs = {}
        for side in range(2):
            for block in range(wides):
                span = slice(block * WIDE, (block + 1) * WIDE)
                d_probs[side, block] = nt(d_outs[side][span], values[: span.stop])
        d_here, d_k, d_v = [None] * wides, [None] * wides, [None] * wides
        for side in range(2):
            head = 2 * i + side
            delta = jnp.sum(d_outs[side].astype(f32) * result, axis=-1, keepdims=True)
            diagonal = [None] * blocks
            for block in range(wides):
                span = slice(block * WIDE, (block + 1) * WIDE)
                p = probs[head, pl.ds(span.start, WIDE), pl.ds(0, span.stop)]
                d_s = (p.astype(f32) * (d_probs[side, block] - delta[span])).astype(bf16)
                part = nn(d_s, keys[side][: span.stop])
                d_here[block] = part if side == 0 else d_here[block] + part
                for j in range(block + 1):
                    cols = slice(j * WIDE, (j + 1) * WIDE)
                    part = tn(d_s[:, cols], here[side][span])
                    d_k[j] = part if d_k[j] is None else d_k[j] + part
                    part = tn(p[:, cols], d_outs[side][span])
                    d_v[j] = part if d_v[j] is None else d_v[j] + part
                wider = d_s.astype(f32)
                for row in range(2):
                    for j in range(2 * block + row + 1):
                        tile = wider[row * TILE : (row + 1) * TILE, j * TILE : (j + 1) * TILE]
                        apart = 2 * block + row - j
                        diagonal[apart] = tile if diagonal[apart] is None else diagonal[apart] + tile
            for apart in range(blocks):
                tile = jnp.concatenate([diagonal[apart], jnp.zeros((TILE, TILE), f32)], axis=1)
                folded = tile[:8]
                for group in range(1, TILE // 8):
                    folded = folded + pltpu.roll(tile[group * 8 : group * 8 + 8], 2 * TILE - 8 * group, 1)
                for s in range(8):
                    sums[s, pl.ds(apart * 8 + head, 1), :] = folded[s : s + 1]
        for block in range(wides):
            rows = pl.ds(block * WIDE, WIDE)
            d_qkv[rows, mine] = d_here[block].astype(bf16)
            d_qkv[rows, at((count + i) * TILE, TILE)] = d_k[block].astype(bf16)
            d_qkv[rows, at((2 * count + i) * TILE, TILE)] = d_v[block].astype(bf16)

    loop(count, pair)
    lines = sums[0]
    for s in range(1, 8):
        lines = lines + pltpu.roll(sums[s], 2 * TILE - s, 1)
    table = None
    for apart in range(blocks):
        here = lax.dot_general(
            lines[apart * 8 : apart * 8 + 8],
            counted[apart],
            (((1,), (0,)), ((), ())),
            precision=lax.Precision.HIGHEST,
            preferred_element_type=f32,
        )
        table = here if table is None else table + here
    return table


def self_back_one_body(count, d_low, normed, qkv, mixed, counted, *refs):
    pieces, probs_in = refs[:6], refs[6]
    d_mixed, d_qkv, table, low, high, weights, probs, sums, sems, in_sems = refs[7:]
    copies = copy_pieces(pieces, weights, sems, TILE + 3 * weights.shape[1])
    fetch_probs(probs_in, probs, in_sems)
    turned = jnp.transpose(normed[...])
    wait(copies)

    def enter(i):
        d_mixed[:, wide(i)] = nn(d_low[...], weights[:, wide(i)]).astype(bf16)

    loop(d_mixed.shape[1] // WIDE, enter)
    sums[...] = jnp.zeros_like(sums)
    table[...] = self_back_pairs(
        0, count, qkv, mixed, d_mixed, probs_in, probs, in_sems, d_qkv, sums, counted
    )
    part = count * TILE

    def grads(i):
        put_halves(nn(turned, d_qkv[:, pl.ds(i * part, part)]), low, high, i * part)

    loop(3, grads)


def self_back_two_body(first, count, qkv, mixed, d_mixed, counted, table_a, probs_in, *refs):
    d_qkv, table, probs, sums, in_sems = refs
    fetch_probs(probs_in, probs, in_sems)
    sums[...] = jnp.zeros_like(sums)
    table[pl.ds(0, 8), :] = table_a[...]
    table[pl.ds(8, 8), :] = self_back_pairs(
        first, count, qkv, mixed, d_mixed, probs_in, probs, in_sems, d_qkv, sums, counted
    )


def self_back_three_body(count, x, d_hidden, gains, normed, gain_c, gain_f, d_qkv_a, d_qkv, table, spread, *refs):
    pieces, (d_x, low, high, weights, total, sems) = refs[:6], refs[6:]
    copies = copy_pieces(pieces, weights, sems, TILE)
    turned = jnp.transpose(normed[...])
    rest = count * TILE
    start = d_qkv_a.shape[1]
    head = low.shape[1] - 3 * rest

    def grads(i):
        put_halves(nn(turned, d_qkv[:, pl.ds(i * rest, rest)]), low, high, head + i * rest)

    loop(3, grads)
    wait(copies)

    def back(i):
        got = nt(d_qkv_a[...], weights[wide(i), pl.ds(0, start)])
        total[:, wide(i)] = got + nt(d_qkv[...], weights[wide(i), pl.ds(start, 3 * rest)])

    loop(x.shape[1] // WIDE, back)
    v = x[...].astype(f32)
    d_v, d_g = norm_back(v, gains[0:1], total[...], inverse_rms(v))
    d_x[...] = (d_v + d_hidden[...]).astype(bf16)
    rows = jnp.concatenate([d_g, gain_c[...], gain_f[...], jnp.zeros((TILE - 3, d_g.shape[1]), f32)], axis=0)
    found = table[...].astype(bf16)
    per_row = spread.shape[0]
    parts = []
    for j in range(per_row):
        left, right = jnp.zeros((16, j * NB), bf16), jnp.zeros((16, head - (j + 1) * NB), bf16)
        wider = ([left] if j else []) + [found] + ([right] if right.shape[1] else [])
        parts.append(nn(spread[j], jnp.concatenate(wider, axis=1)))
    side = jnp.transpose(rows)
    if head == TILE:
        lane = lax.broadcasted_iota(jnp.int32, side.shape, 1)
        side = jnp.where(lane < HD, sum(parts), pltpu.roll(side, HD, 1))
    else:
        side = jnp.concatenate([sum(parts), side], axis=1)[:, :head]
    put_halves(side, low, high, 0)


def place_body(value, perm, out):
    def place(i):
        out[:, wide(i)] = nt(value[...], perm[wide(i), :]).astype(bf16)

    loop(out.shape[1] // WIDE, place)


def stack_body(one, two, three, out, sems):
    copies, row = [], 0
    for i, value in enumerate((one, two, three)):
        copies.append(pltpu.make_async_copy(value, out.at[pl.ds(row, value.shape[0]), :], sems.at[i]))
        copies[-1].start()
        row += value.shape[0]
    wait(copies)


def stack(*values):
    rows, cols = sum(v.shape[0] for v in values), values[0].shape[1]
    out = [(shape((rows, cols), bf16), FAR)]
    return call(stack_body, "stack", [FAR] * 3, out, [pltpu.SemaphoreType.DMA((3,))], 1.0, *values, spare=2)[0]


def pack_body(part, *refs):
    gain_s, gain_c, gain_f, sq, sk, sv, so, cq, ck, cv, co, fg, fu, fo, early, third, sems = refs
    inner = sq.shape[1]
    rest = inner - part
    moves = [(v.at[:, pl.ds(0, part)], early, TILE + i * part) for i, v in enumerate((sq, sk, sv))]
    moves += [(v.at[:, pl.ds(part, rest)], early, TILE + 3 * part + i * rest) for i, v in enumerate((sq, sk, sv))]
    moves += [(v, early, TILE + (3 + i) * inner) for i, v in enumerate((so, cq, ck, cv, co))]
    moves += [(fg, third, 0), (fu, third, fg.shape[1]), (fo, third, 2 * fg.shape[1])]
    copies = []
    for i, (source, out, start) in enumerate(moves):
        copies.append(pltpu.make_async_copy(source, out.at[:, pl.ds(start, source.shape[1])], sems.at[i]))
        copies[-1].start()
    count = gain_s.shape[1]
    rows = jnp.concatenate([gain_s[...], gain_c[...], gain_f[...], jnp.zeros((TILE - 3, count), bf16)], axis=0).astype(f32)
    rows = jnp.concatenate([rows, jnp.zeros((TILE, TILE - count), f32)], axis=1)
    early[:, pl.ds(0, TILE)] = jnp.transpose(rows)[:count].astype(bf16)
    wait(copies)


def core_add_large_body(block, *refs):
    count = 4 if len(refs) > 12 else 2
    ins, outs, (lows, gots, sums, in_sems, out_sems) = refs[:count], refs[count:-5], refs[-5:]
    blocks = []
    for low, got in zip(ins[::2], ins[1::2]):
        blocks += [(low, got, i * block) for i in range(low.shape[1] // block)]
    copies = []
    for i, (low, got, start) in enumerate(blocks):
        cols = pl.ds(i * block, block)
        copies.append([])
        for j, (source, to) in enumerate(((low, lows), (got, gots))):
            copies[-1].append(pltpu.make_async_copy(source.at[:, pl.ds(start, block)], to.at[:, cols], in_sems.at[2 * i + j]))
            copies[-1][-1].start()
    leaving = []
    for i in range(len(blocks)):
        cols = pl.ds(i * block, block)
        wait(copies[i])
        sums[:, cols] = (lows[:, cols].astype(f32) + gots[:, cols].astype(f32)).astype(bf16)
        row = 0
        for j, out in enumerate(outs):
            size = out.shape[0]
            leaving.append(pltpu.make_async_copy(sums.at[pl.ds(row, size), cols], out.at[:, cols], out_sems.at[5 * i + j]))
            leaving[-1].start()
            row += size
    wait(leaving)


def core_add_large(*pairs):
    rows = pairs[0].shape[0]
    cols = [pairs[i].shape[1] for i in range(0, len(pairs), 2)]
    size = rows // 4
    total = sum(cols)
    block = max(n * TILE for n in range(1, 9) if all(c % (n * TILE) == 0 for c in cols))
    count = total // block
    sizes = (size, size, size, size // 2, size // 2)
    return call(
        lambda *refs: core_add_large_body(block, *refs),
        "core_add_large",
        [FAR] * len(pairs),
        [(shape((s, total), bf16), FAR) for s in sizes],
        [pltpu.VMEM((rows, total), bf16)] * 3 + [pltpu.SemaphoreType.DMA((2 * count,)), pltpu.SemaphoreType.DMA((5 * count,))],
        4.0,
        *pairs,
        spare=3,
    )


def core_add_body(split, *refs):
    outs = refs[-5:]

    def add(low, *gots):
        size = HALF // 4
        got = gots[0][...] if len(gots) == 1 else jnp.concatenate([g[...] for g in gots], axis=0)
        total = (low[...].astype(f32) + got.astype(f32)).astype(bf16)
        starts = (0, size, 2 * size, 3 * size, 3 * size + size // 2)
        for out, start in zip(outs, starts):
            out[...] = total[start : start + out.shape[0]]

    if split is None:
        add(*refs[:2])
    else:
        step = pl.program_id(0)
        pl.when(step < split)(lambda: add(*refs[:2]))
        pl.when(step >= split)(lambda: add(*refs[2:-5]))


def core_add(*pairs):
    rows = pairs[0].shape[0]
    cols = [pairs[0].shape[1]] + ([pairs[2].shape[1]] if len(pairs) > 2 else [])
    if sum(cols) > 5000:
        return core_add_large(*pairs)
    size = rows // 4
    block = max(n * TILE for n in range(1, 7) if all(c % (n * TILE) == 0 for c in cols))
    split = None if len(cols) == 1 else cols[0] // block
    sizes = (size, size, size, size // 2, size // 2)
    first = pl.BlockSpec((rows, block), lambda i: (0, i if split is None else jnp.minimum(i, split - 1)))
    second = pl.BlockSpec((rows, block), lambda i: (0, jnp.maximum(i - split, 0)))
    parted = pl.BlockSpec((rows // max(len(pairs) - 3, 1), block), lambda i: (0, jnp.maximum(i - split, 0)))
    total = sum(cols)
    return pl.pallas_call(
        lambda *refs: core_add_body(split, *refs),
        grid=(total // block,),
        out_shape=[shape((s, total), bf16) for s in sizes],
        in_specs=[first, first] if split is None else [first, first, second] + [parted] * (len(pairs) - 3),
        out_specs=[pl.BlockSpec((s, block), lambda i: (0, i)) for s in sizes],
        compiler_params=pltpu.CompilerParams(vmem_limit_bytes=16 * 2**20),
        cost_estimate=pl.CostEstimate(flops=0, bytes_accessed=1024, transcendentals=0),
        name="core_add",
    )(*pairs)


def plane_add_body(to_x, got_x, to_y, got_y, out_x, out_y):
    half = got_x.shape[0]
    out_x[pl.ds(0, half), :] = to_x[pl.ds(0, half), :]
    out_x[pl.ds(half, half), :] = (to_x[pl.ds(half, half), :].astype(f32) + got_x[...].astype(f32)).astype(bf16)
    out_y[pl.ds(0, half), :] = (to_y[pl.ds(0, half), :].astype(f32) + got_y[...].astype(f32)).astype(bf16)
    out_y[pl.ds(half, half), :] = to_y[pl.ds(half, half), :]


def plane_add(to_x, got_x, to_y, got_y):
    return call(
        plane_add_body, "plane_add", [VMEM] * 4, [(shape(to_x.shape, bf16), VMEM)] * 2, [], 2.0, to_x, got_x, to_y, got_y
    )


def own_add_body(own, got_x, got_y, keep, away):
    half = keep.shape[0]
    total = own[...].astype(f32) + got_x[...].astype(f32) + got_y[...].astype(f32)
    keep[...] = total[:half].astype(bf16)
    away[...] = total[half:].astype(bf16)


def own_add(own, got_x, got_y):
    half = shape((own.shape[0] // 2, own.shape[1]), bf16)
    return call(own_add_body, "own_add", [VMEM] * 3, [(half, VMEM)] * 2, [], 2.0, own, got_x, got_y)


def line_add_body(own, got, keep, away):
    half = keep.shape[0]
    total = own[...].astype(f32) + got[...].astype(f32)
    keep[...] = total[:half].astype(bf16)
    away[...] = total[half:].astype(bf16)


def line_add(own, got):
    half = shape((own.shape[0] // 2, own.shape[1]), bf16)
    return call(line_add_body, "line_add", [VMEM] * 2, [(half, VMEM)] * 2, [], 1.5, own, got)


def last_add_body(own, got, *outs):
    start = 0
    for out in outs:
        cols = pl.ds(start, out.shape[1])
        out[...] = own[:, cols].astype(f32) + got[:, cols].astype(f32)
        start += out.shape[1]


def last_add(own, got, widths):
    outs = [(shape((own.shape[0], w), f32), VMEM) for w in widths]
    return call(last_add_body, "last_add", [VMEM] * 2, outs, [], 1.5, own, got)


def bucket_of(distance):
    bucket = np.where(distance < 16, distance, 16)
    for edge in bucket_edges:
        bucket = bucket + (distance >= edge)
    return np.maximum(bucket, 0)


def split_last_body(own_a, got_a, own_b, got_b, side, *outs):
    head = side.shape[1]
    rest = (own_b.shape[1] - head) // 3
    part = outs[0].shape[1] - rest
    side[...] = own_b[:, pl.ds(0, head)].astype(f32) + got_b[:, pl.ds(0, head)].astype(f32)
    for i, out in enumerate(outs[:3]):
        cols = pl.ds(own_a.shape[1] - (3 - i) * part, part)
        out[:, pl.ds(0, part)] = own_a[:, cols].astype(f32) + got_a[:, cols].astype(f32)
        cols = pl.ds(head + i * rest, rest)
        out[:, pl.ds(part, rest)] = own_b[:, cols].astype(f32) + got_b[:, cols].astype(f32)
    for i, out in enumerate(outs[3:]):
        cols = pl.ds(i * out.shape[1], out.shape[1])
        out[...] = own_a[:, cols].astype(f32) + got_a[:, cols].astype(f32)


def layer(
    cube,
    states,
    encoded,
    cotangent,
    dec_lens,
    enc_lens,
    self_query,
    self_key,
    self_value,
    self_out,
    cross_query,
    cross_key,
    cross_value,
    cross_out,
    ffn_gate,
    ffn_up,
    ffn_out,
    gain_self,
    gain_cross,
    gain_ffn,
    table,
):
    _, tokens, width = states.shape
    enc_tokens = encoded.shape[1]
    inner, ff = self_query.shape[1], ffn_gate.shape[1]
    own_rows = self_query.shape[0]
    blocks = tokens // TILE
    pairs = inner // TILE
    early = pairs // 2
    late = pairs - early
    part, rest = early * TILE, late * TILE
    sems = pltpu.SemaphoreType.DMA
    fence = Order(dec_lens)

    def weight_mem(cols):
        return pltpu.VMEM((width, cols), bf16)

    def mem(*dims):
        return pltpu.VMEM(dims, bf16)

    widths = (TILE + 8 * inner, 3 * ff)
    second = TILE + 3 * inner
    packed = call(
        lambda *refs: pack_body(part, *refs),
        "pack",
        [VMEM] * 3 + [FAR] * 11,
        [(shape((own_rows, w), bf16), VMEM) for w in widths],
        [sems((14,))],
        2.0,
        *(gain_self.reshape(1, -1), gain_cross.reshape(1, -1), gain_ffn.reshape(1, -1)),
        *(self_query, self_key, self_value, self_out, cross_query, cross_key, cross_value, cross_out, ffn_gate, ffn_up, ffn_out),
        spare=60,
    )
    A, C = (Gather(cube, p) for p in packed)
    lines_of = cube.rest
    for step in lines_of[:-1]:
        A.line(step)
    perm = cube.permutation(width)

    lane = np.arange(2 * TILE)
    signed = np.where(lane < TILE, lane, lane - 2 * TILE)
    distance = np.arange(blocks)[:, None] * TILE - signed[None, :]
    chosen = (np.arange(NB)[:, None] == bucket_of(distance).reshape(1, -1)).astype(np.float32)
    lines = lax.dot_general(table, jnp.asarray(chosen, bf16), (((0,), (0,)), ((), ())), preferred_element_type=f32)
    lines = jnp.where(jnp.asarray(distance.reshape(1, -1) >= 0), lines, masked_score)
    lines = lines.reshape(H * blocks, 2 * TILE)
    counted = (bucket_of(distance)[:, :, None] == np.arange(NB)) & (distance >= 0)[:, :, None]
    counted = jnp.asarray(counted.astype(np.float32))

    token_bf = shape((tokens, width), bf16)
    token_f32 = shape((tokens, width), f32)
    row_f32 = shape((1, width), f32)

    (bias,) = call(bias_body, "bias", [VMEM], [(shape((H * blocks, TILE, TILE), f32), VMEM)], [], 5.0, lines)
    bias, perm = fence([bias, perm], A)
    A.line(lines_of[-1])
    x = nn(states[0], perm).astype(bf16)
    enc = nn(encoded[0], perm).astype(bf16)
    cot = nn(cotangent[0], perm).astype(bf16)
    x, enc, cot = fence([x, enc, cot], A, C)
    A.plane()
    for step in lines_of[:-1]:
        C.line(step)
    fence([], A, C)
    A.far()
    C.line(lines_of[-1])
    fence([], A, C)
    A.across()
    C.plane()
    (x,) = fence([x], A)
    gains, normed_one, qkv_a, qkv_b = call(
        self_enter_body,
        "self_enter",
        [VMEM] + [FAR] * 6,
        [
            (shape((8, width), f32), VMEM),
            (token_bf, VMEM),
            (shape((tokens, 3 * part), bf16), VMEM),
            (shape((tokens, 3 * rest), bf16), VMEM),
        ],
        [weight_mem(second), sems((10,))],
        6.0,
        *(x, *A.held),
    )

    def self_heads(first, count, qkv):
        return call(
            lambda *refs: self_pairs(first, count, *refs),
            "self_heads",
            [SMEM, VMEM, VMEM],
            [(shape((tokens, count * TILE), bf16), VMEM), (shape((2 * count, tokens, tokens), bf16), FAR)],
            [mem(2 * count, tokens, tokens), sems((count,))],
            8.0,
            *(dec_lens, bias, qkv),
        )

    mixed_one_a, probs_one_a = self_heads(0, early, qkv_a)
    mixed_one_a, qkv_b = fence([mixed_one_a, qkv_b])
    mixed_one_b, probs_one_b = self_heads(early, late, qkv_b)
    (mixed_one_b,) = fence([mixed_one_b])
    hidden_one, normed_two, q_two, kv_two, mixed_two_a, probs_two_a = call(
        lambda *refs: cross_one_body(early, *refs),
        "cross_one",
        [SMEM] + [VMEM] * 5 + [FAR] * 6,
        [
            (token_f32, VMEM),
            (token_bf, VMEM),
            (shape((tokens, inner), bf16), VMEM),
            (shape((enc_tokens, 2 * inner), bf16), VMEM),
            (shape((tokens, part), bf16), VMEM),
            (shape((2 * early, tokens, enc_tokens), bf16), FAR),
        ],
        [weight_mem(4 * inner), mem(2 * early, tokens, enc_tokens), sems((10,)), sems((early,))],
        13.0,
        *(enc_lens, x, mixed_one_a, mixed_one_b, enc, gains, *A.held),
    )
    hidden_one, normed_two, q_two, kv_two, mixed_two_a, probs_two_a = fence(
        [hidden_one, normed_two, q_two, kv_two, mixed_two_a, probs_two_a], C
    )
    C.far()
    hidden_two, mixed_two_b, probs_two_b = call(
        lambda *refs: cross_two_body(early, late, *refs),
        "cross_two",
        [SMEM] + [VMEM] * 4 + [FAR] * 6,
        [(token_f32, VMEM), (shape((tokens, rest), bf16), VMEM), (shape((2 * late, tokens, enc_tokens), bf16), FAR)],
        [weight_mem(inner), mem(2 * late, tokens, enc_tokens), sems((10,)), sems((late,))],
        10.0,
        *(enc_lens, hidden_one, q_two, kv_two, mixed_two_a, *A.held),
    )
    (hidden_two,) = fence([hidden_two], C)
    C.across()
    (hidden_two,) = fence([hidden_two], C)
    units = shape((tokens, ff), bf16)
    near_units = near((tokens, ff), bf16)
    half_ff = shape((HALF, ff), bf16)
    normed_three, slope, act, gated = call(
        ffn_one_body,
        "ffn_one",
        [VMEM] * 2 + [FAR] * 6,
        [(token_bf, VMEM), (near_units, VMEM), (near_units, VMEM), (units, VMEM)],
        [weight_mem(2 * ff), sems((6,))],
        10.0,
        *(hidden_two, gains, *C.held),
    )
    normed_three, gated, slope, act = fence([normed_three, gated, slope, act])
    half_gu = shape((HALF, 2 * ff), bf16)
    d_gu, gu_low, gu_high = call(
        ffn_two_body,
        "ffn_two",
        [VMEM] * 4 + [FAR] * 6,
        [(near((tokens, 2 * ff), bf16), VMEM), (half_gu, VMEM), (half_gu, VMEM)],
        [weight_mem(ff), sems((6,))],
        10.0,
        *(cot, normed_three, slope, act, *C.held),
    )
    gu_low, gu_high, d_gu, gated = fence([gu_low, gu_high, d_gu, gated])
    R1 = Reduce(cube, gu_low, gu_high)
    fo_low, fo_high = call(
        ffn_grad_body, "ffn_grad", [VMEM] * 2, [(half_ff, VMEM)] * 2, [], 4.0, cot, gated
    )
    fo_low, fo_high, d_gu = fence([fo_low, fo_high, d_gu])
    R1.more(fo_low, fo_high)
    (d_gu,) = fence([d_gu], R1)
    R1.far()
    d_hidden_two, d_low_two, gain_f = call(
        ffn_three_body,
        "ffn_three",
        [VMEM] * 4 + [FAR] * 6,
        [(token_f32, VMEM), (token_bf, VMEM), (row_f32, VMEM)],
        [weight_mem(2 * ff), sems((10,))],
        5.0,
        *(hidden_two, cot, gains, d_gu, *C.held),
    )
    d_hidden_two, d_low_two, gain_f = fence([d_hidden_two, d_low_two, gain_f])
    d_mixed_two, d_q_a, d_kv_a = call(
        lambda *refs: cross_back_one_body(early, *refs),
        "cross_back_one",
        [VMEM] * 4 + [FAR] * 7,
        [
            (shape((tokens, inner), bf16), VMEM),
            (shape((tokens, part), bf16), VMEM),
            (shape((enc_tokens, 2 * part), bf16), VMEM),
        ],
        [
            weight_mem(inner),
            mem(2 * early, tokens, enc_tokens),
            sems((10,)),
            sems((early,)),
        ],
        8.0,
        *(d_low_two, q_two, kv_two, mixed_two_a, *A.held, probs_two_a),
    )
    d_mixed_two, d_q_a, d_kv_a = fence([d_mixed_two, d_q_a, d_kv_a], R1)
    R1.plane()
    d_q_b, d_kv_b, d_hidden_one, d_low_one, gain_c = call(
        lambda *refs: cross_back_two_body(early, late, *refs),
        "cross_back_two",
        [VMEM] * 8 + [FAR] * 7,
        [
            (shape((tokens, rest), bf16), VMEM),
            (shape((enc_tokens, 2 * rest), bf16), VMEM),
            (token_f32, VMEM),
            (token_bf, VMEM),
            (row_f32, VMEM),
        ],
        [
            weight_mem(inner),
            mem(2 * late, tokens, enc_tokens),
            sems((10,)),
            sems((late,)),
        ],
        8.0,
        *(hidden_one, d_hidden_two, gains, q_two, kv_two, mixed_two_b, d_mixed_two, d_q_a, *A.held, probs_two_b),
    )
    d_q_b, d_kv_b, d_hidden_one, d_low_one, gain_c = fence([d_q_b, d_kv_b, d_hidden_one, d_low_one, gain_c])
    half_a = shape((HALF, 3 * part), bf16)
    d_mixed_one, d_qkv_a, table_a, self_low_a, self_high_a = call(
        lambda *refs: self_back_one_body(early, *refs),
        "self_back_one",
        [VMEM] * 5 + [FAR] * 7,
        [
            (shape((tokens, inner), bf16), VMEM),
            (shape((tokens, 3 * part), bf16), VMEM),
            (shape((8, NB), f32), VMEM),
            (half_a, VMEM),
            (half_a, VMEM),
        ],
        [
            weight_mem(inner),
            mem(2 * early, tokens, tokens),
            pltpu.VMEM((8, 8 * blocks, 2 * TILE), f32),
            sems((6,)),
            sems((early,)),
        ],
        9.0,
        *(d_low_one, normed_one, qkv_a, mixed_one_a, counted, *A.held, probs_one_a),
    )
    self_low_a, self_high_a, d_qkv_a, d_mixed_one, table_a, d_q_b, d_low_two = fence(
        [self_low_a, self_high_a, d_qkv_a, d_mixed_one, table_a, d_q_b, d_low_two]
    )
    half_cross = shape((HALF, 5 * inner), bf16)
    cross_low, cross_high = call(
        cross_grads_body,
        "cross_grads",
        [VMEM] * 12,
        [(half_cross, VMEM)] * 2,
        [],
        9.0,
        *(d_low_one, mixed_one_a, mixed_one_b, normed_two, d_q_a, d_q_b, enc, d_kv_a, d_kv_b, d_low_two, mixed_two_a, mixed_two_b),
    )
    cross_low, cross_high, d_kv_b = fence([cross_low, cross_high, d_kv_b])
    (grad_enc,) = call(
        enc_body,
        "grad_encoded",
        [VMEM] * 3 + [FAR] * 6,
        [(shape((enc_tokens, width), bf16), VMEM)],
        [weight_mem(2 * inner), mem(enc_tokens, width), sems((10,))],
        5.0,
        *(d_kv_a, d_kv_b, perm, *A.held),
    )
    cross_low, cross_high, grad_enc = fence([cross_low, cross_high, grad_enc], R1)
    R1.line()
    R3 = Reduce(cube, cross_low, cross_high)
    R3.more(self_low_a, self_high_a)
    (d_qkv_a,) = fence([d_qkv_a], R3)
    R3.far()
    per_row = -(-H // own_rows)
    head_cols = TILE if per_row * NB <= HD else per_row * NB + TILE
    placed = np.zeros((per_row, width, 16), np.float32)
    for h in range(H):
        slot = h if h < 2 * early else 8 + h - 2 * early
        placed[h % per_row, h // per_row :: own_rows, slot] = 1.0
    half_b = shape((HALF, head_cols + 3 * rest), bf16)
    d_qkv_b, table_sum = call(
        lambda *refs: self_back_two_body(early, late, *refs),
        "self_back_two",
        [VMEM] * 5 + [FAR],
        [(shape((tokens, 3 * rest), bf16), VMEM), (shape((16, NB), f32), VMEM)],
        [
            mem(2 * late, tokens, tokens),
            pltpu.VMEM((8, 8 * blocks, 2 * TILE), f32),
            sems((late,)),
        ],
        7.0,
        *(qkv_b, mixed_one_b, d_mixed_one, counted, table_a, probs_one_b),
    )
    d_qkv_b, table_sum = fence([d_qkv_b, table_sum], R3, R1)
    R3.plane()
    R1.rest()
    d_x, self_low_b, self_high_b = call(
        lambda *refs: self_back_three_body(late, *refs),
        "self_back_three",
        [VMEM] * 10 + [FAR] * 6,
        [(token_bf, VMEM), (half_b, VMEM), (half_b, VMEM)],
        [
            weight_mem(3 * inner),
            pltpu.VMEM((tokens, width), f32),
            sems((6,)),
        ],
        5.0,
        *(x, d_hidden_one, gains, normed_one, gain_c, gain_f, d_qkv_a, d_qkv_b, table_sum, jnp.asarray(placed, bf16)),
        *A.held,
    )
    self_low_b, self_high_b, d_x, gated = fence([self_low_b, self_high_b, d_x, gated])
    (grad_states,) = call(place_body, "grad_states", [VMEM] * 2, [(token_bf, VMEM)], [], 2.0, d_x, perm)
    (output,) = call(
        output_body,
        "output",
        [VMEM] * 3 + [FAR] * 6,
        [(token_bf, VMEM)],
        [weight_mem(ff), mem(tokens, width), sems((10,))],
        6.0,
        *(hidden_two, gated, perm, *C.held),
    )
    output, grad_states, self_high_b = fence([output, grad_states, self_high_b], R3, R1)
    R5 = Reduce(cube, self_low_b, self_high_b)
    R3.line()
    g_fg, g_fu, g_fo = R1.last((ff, ff, ff))
    (g_fo,) = fence([g_fo], R5)
    R5.far()
    fence([], R3)
    R3.rest()
    fence([], R5)
    R5.plane()
    fence([], R5)
    R5.line()
    fence([], R5)
    R5.rest()
    fence([], R3, R5)
    sizes = (head_cols,) + (inner,) * 8
    side, g_sq, g_sk, g_sv, g_so, g_cq, g_ck, g_cv, g_co = call(
        split_last_body,
        "last_self",
        [VMEM] * 4,
        [(shape((own_rows, w), f32), VMEM) for w in sizes],
        [],
        1.5,
        *(*R3.held, *R5.held),
    )
    heads = [side[h // per_row, (h % per_row) * NB : (h % per_row + 1) * NB] for h in range(H)]
    if per_row == 1:
        grad_table = side[:H, :NB].T
    else:
        grad_table = jnp.stack(heads, axis=1)
    first_gain = HD if head_cols == TILE else per_row * NB
    g_gains = side[:, first_gain : first_gain + 3]
    return (
        output[None],
        grad_states[None],
        grad_enc[None],
        g_sq,
        g_sk,
        g_sv,
        g_so,
        g_cq,
        g_ck,
        g_cv,
        g_co,
        g_fg,
        g_fu,
        g_fo,
        g_gains[:, 0],
        g_gains[:, 1],
        g_gains[:, 2],
        grad_table,
    )


def solution(mesh):
    cube = Cube(mesh)
    both = ("gx", "gy")
    row, flat, one = P(both, None, None), P(both, None), P(both)
    in_specs = (row, row, row, one, one) + (flat,) * 11 + (one,) * 3 + (P(),)
    out_specs = (row, row, row) + (flat,) * 11 + (one,) * 3 + (P(),)

    def per_device(*args):
        return layer(cube, *args)

    return jax.shard_map(per_device, mesh=mesh, in_specs=in_specs, out_specs=out_specs, check_vma=False)
```
